32 devices in a mesh: fsdp: 8 (over z, y), rep: 4 (over x, core).
Axes of the slice: x: 2, y: 2, z: 4, core: 2. Of those that a mesh axis runs over, the one named last changes fastest.
Arguments:
- tokens_in: bfloat16 [4096, 2048], P(('fsdp', 'rep')), may hold values from -6 to 6
- segment_ids: int32 [64, 64], P(('fsdp', 'rep')), may hold values from 0 to 2, never falling along the last dimension, each value on 1 to 48 neighbouring positions
- w_query: bfloat16 [2048, 2048], P('fsdp'), may hold values from -0.125 to 0.125
- w_key: bfloat16 [2048, 512], P('fsdp'), may hold values from -0.125 to 0.125
- w_value: bfloat16 [2048, 512], P('fsdp'), may hold values from -0.125 to 0.125
- w_out: bfloat16 [2048, 2048], P('fsdp'), may hold values from -0.375 to 0.375
- w_gate: bfloat16 [2048, 8192], P('fsdp'), may hold values from -0.125 to 0.125
- w_up: bfloat16 [2048, 8192], P('fsdp'), may hold values from -0.125 to 0.125
- w_down: bfloat16 [8192, 2048], P('fsdp'), may hold values from -0.09375 to 0.09375
- gain_attn: bfloat16 [2048], P('fsdp'), may hold values from 0.5 to 1.5
- gain_ffn: bfloat16 [2048], P('fsdp'), may hold values from 0.5 to 1.5
- gain_query: bfloat16 [64], replicated, may hold values from 0.25 to 1.75
- gain_key: bfloat16 [64], replicated, may hold values from 0.25 to 1.75
- d_out: bfloat16 [4096, 2048], P(('fsdp', 'rep')), may hold values from -6 to 6
Outputs:
- block_out: bfloat16 [4096, 2048], P(('fsdp', 'rep'))
- d_tokens: bfloat16 [4096, 2048], P(('fsdp', 'rep'))
- grad_w_query: float32 [2048, 2048], P('fsdp')
- grad_w_key: float32 [2048, 512], P('fsdp')
- grad_w_value: float32 [2048, 512], P('fsdp')
- grad_w_out: float32 [2048, 2048], P('fsdp')
- grad_w_gate: float32 [2048, 8192], P('fsdp')
- grad_w_up: float32 [2048, 8192], P('fsdp')
- grad_w_down: float32 [8192, 2048], P('fsdp')
- grad_gain_attn: float32 [2048], P('fsdp')
- grad_gain_ffn: float32 [2048], P('fsdp')
- grad_gain_query: float32 [64], replicated
- grad_gain_key: float32 [64], replicated
- rms_stats: float32 [5], replicated
The draws below stay inside these ranges and needn't reach their ends.
All inputs are finite; a program needn't handle non-finite values.
Results may differ from the reference program's by a relative error of at most 0.02.
Values may be sent and summed in bfloat16 or wider, within the bound.
No kernel may reach another device: no remote copies, remote signals or barrier semaphores. Data moves between devices by JAX's collectives and lax.ppermute only.
A program may use at most 448 MiB of HBM per device.

```python
import math
import jax
import jax.numpy as jnp
import numpy as np
from jax import lax

D = 2048
H = 32
KV = 8
HD = 64
FF = 8192
MB_TOK = 64
PACKS = 64
TOKENS = 4096


def block_scale(stream_key, extent, cuts, smallest, largest):
    factor_of, own = 1.0, jax.random.fold_in(stream_key, 6)
    for dim, parts in cuts:
        steps = jnp.exp(jax.random.uniform(jax.random.fold_in(own, dim), (parts,), jnp.float32, smallest / len(cuts), largest / len(cuts)))
        factor_of = factor_of * jnp.repeat(steps, extent[dim] // parts).reshape([-1 if axis == dim else 1 for axis in range(len(extent))])
    return factor_of


def split_up(number_of, total, bound, lean):
    weights = [(1 << 20) // math.isqrt(standing ** lean) + 1 for standing in range(2, number_of + 1)]
    rest, given = total - bound - (number_of - 1), [1] * (number_of - 1)
    while rest > 0:
        movable = [i for i in range(number_of - 1) if given[i] < bound]
        pool, remaining = sum([weights[i] for i in movable]), rest
        for i in movable:
            more = min(bound - given[i], max(1, remaining * weights[i] // pool), rest)
            given[i] = given[i] + more
            rest = rest - more
    return np.array([bound] + given)


def ragged_sizes(rng, number_of, total, limit, lean):
    if number_of == 2:
        one = jax.random.randint(rng, (), max(1, total - limit), min(limit, total - 1) + 1)
        return jnp.stack([one, total - one])
    sizes = jnp.asarray(split_up(number_of, total, limit, lean), jnp.int32)
    twos = (number_of - 1) // 2
    donor, sink = sizes[1:1 + 2 * twos:2], sizes[2:2 + 2 * twos:2]
    slack = jnp.minimum(donor - 1, limit - sink)
    moved = jax.random.randint(jax.random.fold_in(rng, 1), (twos,), 0, 1 << 20) % (slack + 1)
    sizes = sizes.at[1:1 + 2 * twos:2].set(donor - moved).at[2:2 + 2 * twos:2].set(sink + moved)
    return sizes[jax.random.permutation(jax.random.fold_in(rng, 2), number_of)]


def normal_values(key, dims, deviation, limit, cuts=(), kind=jnp.bfloat16):
    drawn = jax.random.normal(key, dims, jnp.float32) * deviation
    if len(cuts) > 0:
        drawn = block_scale(key, dims, cuts, -0.22, 0.18) * drawn
    return jnp.clip(drawn, min=-limit, max=limit).astype(kind)


def setup_inputs(seed: int = 0) -> dict:
    streams_of = jax.random.split(jax.random.key(seed), 15)
    return {
        "tokens_in": normal_values(streams_of[0], (TOKENS, D), 1.0, 6.0, ((0, 32),)),
        "segment_ids": jax.vmap(lambda own: jnp.searchsorted(jnp.cumsum(ragged_sizes(own, 3, MB_TOK, 3 * MB_TOK // 4, 1)), jnp.arange(MB_TOK), side="right"))(jax.random.split(streams_of[1], PACKS)).reshape((PACKS, MB_TOK)).astype(jnp.int32),
        "w_query": normal_values(streams_of[2], (D, H * HD), D ** -0.5, 0.125, ((0, 8),)),
        "w_key": normal_values(streams_of[3], (D, KV * HD), D ** -0.5, 0.125, ((0, 8),)),
        "w_value": normal_values(streams_of[4], (D, KV * HD), D ** -0.5, 0.125, ((0, 8),)),
        "w_out": normal_values(streams_of[5], (H * HD, D), (H * HD // 8) ** -0.5, 0.375, ((0, 8),)),
        "w_gate": normal_values(streams_of[6], (D, FF), D ** -0.5, 0.125, ((0, 8),)),
        "w_up": normal_values(streams_of[7], (D, FF), D ** -0.5, 0.125, ((0, 8),)),
        "w_down": normal_values(streams_of[8], (FF, D), (FF // 2) ** -0.5, 0.09375, ((0, 8),)),
        "gain_attn": jnp.clip(1.0 + 0.1 * jax.random.normal(streams_of[9], (D,), jnp.float32), 0.5, 1.5).astype(jnp.bfloat16),
        "gain_ffn": jnp.clip(1.0 + 0.1 * jax.random.normal(streams_of[10], (D,), jnp.float32), 0.5, 1.5).astype(jnp.bfloat16),
        "gain_query": jnp.clip(1.0 + 0.15 * jax.random.normal(streams_of[11], (HD,), jnp.float32), 0.25, 1.75).astype(jnp.bfloat16),
        "gain_key": jnp.clip(1.0 + 0.15 * jax.random.normal(streams_of[12], (HD,), jnp.float32), 0.25, 1.75).astype(jnp.bfloat16),
        "d_out": normal_values(streams_of[13], (TOKENS, D), 1.0, 6.0, ((0, 32),)),
    }


@jax.custom_vjp
def low(v):
    return lax.optimization_barrier(v.astype(jnp.bfloat16)).astype(jnp.float32)

@jax.custom_vjp
def low_back(v):
    return v

def low_keep(v):
    return (low(v), None)

def low_pass(kept, grad):
    return (grad,)

def back_keep(v):
    return (v, None)

def back_low(kept, grad):
    return (low(grad),)
low.defvjp(low_keep, low_pass)
low_back.defvjp(back_keep, back_low)
EPS = 1e-05
THETA = 1000000.0
NEG = -1e+30

def norm_rows(values, gain):
    return values * lax.rsqrt(lax.optimization_barrier(jnp.mean(values * values, axis=-1, keepdims=True)) + EPS) * gain

def rotate(values, cosine, sine):
    half_dim = values.shape[-1] // 2
    first_half = values[..., :half_dim]
    second_half = values[..., half_dim:]
    return jnp.concatenate([first_half * cosine - second_half * sine, second_half * cosine + first_half * sine], axis=-1)

def angles(seg_row):
    token_index = jnp.arange(seg_row.shape[0])
    earlier = (seg_row[:, None] == seg_row[None, :]) & (token_index[None, :] < token_index[:, None])
    position = lax.optimization_barrier(jnp.sum(earlier.astype(jnp.int32), axis=1))
    half_dim = HD // 2
    frequency = jnp.exp(jnp.arange(half_dim).astype(jnp.float32) * (-2.0 * math.log(THETA) / HD))
    phase = position.astype(jnp.float32)[:, None] * frequency[None, :]
    return (jnp.cos(phase)[:, None, :], jnp.sin(phase)[:, None, :])

def allowed_pairs(seg_row):
    token_index = jnp.arange(seg_row.shape[0])
    return (seg_row[:, None] == seg_row[None, :]) & (token_index[None, :] <= token_index[:, None])

def softmax_rows(scores, allowed):
    masked = jnp.where(allowed, scores, NEG)
    row_max = lax.optimization_barrier(jnp.max(masked, axis=-1, keepdims=True))
    exponent = jnp.exp(masked - row_max)
    return exponent / lax.optimization_barrier(jnp.sum(exponent, axis=-1, keepdims=True))

def swiglu(gate_in, up_in):
    return gate_in * jax.nn.sigmoid(gate_in) * up_in

def pack_attention(pieces):
    query_pack, key_pack, value_pack, seg_row = pieces
    highest = lax.Precision.HIGHEST
    row_count = query_pack.shape[0]
    group_size = H // KV
    grouped = query_pack.reshape(row_count, KV, group_size, HD)
    scores = low_back(jnp.einsum('ikgd,jkd->kgij', grouped, key_pack, precision=highest) * HD ** (-0.5))
    attn_probs = low(softmax_rows(scores, allowed_pairs(seg_row)))
    mixed = jnp.einsum('kgij,jkd->ikgd', attn_probs, value_pack, precision=highest)
    return mixed.reshape(row_count, H * HD)

def forward(tokens_f, w_query, w_key, w_value, w_out, w_gate, w_up, w_down, gain_attn, gain_ffn, gain_query, gain_key, cosine, sine, segment_ids):
    highest = lax.Precision.HIGHEST
    row_count = tokens_f.shape[0]
    attn_in = low(norm_rows(tokens_f, gain_attn))
    query_raw = low_back(jnp.dot(attn_in, w_query, precision=highest))
    key_raw = low_back(jnp.dot(attn_in, w_key, precision=highest))
    value_all = low(low_back(jnp.dot(attn_in, w_value, precision=highest)))
    query_all = low(rotate(norm_rows(query_raw.reshape(row_count, H, HD), gain_query), cosine, sine))
    key_all = low(rotate(norm_rows(key_raw.reshape(row_count, KV, HD), gain_key), cosine, sine))
    pack_count = row_count // MB_TOK
    mixed = lax.map(jax.checkpoint(pack_attention), (query_all.reshape(pack_count, MB_TOK, H, HD), key_all.reshape(pack_count, MB_TOK, KV, HD), value_all.reshape(pack_count, MB_TOK, KV, HD), segment_ids))
    mixed = low(low_back(mixed.reshape(row_count, H * HD)))
    attn_branch = low_back(jnp.dot(mixed, w_out, precision=highest))
    middle = tokens_f + attn_branch
    ffn_in = low(norm_rows(middle, gain_ffn))
    gate_all = low_back(jnp.dot(ffn_in, w_gate, precision=highest))
    up_all = low_back(jnp.dot(ffn_in, w_up, precision=highest))
    hidden = low(low_back(swiglu(gate_all, up_all)))
    ffn_branch = low_back(jnp.dot(hidden, w_down, precision=highest))
    return (middle + ffn_branch, (middle, attn_branch, ffn_branch))

def reference(tokens_in, segment_ids, w_query, w_key, w_value, w_out, w_gate, w_up, w_down, gain_attn, gain_ffn, gain_query, gain_key, d_out):
    floats = [item.astype(jnp.float32) for item in (tokens_in, w_query, w_key, w_value, w_out, w_gate, w_up, w_down, gain_attn, gain_ffn, gain_query, gain_key)]
    row_count = tokens_in.shape[0]
    cosine, sine = jax.vmap(angles)(segment_ids)
    cosine = cosine.reshape(row_count, 1, HD // 2)
    sine = sine.reshape(row_count, 1, HD // 2)

    def apply_block(*params):
        return forward(*params, cosine, sine, segment_ids)
    block_out, pull_back, extras = jax.vjp(apply_block, *floats, has_aux=True)
    grads = pull_back(d_out.astype(jnp.float32))
    middle, attn_branch, ffn_branch = extras
    d_tokens = grads[0]

    def root_mean(values):
        return jnp.sqrt(jnp.sum(values * values) / (row_count * D))
    stats = jnp.stack([root_mean(middle), root_mean(attn_branch), root_mean(ffn_branch), root_mean(block_out), root_mean(d_tokens)])
    return (block_out.astype(jnp.bfloat16), d_tokens.astype(jnp.bfloat16), grads[1], grads[2], grads[3], grads[4], grads[5], grads[6], grads[7], grads[8], grads[9], grads[10], grads[11], stats)
```

```python
import math

import jax
import jax.numpy as jnp
from jax import lax
from jax.sharding import PartitionSpec as P

HD = 64
EPS = 1e-05
THETA = 1000000.0
NEG = -1e30
BF = jnp.bfloat16
F32 = jnp.float32


def matmul(left, right):
    return jnp.dot(left, right, preferred_element_type=F32)


def left_tmul(left, right):
    return lax.dot_general(left, right, (((0,), (0,)), ((), ())), preferred_element_type=F32)


def right_tmul(left, right):
    return lax.dot_general(left, right, (((1,), (1,)), ((), ())), preferred_element_type=F32)


def unit_rows(values):
    root = lax.rsqrt(jnp.mean(values * values, axis=-1, keepdims=True) + EPS)
    return values * root, root


def unit_back(unit, root, grad):
    return root * (grad - unit * jnp.mean(grad * unit, axis=-1, keepdims=True))


def rotate(values, cosine, sine):
    half = values.shape[-1] // 2
    first, second = values[..., :half], values[..., half:]
    return jnp.concatenate(
        [first * cosine - second * sine, second * cosine + first * sine], axis=-1
    )


def phases(segments):
    index = jnp.arange(segments.shape[1])
    same = segments[:, :, None] == segments[:, None, :]
    position = jnp.sum((same & (index[None, :] < index[:, None])).astype(jnp.int32), axis=2)
    frequency = jnp.exp(jnp.arange(HD // 2).astype(F32) * (-2.0 * math.log(THETA) / HD))
    phase = position.astype(F32)[:, :, None, None] * frequency
    return jnp.cos(phase), jnp.sin(phase), same & (index[None, :] <= index[:, None])


def gather_rows(values):
    return lax.all_gather(values, "fsdp", axis=0, tiled=True)


def scatter_rows(values):
    return lax.psum_scatter(values.astype(BF), "fsdp", scatter_dimension=0, tiled=True)


def rows_to_columns(weight):
    return lax.all_to_all(weight, "fsdp", 1, 0, tiled=True)


def columns_to_rows(grad):
    ranks, copies = lax.axis_size("fsdp"), lax.axis_size("rep")
    rows, columns = grad.shape
    part = rows // (ranks * copies)
    blocks = grad.astype(BF).reshape(ranks, copies, part, columns)
    own = lax.psum_scatter(blocks, "rep", scatter_dimension=1, tiled=True)
    own = own.reshape(ranks, part, columns)
    moved = lax.all_to_all(own, "fsdp", 0, 0, tiled=True)
    whole = lax.all_gather(moved, "rep", axis=0, tiled=False)
    return whole.transpose(0, 2, 1, 3).reshape(copies * part, ranks, columns)


def local(
    tokens_in,
    segment_ids,
    w_query,
    w_key,
    w_value,
    w_out,
    w_gate,
    w_up,
    w_down,
    gain_attn,
    gain_ffn,
    gain_query,
    gain_key,
    d_out,
):
    ranks = lax.axis_size("fsdp")
    rank = lax.axis_index("fsdp")
    width = tokens_in.shape[1]
    pack = segment_ids.shape[1]
    heads = w_query.shape[1] // HD
    kv_heads = w_key.shape[1] // HD
    share = max(1, ranks // kv_heads)
    q_here = heads // ranks
    kv_here = max(1, kv_heads // ranks)
    group = q_here // kv_here
    q_cols, kv_cols = q_here * HD, kv_here * HD
    scale = HD ** (-0.5)

    gains = lax.all_gather(jnp.stack([gain_attn, gain_ffn]), "fsdp", axis=1, tiled=True)
    attn_gain = gains[0].astype(F32)
    ffn_gain = gains[1].astype(F32)
    q_gain = gain_query.astype(F32)
    k_gain = gain_key.astype(F32)

    def by_rank(weight, columns, repeats):
        split = weight.reshape(weight.shape[0], -1, columns)
        return jnp.repeat(split, repeats, axis=1) if repeats > 1 else split

    qkv_rows = jnp.concatenate(
        [
            by_rank(w_query, q_cols, 1),
            by_rank(w_key, kv_cols, share),
            by_rank(w_value, kv_cols, share),
        ],
        axis=2,
    ).reshape(w_query.shape[0], -1)
    w_qkv = rows_to_columns(qkv_rows)
    w_gate_here = rows_to_columns(w_gate)
    w_up_here = rows_to_columns(w_up)

    tokens = tokens_in.astype(F32)
    unit_tokens, root_tokens = unit_rows(tokens)
    attn_in = gather_rows((unit_tokens * attn_gain).astype(BF))
    segments = lax.all_gather(segment_ids, "fsdp", axis=0, tiled=True)
    g_ffn = gather_rows(d_out)
    cosine, sine, allowed = phases(segments)
    packs = segments.shape[0]
    total = packs * pack

    qkv = matmul(attn_in, w_qkv)
    q_raw = qkv[:, :q_cols].reshape(packs, pack, q_here, HD)
    k_raw = qkv[:, q_cols : q_cols + kv_cols].reshape(packs, pack, kv_here, HD)
    value = qkv[:, q_cols + kv_cols :].reshape(packs, pack, kv_here, HD).astype(BF)
    q_unit, q_root = unit_rows(q_raw)
    k_unit, k_root = unit_rows(k_raw)
    query = rotate(q_unit * q_gain, cosine, sine).astype(BF)
    query = query.reshape(packs, pack, kv_here, group, HD)
    key = rotate(k_unit * k_gain, cosine, sine).astype(BF)
    scores = jnp.einsum("pikgd,pjkd->pkgij", query, key, preferred_element_type=F32) * scale
    masked = jnp.where(allowed[:, None, None], scores, NEG)
    exponent = jnp.exp(masked - jnp.max(masked, axis=-1, keepdims=True))
    probs = exponent / jnp.sum(exponent, axis=-1, keepdims=True)
    probs_low = probs.astype(BF)
    mixed = jnp.einsum("pkgij,pjkd->pikgd", probs_low, value, preferred_element_type=F32)
    mixed = mixed.reshape(total, q_cols).astype(BF)
    attn_branch = scatter_rows(matmul(mixed, w_out)).astype(F32)

    middle = tokens + attn_branch
    unit_middle, root_middle = unit_rows(middle)
    ffn_in = gather_rows((unit_middle * ffn_gain).astype(BF))
    gate = matmul(ffn_in, w_gate_here)
    up = matmul(ffn_in, w_up_here)
    sig = jax.nn.sigmoid(gate)
    silu = gate * sig
    hidden = (silu * up).astype(BF)
    ffn_branch = scatter_rows(matmul(hidden, w_down)).astype(F32)
    block = middle + ffn_branch

    grad_down = left_tmul(hidden, g_ffn)
    g_hidden = right_tmul(g_ffn, w_down).astype(BF).astype(F32)
    g_gate = (g_hidden * up * sig * (1 + gate * (1 - sig))).astype(BF)
    g_up = (g_hidden * silu).astype(BF)
    g_ffn_in = scatter_rows(right_tmul(g_gate, w_gate_here) + right_tmul(g_up, w_up_here))
    g_ffn_in = g_ffn_in.astype(F32)
    grad_gate = left_tmul(ffn_in, g_gate)
    grad_up = left_tmul(ffn_in, g_up)
    ffn_gain_grad = jnp.sum(g_ffn_in * unit_middle, axis=0)
    g_middle = d_out.astype(F32) + unit_back(unit_middle, root_middle, g_ffn_in * ffn_gain)

    g_attn = gather_rows(g_middle.astype(BF))
    grad_out = left_tmul(mixed, g_attn)
    g_mixed = right_tmul(g_attn, w_out).astype(BF).reshape(packs, pack, kv_here, group, HD)
    g_probs = jnp.einsum("pikgd,pjkd->pkgij", g_mixed, value, preferred_element_type=F32)
    g_value = jnp.einsum("pkgij,pikgd->pjkd", probs_low, g_mixed, preferred_element_type=F32)
    g_scores = probs * (g_probs - jnp.sum(probs * g_probs, axis=-1, keepdims=True))
    g_scores = g_scores.astype(BF)
    g_query = jnp.einsum("pkgij,pjkd->pikgd", g_scores, key, preferred_element_type=F32) * scale
    g_key = jnp.einsum("pkgij,pikgd->pjkd", g_scores, query, preferred_element_type=F32) * scale
    owner = jnp.ones((), F32)
    if share > 1:
        together = [[first * share + step for step in range(share)] for first in range(kv_heads)]
        g_value, g_key = lax.psum((g_value, g_key), "fsdp", axis_index_groups=together)
        owner = (rank % share == 0).astype(F32)
    q_back = rotate(g_query.reshape(packs, pack, q_here, HD), cosine, -sine)
    k_back = rotate(g_key, cosine, -sine)
    q_gain_grad = jnp.sum(q_back * q_unit, axis=(0, 1, 2))
    k_gain_grad = jnp.sum(k_back * k_unit, axis=(0, 1, 2)) * owner
    g_qkv = jnp.concatenate(
        [
            unit_back(q_unit, q_root, q_back * q_gain).reshape(total, q_cols),
            unit_back(k_unit, k_root, k_back * k_gain).reshape(total, kv_cols) * owner,
            g_value.reshape(total, kv_cols) * owner,
        ],
        axis=1,
    ).astype(BF)
    g_attn_in = scatter_rows(right_tmul(g_qkv, w_qkv)).astype(F32)
    grad_qkv = left_tmul(attn_in, g_qkv)
    attn_gain_grad = jnp.sum(g_attn_in * unit_tokens, axis=0)
    d_tokens = g_middle + unit_back(unit_tokens, root_tokens, g_attn_in * attn_gain)

    qkv_sum = columns_to_rows(grad_qkv)
    q_sum = qkv_sum[:, :, :q_cols].reshape(qkv_sum.shape[0], -1)
    k_sum = qkv_sum[:, ::share, q_cols : q_cols + kv_cols].reshape(qkv_sum.shape[0], -1)
    v_sum = qkv_sum[:, ::share, q_cols + kv_cols :].reshape(qkv_sum.shape[0], -1)
    gate_sum = columns_to_rows(grad_gate).reshape(w_gate.shape)
    up_sum = columns_to_rows(grad_up).reshape(w_up.shape)
    out_sum = lax.psum(grad_out.astype(BF), "rep")
    down_sum = lax.psum(grad_down.astype(BF), "rep")
    squares = jnp.stack(
        [jnp.sum(item * item) for item in (middle, attn_branch, ffn_branch, block, d_tokens)]
    )
    small = jnp.concatenate([attn_gain_grad, ffn_gain_grad, q_gain_grad, k_gain_grad, squares])
    small = lax.psum(small, ("fsdp", "rep"))
    gain_rows = gain_attn.shape[0]
    attn_gain_sum = lax.dynamic_slice(small, (rank * gain_rows,), (gain_rows,))
    ffn_gain_sum = lax.dynamic_slice(small, (width + rank * gain_rows,), (gain_rows,))
    entries = tokens_in.shape[0] * ranks * lax.axis_size("rep") * width
    stats = jnp.sqrt(small[2 * width + 2 * HD :] / entries)
    return (
        block.astype(BF),
        d_tokens.astype(BF),
        q_sum.astype(F32),
        k_sum.astype(F32),
        v_sum.astype(F32),
        out_sum.astype(F32),
        gate_sum.astype(F32),
        up_sum.astype(F32),
        down_sum.astype(F32),
        attn_gain_sum,
        ffn_gain_sum,
        small[2 * width : 2 * width + HD],
        small[2 * width + HD : 2 * width + 2 * HD],
        stats,
    )


def solution(mesh):
    rows = P(("fsdp", "rep"), None)
    weight = P("fsdp", None)
    return jax.shard_map(
        local,
        mesh=mesh,
        in_specs=(rows, rows, *[weight] * 7, P("fsdp"), P("fsdp"), P(), P(), rows),
        out_specs=(rows, rows, *[weight] * 7, P("fsdp"), P("fsdp"), P(), P(), P()),
        check_vma=False,
    )
```

```python
import math

import jax
import jax.numpy as jnp
from jax import lax
from jax.sharding import PartitionSpec as P

HD = 64
EPS = 1e-05
THETA = 1000000.0
NEG = -1e30
BF = jnp.bfloat16
F32 = jnp.float32


def matmul(left, right):
    return jnp.dot(left, right, preferred_element_type=F32)


def left_tmul(left, right):
    return lax.dot_general(left, right, (((0,), (0,)), ((), ())), preferred_element_type=F32)


def right_tmul(left, right):
    return lax.dot_general(left, right, (((1,), (1,)), ((), ())), preferred_element_type=F32)


def unit_rows(values):
    root = lax.rsqrt(jnp.mean(values * values, axis=-1, keepdims=True) + EPS)
    return values * root, root


def unit_back(unit, root, grad):
    return root * (grad - unit * jnp.mean(grad * unit, axis=-1, keepdims=True))


def rotate(values, cosine, sine):
    half = values.shape[-1] // 2
    first, second = values[..., :half], values[..., half:]
    return jnp.concatenate(
        [first * cosine - second * sine, second * cosine + first * sine], axis=-1
    )


def phases(segments):
    index = jnp.arange(segments.shape[1])
    same = segments[:, :, None] == segments[:, None, :]
    position = jnp.sum((same & (index[None, :] < index[:, None])).astype(jnp.int32), axis=2)
    frequency = jnp.exp(jnp.arange(HD // 2).astype(F32) * (-2.0 * math.log(THETA) / HD))
    phase = position.astype(F32)[:, :, None, None] * frequency
    return jnp.cos(phase), jnp.sin(phase), same & (index[None, :] <= index[:, None])


def move(values, send):
    ranks, copies = lax.axis_size("fsdp"), lax.axis_size("rep")
    pairs = []
    for f in range(ranks):
        for r in range(copies):
            to = send(f, r)
            if to is not None:
                pairs.append((f * copies + r, to[0] * copies + to[1]))
    return lax.ppermute(values, ("fsdp", "rep"), pairs)


def ring(values, step):
    ranks = lax.axis_size("fsdp")
    return move(values, lambda f, r: ((f + 2 * step) % ranks, r))


def swap_core(values):
    return move(values, lambda f, r: (f, r ^ 1))


def swap_x(values):
    return move(values, lambda f, r: (f, r ^ 2))


def swap_twin(values):
    return move(values, lambda f, r: (f ^ 1, r ^ 1))


def place():
    f, r = lax.axis_index("fsdp"), lax.axis_index("rep")
    return f // 2, f % 2, r // 2, r % 2


def pick(values, index, axis=0):
    return lax.dynamic_index_in_dim(values, index, axis, keepdims=False)


def ordered(slots, z):
    depth = len(slots)
    out = jnp.zeros((depth, *slots[0].shape), slots[0].dtype)
    for k, slot in enumerate(slots):
        out = lax.dynamic_update_index_in_dim(out, slot, (z - k) % depth, 0)
    return out


def both(own, other, first):
    return jnp.where(first == 0, jnp.stack([own, other]), jnp.stack([other, own]))


def gather_group(values):
    depth = lax.axis_size("fsdp") // 2
    half = values.shape[0] // 2
    rise, fall = values[:half], values[half:]
    slots = []
    for s in range(depth):
        if s > 0:
            rise, fall = ring(rise, 1), ring(fall, -1)
        here = jnp.concatenate([rise, fall], axis=0)
        slots.append(jnp.stack([here, swap_core(here)]))
    return jnp.stack(slots)


def scatter_group(partial):
    depth, _, rows = partial.shape[:3]
    half = rows // 2
    rise = fall = None
    for s in (*range(1, depth), 0):
        there = swap_core(partial[s, 1])
        total = partial[s, 0].astype(F32) + there.astype(F32)
        up, down = total[:half], total[half:]
        if rise is not None:
            up = up + ring(rise, 1).astype(F32)
            down = down + ring(fall, -1).astype(F32)
        rise, fall = up.astype(BF), down.astype(BF)
    return jnp.concatenate([rise, fall], axis=0)


def rows_to_columns(weight):
    z, y, x, core = place()
    rows, ranks, columns = weight.shape
    depth, half = ranks // 2, rows // 2
    mine = lax.dynamic_slice_in_dim(weight, x * half, half, axis=0)
    mine = pick(mine.reshape(half, depth, 2, columns), y ^ core, 2)
    slots = [ring(pick(mine, (z + k) % depth, 1), k) if k else pick(mine, z, 1) for k in range(depth)]
    same_x = ordered(slots, z)
    same_y = both(same_x, swap_x(same_x), x)
    whole = both(same_y, swap_twin(same_y), y)
    return whole.transpose(2, 0, 1, 3, 4).reshape(rows * ranks, columns)


def columns_to_rows(grad):
    z, y, x, core = place()
    ranks = lax.axis_size("fsdp")
    depth = ranks // 2
    rows, columns = grad.shape[0] // ranks, grad.shape[1]
    half = rows // 2
    blocks = grad.reshape(depth, 2, rows, columns).astype(BF)
    total = pick(blocks, y, 1).astype(F32) + swap_twin(pick(blocks, 1 - y, 1)).astype(F32)
    total = total.astype(BF).reshape(depth, 2, half, columns)
    total = pick(total, x, 1).astype(F32) + swap_x(pick(total, 1 - x, 1)).astype(F32)
    total = total.astype(BF)
    slots = [ring(pick(total, (z + k) % depth), k) if k else pick(total, z) for k in range(depth)]
    same_x = ordered(slots, z)
    same_core = both(same_x, swap_x(same_x), x)
    whole = both(same_core, swap_core(same_core), y ^ core)
    return whole.transpose(1, 3, 2, 0, 4).reshape(rows, ranks, columns)


def rows_here(weight):
    z, y, x, core = place()
    half = weight.shape[0] // 2
    part = lax.dynamic_slice_in_dim(weight, x * half, half, axis=0)
    part = move(part, lambda f, r: (f ^ 1, r) if r % 2 else None)
    other = move(part, lambda f, r: (f, r ^ 2) if r % 2 else None)
    return jnp.where(core == 0, weight, both(part, other, x).reshape(weight.shape))


def rows_sum(grad):
    z, y, x, core = place()
    rows, columns = grad.shape
    first, second = jnp.split(grad.astype(BF), 2, axis=0)
    crossed = move(
        jnp.where(core == 0, second, first),
        lambda f, r: (f ^ 1, r ^ 1) if r % 2 else (f, r ^ 1),
    )
    beside = move(second, lambda f, r: (f ^ 1, r) if r % 2 else None)
    total = jnp.where(core == 0, first, beside).astype(F32) + crossed.astype(F32)
    total = total.astype(BF).reshape(2, rows // 4, columns)
    quarter = pick(total, x).astype(F32) + swap_x(pick(total, 1 - x)).astype(F32)
    quarter = quarter.astype(BF)
    half = both(quarter, swap_x(quarter), x)
    return both(half, swap_core(half), core).reshape(rows, columns)


def gather_rows(values):
    return gather_group(values).reshape(-1, values.shape[1])


def scatter_rows(values):
    depth = lax.axis_size("fsdp") // 2
    return scatter_group(values.astype(BF).reshape(depth, 2, -1, values.shape[1]))


def local(
    tokens_in,
    segment_ids,
    w_query,
    w_key,
    w_value,
    w_out,
    w_gate,
    w_up,
    w_down,
    gain_attn,
    gain_ffn,
    gain_query,
    gain_key,
    d_out,
):
    ranks = lax.axis_size("fsdp")
    rank = lax.axis_index("fsdp")
    depth = ranks // 2
    z, y, x, core = place()
    width = tokens_in.shape[1]
    pack = segment_ids.shape[1]
    heads = w_query.shape[1] // HD
    kv_heads = w_key.shape[1] // HD
    share = max(1, ranks // kv_heads)
    q_here = heads // ranks
    kv_here = max(1, kv_heads // ranks)
    group = q_here // kv_here
    q_cols, kv_cols = q_here * HD, kv_here * HD
    scale = HD ** (-0.5)

    seg_size = segment_ids.size
    pieces = jnp.concatenate([segment_ids.reshape(-1).astype(BF), gain_attn, gain_ffn])
    pieces = [ring(pieces, k) if k else pieces for k in range(depth)]
    packs_here = segment_ids.shape[0] // 2
    seg_slots = []
    for s in range(depth):
        rise = pieces[s][:seg_size].reshape(2, packs_here, pack)[0]
        fall = pieces[(depth - s) % depth][:seg_size].reshape(2, packs_here, pack)[1]
        seg_slots.append(jnp.concatenate([rise, fall], axis=0))
    seg_slots = jnp.stack(seg_slots)
    segments = jnp.stack([seg_slots, swap_core(seg_slots)], axis=1).reshape(-1, pack)
    gains = ordered([piece[seg_size:] for piece in pieces], z)
    gains = both(gains, move(gains, lambda f, r: (f ^ 1, r)), y)
    gains = gains.reshape(2, depth, 2, -1).transpose(2, 1, 0, 3).reshape(2, -1).astype(F32)
    attn_gain, ffn_gain = gains[0], gains[1]
    q_gain = gain_query.astype(F32)
    k_gain = gain_key.astype(F32)

    def by_rank(weight, columns, repeats):
        split = weight.reshape(weight.shape[0], -1, columns)
        return jnp.repeat(split, repeats, axis=1) if repeats > 1 else split

    qkv_rows = jnp.concatenate(
        [
            by_rank(w_query, q_cols, 1),
            by_rank(w_key, kv_cols, share),
            by_rank(w_value, kv_cols, share),
        ],
        axis=2,
    )
    w_qkv = rows_to_columns(qkv_rows)
    w_out_here = rows_here(w_out)
    w_gate_here = rows_to_columns(w_gate.reshape(w_gate.shape[0], ranks, -1))
    w_up_here = rows_to_columns(w_up.reshape(w_up.shape[0], ranks, -1))
    w_down_here = rows_here(w_down)

    tokens = tokens_in.astype(F32)
    unit_tokens, root_tokens = unit_rows(tokens)
    attn_in = gather_rows((unit_tokens * attn_gain).astype(BF))
    g_ffn = gather_rows(d_out)
    cosine, sine, allowed = phases(segments)
    packs = segments.shape[0]
    total = packs * pack

    qkv = matmul(attn_in, w_qkv)
    q_raw = qkv[:, :q_cols].reshape(packs, pack, q_here, HD)
    k_raw = qkv[:, q_cols : q_cols + kv_cols].reshape(packs, pack, kv_here, HD)
    value = qkv[:, q_cols + kv_cols :].reshape(packs, pack, kv_here, HD).astype(BF)
    q_unit, q_root = unit_rows(q_raw)
    k_unit, k_root = unit_rows(k_raw)
    query = rotate(q_unit * q_gain, cosine, sine).astype(BF)
    query = query.reshape(packs, pack, kv_here, group, HD)
    key = rotate(k_unit * k_gain, cosine, sine).astype(BF)
    scores = jnp.einsum("pikgd,pjkd->pkgij", query, key, preferred_element_type=F32) * scale
    masked = jnp.where(allowed[:, None, None], scores, NEG)
    exponent = jnp.exp(masked - jnp.max(masked, axis=-1, keepdims=True))
    probs = exponent / jnp.sum(exponent, axis=-1, keepdims=True)
    probs_low = probs.astype(BF)
    mixed = jnp.einsum("pkgij,pjkd->pikgd", probs_low, value, preferred_element_type=F32)
    mixed = mixed.reshape(total, q_cols).astype(BF)
    attn_branch = scatter_rows(matmul(mixed, w_out_here)).astype(F32)

    middle = tokens + attn_branch
    unit_middle, root_middle = unit_rows(middle)
    ffn_in = gather_rows((unit_middle * ffn_gain).astype(BF))
    gate = matmul(ffn_in, w_gate_here)
    up = matmul(ffn_in, w_up_here)
    sig = jax.nn.sigmoid(gate)
    silu = gate * sig
    hidden = (silu * up).astype(BF)
    ffn_branch = scatter_rows(matmul(hidden, w_down_here)).astype(F32)
    block = middle + ffn_branch

    grad_down = left_tmul(hidden, g_ffn)
    g_hidden = right_tmul(g_ffn, w_down_here).astype(BF).astype(F32)
    g_gate = (g_hidden * up * sig * (1 + gate * (1 - sig))).astype(BF)
    g_up = (g_hidden * silu).astype(BF)
    g_ffn_in = scatter_rows(right_tmul(g_gate, w_gate_here) + right_tmul(g_up, w_up_here))
    g_ffn_in = g_ffn_in.astype(F32)
    grad_gate = left_tmul(ffn_in, g_gate)
    grad_up = left_tmul(ffn_in, g_up)
    ffn_gain_grad = jnp.sum(g_ffn_in * unit_middle, axis=0)
    g_middle = d_out.astype(F32) + unit_back(unit_middle, root_middle, g_ffn_in * ffn_gain)

    g_attn = gather_rows(g_middle.astype(BF))
    grad_out = left_tmul(mixed, g_attn)
    g_mixed = right_tmul(g_attn, w_out_here).astype(BF).reshape(packs, pack, kv_here, group, HD)
    g_probs = jnp.einsum("pikgd,pjkd->pkgij", g_mixed, value, preferred_element_type=F32)
    g_value = jnp.einsum("pkgij,pikgd->pjkd", probs_low, g_mixed, preferred_element_type=F32)
    g_scores = probs * (g_probs - jnp.sum(probs * g_probs, axis=-1, keepdims=True))
    g_scores = g_scores.astype(BF)
    g_query = jnp.einsum("pkgij,pjkd->pikgd", g_scores, key, preferred_element_type=F32) * scale
    g_key = jnp.einsum("pkgij,pikgd->pjkd", g_scores, query, preferred_element_type=F32) * scale
    q_back = rotate(g_query.reshape(packs, pack, q_here, HD), cosine, -sine)
    k_back = rotate(g_key, cosine, -sine)
    q_gain_grad = jnp.sum(q_back * q_unit, axis=(0, 1, 2))
    k_gain_grad = jnp.sum(k_back * k_unit, axis=(0, 1, 2))
    g_qkv = jnp.concatenate(
        [
            unit_back(q_unit, q_root, q_back * q_gain).reshape(total, q_cols),
            unit_back(k_unit, k_root, k_back * k_gain).reshape(total, kv_cols),
            g_value.reshape(total, kv_cols),
        ],
        axis=1,
    ).astype(BF)
    g_attn_in = scatter_rows(right_tmul(g_qkv, w_qkv)).astype(F32)
    grad_qkv = left_tmul(attn_in, g_qkv)
    attn_gain_grad = jnp.sum(g_attn_in * unit_tokens, axis=0)
    d_tokens = g_middle + unit_back(unit_tokens, root_tokens, g_attn_in * attn_gain)

    qkv_sum = columns_to_rows(grad_qkv)
    q_sum = qkv_sum[:, :, :q_cols].reshape(qkv_sum.shape[0], -1)
    kv_sum = qkv_sum[:, :, q_cols:]
    if share > 1:
        kv_sum = kv_sum.astype(F32).reshape(kv_sum.shape[0], -1, share, 2 * kv_cols).sum(axis=2)
    k_sum = kv_sum[:, :, :kv_cols].reshape(kv_sum.shape[0], -1)
    v_sum = kv_sum[:, :, kv_cols:].reshape(kv_sum.shape[0], -1)
    gate_sum = columns_to_rows(grad_gate).reshape(w_gate.shape)
    up_sum = columns_to_rows(grad_up).reshape(w_up.shape)
    out_sum = rows_sum(grad_out)
    down_sum = rows_sum(grad_down)
    squares = jnp.stack(
        [jnp.sum(item * item) for item in (middle, attn_branch, ffn_branch, block, d_tokens)]
    )
    small = jnp.concatenate([attn_gain_grad, ffn_gain_grad, q_gain_grad, k_gain_grad, squares])
    small = lax.psum(small, ("fsdp", "rep"))
    gain_rows = gain_attn.shape[0]
    attn_gain_sum = lax.dynamic_slice(small, (rank * gain_rows,), (gain_rows,))
    ffn_gain_sum = lax.dynamic_slice(small, (width + rank * gain_rows,), (gain_rows,))
    entries = tokens_in.shape[0] * ranks * lax.axis_size("rep") * width
    stats = jnp.sqrt(small[2 * width + 2 * HD :] / entries)
    return (
        block.astype(BF),
        d_tokens.astype(BF),
        q_sum.astype(F32),
        k_sum.astype(F32),
        v_sum.astype(F32),
        out_sum.astype(F32),
        gate_sum.astype(F32),
        up_sum.astype(F32),
        down_sum.astype(F32),
        attn_gain_sum,
        ffn_gain_sum,
        small[2 * width : 2 * width + HD],
        small[2 * width + HD : 2 * width + 2 * HD],
        stats,
    )


def solution(mesh):
    rows = P(("fsdp", "rep"), None)
    weight = P("fsdp", None)
    return jax.shard_map(
        local,
        mesh=mesh,
        in_specs=(rows, rows, *[weight] * 7, P("fsdp"), P("fsdp"), P(), P(), rows),
        out_specs=(rows, rows, *[weight] * 7, P("fsdp"), P("fsdp"), P(), P(), P()),
        check_vma=False,
    )
```

```python
import functools
import math

import jax
import jax.numpy as jnp
from jax import lax
from jax.experimental import pallas as pl
from jax.experimental.pallas import tpu as pltpu
from jax.sharding import PartitionSpec as P

HD = 64
EPS = 1e-05
THETA = 1000000.0
NEG = -1e30
BF = jnp.bfloat16
F32 = jnp.float32
ATTENTION_BYTES = 24 * 1024 * 1024
PLACE_BYTES = 24 * 1024 * 1024


def matmul(left, right):
    return jnp.dot(left, right, preferred_element_type=F32)


def left_tmul(left, right):
    return lax.dot_general(left, right, (((0,), (0,)), ((), ())), preferred_element_type=F32)


def right_tmul(left, right):
    return lax.dot_general(left, right, (((1,), (1,)), ((), ())), preferred_element_type=F32)


def unit_rows(values):
    root = lax.rsqrt(jnp.mean(values * values, axis=-1, keepdims=True) + EPS)
    return values * root, root


def unit_back(unit, root, grad):
    return root * (grad - unit * jnp.mean(grad * unit, axis=-1, keepdims=True))


def turn(values, cosine, sine):
    half = values.shape[-1] // 2
    swapped = jnp.concatenate([values[:, half:], values[:, :half]], axis=1)
    return values * cosine + swapped * sine


def phases(segments):
    index = jnp.arange(segments.shape[1])
    same = segments[:, :, None] == segments[:, None, :]
    position = jnp.sum((same & (index[None, :] < index[:, None])).astype(jnp.int32), axis=2)
    frequency = jnp.exp(jnp.arange(HD // 2).astype(F32) * (-2.0 * math.log(THETA) / HD))
    phase = position.astype(F32).reshape(-1, 1) * frequency
    cosine, sine = jnp.cos(phase), jnp.sin(phase)
    return jnp.concatenate([cosine, cosine], axis=1), jnp.concatenate([-sine, sine], axis=1)


def head(values, index):
    return values[:, index * HD : (index + 1) * HD]


def allowed_block(column, row):
    size = column.shape[0]
    later = lax.broadcasted_iota(jnp.int32, (size, size), 1)
    return (column == row) & (later <= lax.broadcasted_iota(jnp.int32, (size, size), 0))


def probabilities(query, key, allowed):
    scores = right_tmul(query, key) * HD ** (-0.5)
    exponent = jnp.where(allowed, jnp.exp(scores), 0.0)
    return exponent * (1.0 / jnp.sum(exponent, axis=-1, keepdims=True))


def attention_kernel(q_here, kv_here, *refs):
    (here_ref, other_ref, column_ref, row_ref, cos_ref, sin_ref, gain_ref, q_gain_ref, k_gain_ref) = refs[:9]
    w_qkv_ref, w_out_ref, attn_in_ref, qkv_ref, mixed_ref, own_ref, away_ref = refs[9:]
    group = q_here // kv_here
    rows = here_ref.shape[0]
    gain = gain_ref[...]
    for index, tokens_ref in enumerate((here_ref, other_ref)):
        unit, _ = unit_rows(tokens_ref[...].astype(F32))
        attn_in_ref[index * rows : (index + 1) * rows, :] = (unit * gain).astype(BF)
    qkv = matmul(attn_in_ref[...], w_qkv_ref[...])
    qkv_ref[...] = qkv
    blocks = [slice(index * rows, (index + 1) * rows) for index in range(2)]
    allowed = [allowed_block(column_ref[part, :], row_ref[index]) for index, part in enumerate(blocks)]
    cosine, sine = cos_ref[...], sin_ref[...]
    for kv in range(kv_here):
        key = turn(unit_rows(head(qkv, q_here + kv))[0] * k_gain_ref[...], cosine, sine).astype(BF)
        value = head(qkv, q_here + kv_here + kv).astype(BF)
        for h in range(kv * group, (kv + 1) * group):
            query = turn(unit_rows(head(qkv, h))[0] * q_gain_ref[...], cosine, sine).astype(BF)
            for index, part in enumerate(blocks):
                probs = probabilities(query[part], key[part], allowed[index])
                mixed_ref[part, h * HD : (h + 1) * HD] = matmul(probs.astype(BF), value[part]).astype(BF)
    mixed = mixed_ref[...]
    own_ref[...] = matmul(mixed[:rows], w_out_ref[...]).astype(BF)
    away_ref[...] = matmul(mixed[rows:], w_out_ref[...]).astype(BF)


def attention_back_kernel(q_here, kv_here, *refs):
    (here_ref, other_ref, qkv_ref, column_ref, row_ref, cos_ref, sin_ref, q_gain_ref, k_gain_ref) = refs[:9]
    w_qkv_ref, w_out_ref, g_attn_ref, g_qkv_ref, own_ref, away_ref, gains_ref = refs[9:]
    group = q_here // kv_here
    rows = here_ref.shape[0]
    g_attn_ref[:rows, :] = here_ref[...]
    g_attn_ref[rows:, :] = other_ref[...]
    g_mixed = right_tmul(g_attn_ref[...], w_out_ref[...]).astype(BF)
    qkv = qkv_ref[...]
    blocks = [slice(index * rows, (index + 1) * rows) for index in range(2)]
    allowed = [allowed_block(column_ref[part, :], row_ref[index]) for index, part in enumerate(blocks)]
    cosine, sine = cos_ref[...], sin_ref[...]
    q_gain, k_gain = q_gain_ref[...], k_gain_ref[...]
    scale = HD ** (-0.5)
    q_sum = jnp.zeros((1, HD), F32)
    k_sum = jnp.zeros((1, HD), F32)
    pieces = {}
    for kv in range(kv_here):
        k_unit, k_root = unit_rows(head(qkv, q_here + kv))
        key = turn(k_unit * k_gain, cosine, sine).astype(BF)
        value = head(qkv, q_here + kv_here + kv).astype(BF)
        g_k, g_v = [0.0, 0.0], [0.0, 0.0]
        for h in range(kv * group, (kv + 1) * group):
            q_unit, q_root = unit_rows(head(qkv, h))
            query = turn(q_unit * q_gain, cosine, sine).astype(BF)
            g_head = head(g_mixed, h)
            g_query = []
            for index, part in enumerate(blocks):
                probs = probabilities(query[part], key[part], allowed[index])
                g_probs = right_tmul(g_head[part], value[part])
                g_v[index] = g_v[index] + left_tmul(probs.astype(BF), g_head[part])
                g_scores = probs * (g_probs - jnp.sum(probs * g_probs, axis=-1, keepdims=True))
                g_scores = g_scores.astype(BF)
                g_k[index] = g_k[index] + left_tmul(g_scores, query[part])
                g_query.append(matmul(g_scores, key[part]))
            back = turn(jnp.concatenate(g_query, axis=0) * scale, cosine, -sine)
            q_sum = q_sum + jnp.sum(back * q_unit, axis=0, keepdims=True)
            pieces[h] = unit_back(q_unit, q_root, back * q_gain).astype(BF)
        back = turn(jnp.concatenate(g_k, axis=0) * scale, cosine, -sine)
        k_sum = k_sum + jnp.sum(back * k_unit, axis=0, keepdims=True)
        pieces[q_here + kv] = unit_back(k_unit, k_root, back * k_gain).astype(BF)
        pieces[q_here + kv_here + kv] = jnp.concatenate(g_v, axis=0).astype(BF)
    g_qkv = jnp.concatenate([pieces[index] for index in range(q_here + 2 * kv_here)], axis=1)
    g_qkv_ref[...] = g_qkv
    own_ref[...] = right_tmul(g_qkv[:rows], w_qkv_ref[...]).astype(BF)
    away_ref[...] = right_tmul(g_qkv[rows:], w_qkv_ref[...]).astype(BF)
    gains_ref[...] = jnp.concatenate([q_sum, k_sum], axis=0)


def in_vmem(count):
    return [pl.BlockSpec(memory_space=pltpu.VMEM)] * count


def attention(here, other, extras, w_qkv, w_out, q_here, kv_here):
    rows, width = here.shape
    wide = w_qkv.shape[1]
    return pl.pallas_call(
        functools.partial(attention_kernel, q_here, kv_here),
        in_specs=in_vmem(11),
        out_specs=in_vmem(5),
        out_shape=[
            jax.ShapeDtypeStruct((2 * rows, width), BF),
            jax.ShapeDtypeStruct((2 * rows, wide), F32),
            jax.ShapeDtypeStruct((2 * rows, q_here * HD), BF),
            jax.ShapeDtypeStruct((rows, width), BF),
            jax.ShapeDtypeStruct((rows, width), BF),
        ],
        compiler_params=pltpu.CompilerParams(vmem_limit_bytes=ATTENTION_BYTES),
        cost_estimate=pl.CostEstimate(
            flops=16 * rows * width * wide, bytes_accessed=40 * rows * width, transcendentals=0
        ),
        name="attention",
    )(here, other, *extras, w_qkv, w_out)


def attention_back(here, other, qkv, extras, w_qkv, w_out, q_here, kv_here):
    rows, width = here.shape
    wide = w_qkv.shape[1]
    return pl.pallas_call(
        functools.partial(attention_back_kernel, q_here, kv_here),
        in_specs=in_vmem(11),
        out_specs=in_vmem(5),
        out_shape=[
            jax.ShapeDtypeStruct((2 * rows, width), BF),
            jax.ShapeDtypeStruct((2 * rows, wide), BF),
            jax.ShapeDtypeStruct((rows, width), BF),
            jax.ShapeDtypeStruct((rows, width), BF),
            jax.ShapeDtypeStruct((2, HD), F32),
        ],
        compiler_params=pltpu.CompilerParams(vmem_limit_bytes=ATTENTION_BYTES),
        cost_estimate=pl.CostEstimate(
            flops=16 * rows * width * wide, bytes_accessed=40 * rows * width, transcendentals=0
        ),
        name="attention_back",
    )(here, other, qkv, *extras, w_qkv, w_out)


def place_kernel(starts, widths, row_ref, column_ref, *refs):
    source_refs, out_refs = refs[: len(starts)], refs[len(starts) :]
    step = pl.program_id(0)
    ends = [*starts[1:], pl.num_programs(0)]
    for source_ref, start, end in zip(source_refs, starts, ends):

        @pl.when((step >= start) & (step < end))
        def _(source_ref=source_ref):
            first = 0
            for width, out_ref in zip(widths, out_refs):
                block = source_ref[0, :, first : first + width].astype(out_ref.dtype)
                out_ref[...] = block.reshape(out_ref.shape)
                first += width


def place_blocks(sources, row_blocks, column_blocks, row_count, column_count, widths, dtype, rows):
    columns = sources[0].shape[2]
    counts = [source.shape[0] for source in sources]
    starts = [sum(counts[:index]) for index in range(len(counts))]

    def source_spec(start, count):
        return pl.BlockSpec(
            (1, rows, columns),
            lambda step, row, column: (jnp.clip(step - start, 0, count - 1), 0, 0),
        )

    if column_count > 1 and any(width % 128 for width in widths):
        widths = [columns]
        shapes = [(column_count, row_count * rows, columns)]
        out_specs = [
            pl.BlockSpec((1, rows, columns), lambda step, row, column: (column[step], row[step], 0))
        ]
    else:
        shapes = [(row_count * rows, column_count * width) for width in widths]
        out_specs = [
            pl.BlockSpec((rows, width), lambda step, row, column: (row[step], column[step]))
            for width in widths
        ]
    return pl.pallas_call(
        functools.partial(place_kernel, starts, widths),
        grid_spec=pltpu.PrefetchScalarGridSpec(
            num_scalar_prefetch=2,
            grid=(sum(counts),),
            in_specs=[source_spec(start, count) for start, count in zip(starts, counts)],
            out_specs=out_specs,
        ),
        out_shape=[jax.ShapeDtypeStruct(shape, dtype) for shape in shapes],
        compiler_params=pltpu.CompilerParams(vmem_limit_bytes=PLACE_BYTES),
        name="place_blocks",
    )(row_blocks.astype(jnp.int32), column_blocks.astype(jnp.int32), *sources)


def after(values, *others):
    return lax.optimization_barrier((values, *others))[0]


def move(values, send):
    ranks, copies = lax.axis_size("fsdp"), lax.axis_size("rep")
    pairs = []
    for f in range(ranks):
        for r in range(copies):
            to = send(f, r)
            if to is not None:
                pairs.append((f * copies + r, to[0] * copies + to[1]))
    return lax.ppermute(values, ("fsdp", "rep"), pairs)


def ring(values, step):
    ranks = lax.axis_size("fsdp")
    return move(values, lambda f, r: ((f + 2 * step) % ranks, r))


def swap_core(values):
    return move(values, lambda f, r: (f, r ^ 1))


def swap_x(values):
    return move(values, lambda f, r: (f, r ^ 2))


def swap_twin(values):
    return move(values, lambda f, r: (f ^ 1, r ^ 1))


def place():
    f, r = lax.axis_index("fsdp"), lax.axis_index("rep")
    return f // 2, f % 2, r // 2, r % 2


def pick(values, index, axis=0):
    return lax.dynamic_index_in_dim(values, index, axis, keepdims=False)


def ordered(slots, z):
    depth = len(slots)
    out = jnp.zeros((depth, *slots[0].shape), slots[0].dtype)
    for k, slot in enumerate(slots):
        out = lax.dynamic_update_index_in_dim(out, slot, (z - k) % depth, 0)
    return out


def add(left, right):
    return (left.astype(F32) + right.astype(F32)).astype(BF)


def gather_group(values, name):
    slots = []
    for s in range(lax.axis_size("fsdp") // 2):
        with jax.named_scope(f"gather_{name}_{s}"):
            if s > 0:
                values = ring(values, 1)
            slots.append((values, swap_core(values)))
    return slots


def scatter_group(partial, name, beside=None):
    moving = None
    for step, (own, away) in enumerate((*partial[1:], partial[0])):
        with jax.named_scope(f"scatter_{name}_{step}"):
            total = own.astype(F32) + swap_core(away).astype(F32)
            if moving is not None:
                total = total + ring(moving, 1).astype(F32)
            moving = total.astype(BF)
        if beside is not None:
            beside(step, moving)
    return total


def total_sum(values):
    for bit in range(2):
        values = values + move(values, lambda f, r: (f, r ^ (1 << bit)))
    for bit in range((lax.axis_size("fsdp") - 1).bit_length()):
        values = values + move(values, lambda f, r: (f ^ (1 << bit), r))
    return values


def columns_in(cut, rows, y_first, name):
    z, y, x, core = place()
    depth = lax.axis_size("fsdp") // 2
    slots = []
    with jax.named_scope(f"{name}_along_z"):
        for k in range(depth):
            part = cut(2 * ((z + k) % depth) + (y ^ core))
            slots.append(ring(part, k) if k else part)
        same = jnp.stack(slots)
    with jax.named_scope(f"{name}_across"):
        across_x, across_y = swap_x(same), swap_twin(same)
    with jax.named_scope(f"{name}_across_both"):
        rest = swap_x(across_y) if y_first else swap_twin(across_x)
    where_z = (z - jnp.arange(depth)) % depth
    index = lambda yy, xx: (where_z * 2 + yy) * 2 + xx
    places = [index(y, x), index(y, 1 - x), index(1 - y, x), index(1 - y, 1 - x)]
    places = jnp.concatenate(places)
    sources = [same, across_x, across_y, rest]
    joined = place_blocks(sources, places, jnp.zeros_like(places), 4 * depth, 1, [same.shape[2]], BF, rows)[0]
    return joined, same, across_y


def scoped(step):
    def wrap(method):
        def named(self):
            with jax.named_scope(f"{self.name}_{step}"):
                return method(self)

        return named

    return wrap


class ColumnsOut:
    def __init__(self, grad, y_first, name):
        self.name = name
        z, y, x, core = place()
        self.depth = lax.axis_size("fsdp") // 2
        self.y_first = y_first
        columns = grad.shape[1]
        self.blocks = grad.reshape(self.depth, 2, 2, -1, columns)
        axis, index = (1, 1 - y) if y_first else (2, 1 - x)
        self.payload = pick(self.blocks, index, axis)

    @scoped("first")
    def first(self):
        z, y, x, core = place()
        axis, index = (1, y) if self.y_first else (2, x)
        swap = swap_twin if self.y_first else swap_x
        came, own = swap(self.payload), pick(self.blocks, index, axis)
        here, there = (x, 1 - x) if self.y_first else (y, 1 - y)
        self.payload = add(pick(own, there, 1), pick(came, there, 1))
        self.kept = (pick(own, here, 1), pick(came, here, 1))

    @scoped("second")
    def second(self):
        z, y, x, core = place()
        swap = swap_x if self.y_first else swap_twin
        came = swap(self.payload).astype(F32)
        total = (self.kept[0].astype(F32) + self.kept[1].astype(F32) + came).astype(BF)
        self.payload = [pick(total, (z + k) % self.depth) for k in range(self.depth)]

    @scoped("third")
    def third(self):
        slots = [ring(part, k) if k else part for k, part in enumerate(self.payload)]
        self.payload = jnp.stack(slots)

    @scoped("last")
    def last(self):
        same = self.payload
        across = swap_x(same)
        return same, across, swap_core(same), swap_core(across)


def columns_placed(parts, widths):
    z, y, x, core = place()
    depth = parts[0].shape[0]
    ones = jnp.ones((depth,), jnp.int32)
    rows = jnp.concatenate([x * ones, (1 - x) * ones] * 2)
    where_z = (z - jnp.arange(depth)) % depth
    own, other = 2 * where_z + (y ^ core), 2 * where_z + (1 - (y ^ core))
    columns = jnp.concatenate([own, own, other, other])
    return place_blocks(parts, rows, columns, 2, 2 * depth, widths, F32, parts[0].shape[1])


def rows_here(weights):
    z, y, x, core = place()
    halves = [weight.shape[0] // 2 for weight in weights]
    parts = [lax.dynamic_slice_in_dim(w, x * half, half, axis=0) for w, half in zip(weights, halves)]
    part = jnp.concatenate(parts, axis=0)
    with jax.named_scope("w_down_across"):
        part = move(part, lambda f, r: (f ^ 1, r) if r % 2 else None)
        other = move(part, lambda f, r: (f, r ^ 2) if r % 2 else None)
    out, first = [], 0
    for weight, half in zip(weights, halves):
        mine, its = part[first : first + half], other[first : first + half]
        low = jnp.where(core == 0, weight[:half], jnp.where(x == 0, mine, its))
        high = jnp.where(core == 0, weight[half:], jnp.where(x == 0, its, mine))
        out.append(jnp.concatenate([low, high], axis=0))
        first += half
    return out


class RowsOut:
    def __init__(self, grad, name):
        self.name = name
        self.grad = self.payload = grad

    @scoped("first")
    def first(self):
        z, y, x, core = place()
        came = move(self.payload, lambda f, r: (f ^ 1, r ^ 1) if r % 2 else None)
        half = self.grad.shape[0] // 2
        part = lambda array, index: lax.dynamic_slice_in_dim(array, index * half, half, axis=0)
        self.payload = add(part(self.grad, 1 - x), part(came, 1 - x))
        self.kept = (part(self.grad, x), part(came, x))

    @scoped("second")
    def second(self):
        came = move(self.payload, lambda f, r: None if r % 2 else (f, r ^ 2)).astype(F32)
        self.payload = (self.kept[0].astype(F32) + self.kept[1].astype(F32) + came).astype(BF)

    @scoped("third")
    def third(self):
        came = move(self.payload, lambda f, r: None if r % 2 else (f, r ^ 2))
        self.payload = jnp.stack([self.payload, came])

    @scoped("last")
    def last(self):
        z, y, x, core = place()
        came = move(self.payload, lambda f, r: None if r % 2 else (f, r ^ 1))
        parts = jnp.where(core == 0, self.payload, came)
        places = jnp.stack([x, 1 - x])
        rows, columns = parts.shape[1:]
        return place_blocks([parts], places, jnp.zeros_like(places), 2, 1, [columns], F32, rows)[0]


def local(
    tokens_in,
    segment_ids,
    w_query,
    w_key,
    w_value,
    w_out,
    w_gate,
    w_up,
    w_down,
    gain_attn,
    gain_ffn,
    gain_query,
    gain_key,
    d_out,
):
    ranks = lax.axis_size("fsdp")
    rank = lax.axis_index("fsdp")
    depth = ranks // 2
    z, y, x, core = place()
    width = tokens_in.shape[1]
    pack = segment_ids.shape[1]
    heads = w_query.shape[1] // HD
    kv_heads = w_key.shape[1] // HD
    share = max(1, ranks // kv_heads)
    q_here = heads // ranks
    kv_here = max(1, kv_heads // ranks)
    group = q_here // kv_here
    q_cols, kv_cols = q_here * HD, kv_here * HD
    scale = HD ** (-0.5)

    q_gain = gain_query.astype(F32)[None]
    k_gain = gain_key.astype(F32)[None]

    token_slots = gather_group(tokens_in, "tokens")
    rows_x = w_query.shape[0] // 2
    cut = lambda weight, start, size: lax.dynamic_slice(weight, (x * rows_x, start), (rows_x, size))
    wide = q_cols + 2 * kv_cols
    seg_size = segment_ids.size
    extra = jnp.concatenate([segment_ids.reshape(-1).astype(BF), gain_attn, gain_ffn])
    extra = jnp.pad(extra, (0, 16 * wide - extra.size)).reshape(16, wide)

    def cut_qkv(block):
        kv = block // share * kv_cols
        parts = [cut(w_query, block * q_cols, q_cols), cut(w_key, kv, kv_cols), cut(w_value, kv, kv_cols)]
        return jnp.concatenate([jnp.concatenate(parts, axis=1), extra], axis=0)

    def cutter(weight):
        size = weight.shape[1] // ranks
        return lambda block: cut(weight, block * size, size)

    w_qkv, own_slots, twin_slots = columns_in(cut_qkv, rows_x, False, "w_qkv")
    w_out_here, w_down_here = rows_here((w_out, w_down))
    own_extra = own_slots[:, rows_x:].reshape(depth, -1)
    twin_extra = twin_slots[:, rows_x:].reshape(depth, -1)
    seg_slots = own_extra[:, :seg_size].reshape(depth, 1, -1, pack)
    segments = jnp.concatenate([seg_slots, swap_core(seg_slots)], axis=1).reshape(-1, pack).astype(jnp.int32)
    span = slice(seg_size, seg_size + 2 * gain_attn.size)
    pieces = jnp.stack([own_extra[:, span], twin_extra[:, span]], axis=1)
    pieces = ordered([pieces[k] for k in range(depth)], z).astype(F32)
    pieces = jnp.where(y == 0, pieces, pieces[:, ::-1])
    gains = pieces.reshape(depth, 2, 2, -1).transpose(2, 0, 1, 3).reshape(2, -1)
    attn_gain, ffn_gain = gains[0], gains[1]

    w_gate_here, gate_slots, _ = columns_in(cutter(after(w_gate, token_slots[-1][0])), rows_x, False, "w_gate")
    w_up_here, _, _ = columns_in(cutter(after(w_up, gate_slots)), rows_x, True, "w_up")

    cosine, sine = phases(segments)
    block_rows = tokens_in.shape[0]
    marks = segments + 4 * (jnp.arange(segments.shape[0], dtype=jnp.int32) % (block_rows // pack))[:, None]
    column = marks.reshape(depth, 2 * block_rows, 1)
    row = marks.reshape(depth, 2, 1, block_rows)
    cosine, sine = cosine.reshape(depth, -1, HD), sine.reshape(depth, -1, HD)
    kept, partial = [], []
    for s, (here, other) in enumerate(token_slots):
        extras = (column[s], row[s], cosine[s], sine[s], attn_gain[None], q_gain, k_gain)
        *keep, own, away = attention(here, other, extras, w_qkv, w_out_here, q_here, kv_here)
        kept.append(keep)
        partial.append((own, away))
    tokens = tokens_in.astype(F32)
    unit_tokens, root_tokens = unit_rows(tokens)
    attn_branch = scatter_group(partial, "attn_branch")

    middle = tokens + attn_branch
    unit_middle, root_middle = unit_rows(middle)
    ffn_slots = gather_group((unit_middle * ffn_gain).astype(BF), "ffn_in")
    grad_slots = gather_group(after(d_out, ffn_slots[-1][0]), "d_out")
    glu_kept, back_partial, down_partial = [], [], []
    for pair, grad_pair in zip(ffn_slots, grad_slots):
        ffn_in = jnp.concatenate(pair, axis=0)
        g_ffn = jnp.concatenate(grad_pair, axis=0)
        gate, up = matmul(ffn_in, w_gate_here), matmul(ffn_in, w_up_here)
        sig = jax.nn.sigmoid(gate)
        silu = gate * sig
        hidden = (silu * up).astype(BF)
        g_hidden = right_tmul(g_ffn, w_down_here).astype(BF).astype(F32)
        g_gate = (g_hidden * up * sig * (1 + gate * (1 - sig))).astype(BF)
        g_up = (g_hidden * silu).astype(BF)
        part = (right_tmul(g_gate, w_gate_here) + right_tmul(g_up, w_up_here)).astype(BF)
        back_partial.append((part[:block_rows], part[block_rows:]))
        glu_kept.append((ffn_in, g_ffn, hidden, g_gate, g_up))
    ffn_in, g_ffn, hidden, g_gate, g_up = (jnp.concatenate(items, axis=0) for items in zip(*glu_kept))
    out_steps = {}

    def beside(step, sent):
        if step == 0:
            grad = left_tmul(*after((hidden, g_ffn), sent)).astype(BF)
            name = "down"
            out_steps[name] = RowsOut(grad, "sum_" + name)
        if step == 1:
            grad = left_tmul(*after((ffn_in, g_gate), sent)).astype(BF)
            name = "gate"
            out_steps[name] = ColumnsOut(grad, True, "sum_" + name)
        if step == 2:
            grad = left_tmul(*after((ffn_in, g_up), sent)).astype(BF)
            name = "up"
            out_steps[name] = ColumnsOut(grad, False, "sum_" + name)

    g_ffn_in = scatter_group(back_partial, "g_ffn_in", beside)
    down_steps, gate_steps, up_steps = (out_steps[name] for name in ("down", "gate", "up"))
    g_ffn_in = after(g_ffn_in, down_steps.payload, gate_steps.payload, up_steps.payload)
    ffn_gain_grad = jnp.sum(g_ffn_in * unit_middle, axis=0)
    g_middle = d_out.astype(F32) + unit_back(unit_middle, root_middle, g_ffn_in * ffn_gain)

    attn_slots = gather_group(g_middle.astype(BF), "g_attn")
    down_steps.first()
    up_steps.first()
    back_kept, partial = [None] * depth, [None] * depth
    head_gains = 0.0
    for s in (*range(1, depth), 0):
        here, other = attn_slots[s]
        if s == min(2, depth - 1):
            here = after(here, down_steps.payload, up_steps.payload)
            down_steps.second()
        if s == min(3, depth - 1):
            here = after(here, down_steps.payload)
            gate_steps.first()
            up_steps.second()
            down_steps.third()
        extras = (column[s], row[s], cosine[s], sine[s], q_gain, k_gain)
        g_attn, g_qkv, own, away, gain_part = attention_back(
            here, other, kept[s][1], extras, w_qkv, w_out_here, q_here, kv_here
        )
        head_gains = head_gains + gain_part
        back_kept[s] = (g_attn, g_qkv)
        partial[s] = (own, away)
    attn_in, _, mixed = (jnp.concatenate(items, axis=0) for items in zip(*kept))
    g_attn, g_qkv = (jnp.concatenate(items, axis=0) for items in zip(*back_kept))

    def beside_back(step, sent):
        if step == 0:
            grad = left_tmul(*after((attn_in, g_qkv), sent)).astype(BF)
            name = "qkv"
            out_steps[name] = ColumnsOut(grad, True, "sum_" + name)
        if step == 1:
            grad = left_tmul(*after((mixed, g_attn), sent)).astype(BF)
            name = "out"
            out_steps[name] = RowsOut(grad, "sum_" + name)

    g_attn_in = scatter_group(partial, "g_attn_in", beside_back)
    g_attn_in = after(g_attn_in, gate_steps.payload, up_steps.payload, out_steps["qkv"].payload)
    attn_gain_grad = jnp.sum(g_attn_in * unit_tokens, axis=0)
    d_tokens = g_middle + unit_back(unit_tokens, root_tokens, g_attn_in * attn_gain)

    for s in range(depth):
        part = matmul(after(glu_kept[s][2], attn_slots[-1][0]), w_down_here).astype(BF)
        down_partial.append((part[:block_rows], part[block_rows:]))
    ffn_branch = scatter_group(down_partial, "ffn_branch")
    block = middle + ffn_branch

    qkv_steps, out_proj_steps = out_steps["qkv"], out_steps["out"]
    gate_steps.second()
    for steps in (qkv_steps, out_proj_steps):
        steps.first()
        steps.second()
    for steps in (up_steps, gate_steps, qkv_steps, out_proj_steps):
        steps.third()
    qkv_sum = columns_placed(qkv_steps.last(), [q_cols, 2 * kv_cols])
    if len(qkv_sum) == 2:
        q_sum = qkv_sum[0]
        kv_sum = qkv_sum[1].reshape(q_sum.shape[0], ranks, 2 * kv_cols)
    else:
        rows = qkv_sum[0].transpose(1, 0, 2)
        q_sum = rows[:, :, :q_cols].reshape(rows.shape[0], -1)
        kv_sum = rows[:, :, q_cols:]
    if share > 1:
        kv_sum = kv_sum.reshape(kv_sum.shape[0], -1, share, 2 * kv_cols).sum(axis=2)
    k_sum = kv_sum[:, :, :kv_cols].reshape(kv_sum.shape[0], -1)
    v_sum = kv_sum[:, :, kv_cols:].reshape(kv_sum.shape[0], -1)
    (up_sum,) = columns_placed(up_steps.last(), [w_up_here.shape[1]])
    (gate_sum,) = columns_placed(gate_steps.last(), [w_gate_here.shape[1]])
    out_sum = out_proj_steps.last()
    down_sum = down_steps.last()
    squares = jnp.stack(
        [jnp.sum(item * item) for item in (middle, attn_branch, ffn_branch, block, d_tokens)]
    )
    small = jnp.concatenate([attn_gain_grad, ffn_gain_grad, head_gains[0], head_gains[1], squares])
    with jax.named_scope("total_sum"):
        small = total_sum(small)
    gain_rows = gain_attn.shape[0]
    attn_gain_sum = lax.dynamic_slice(small, (rank * gain_rows,), (gain_rows,))
    ffn_gain_sum = lax.dynamic_slice(small, (width + rank * gain_rows,), (gain_rows,))
    entries = tokens_in.shape[0] * ranks * lax.axis_size("rep") * width
    stats = jnp.sqrt(small[2 * width + 2 * HD :] / entries)
    return (
        block.astype(BF),
        d_tokens.astype(BF),
        q_sum,
        k_sum,
        v_sum,
        out_sum,
        gate_sum,
        up_sum,
        down_sum,
        attn_gain_sum,
        ffn_gain_sum,
        small[2 * width : 2 * width + HD],
        small[2 * width + HD : 2 * width + 2 * HD],
        stats,
    )


def solution(mesh):
    rows = P(("fsdp", "rep"), None)
    weight = P("fsdp", None)
    return jax.shard_map(
        local,
        mesh=mesh,
        in_specs=(rows, rows, *[weight] * 7, P("fsdp"), P("fsdp"), P(), P(), rows),
        out_specs=(rows, rows, *[weight] * 7, P("fsdp"), P("fsdp"), P(), P(), P()),
        check_vma=False,
    )
```

```python
import functools
import math

import jax
import jax.numpy as jnp
from jax import lax
from jax.experimental import pallas as pl
from jax.experimental.pallas import tpu as pltpu
from jax.sharding import PartitionSpec as P

HD = 64
EPS = 1e-05
THETA = 1000000.0
NEG = -1e30
BF = jnp.bfloat16
F32 = jnp.float32
ATTENTION_BYTES = 24 * 1024 * 1024
PLACE_BYTES = 44 * 1024 * 1024
LOW_COST = pl.CostEstimate(flops=1, bytes_accessed=1, transcendentals=0)


def matmul(left, right):
    return jnp.dot(left, right, preferred_element_type=F32)


def left_tmul(left, right):
    return lax.dot_general(left, right, (((0,), (0,)), ((), ())), preferred_element_type=F32)


def right_tmul(left, right):
    return lax.dot_general(left, right, (((1,), (1,)), ((), ())), preferred_element_type=F32)


def unit_rows(values):
    root = lax.rsqrt(jnp.mean(values * values, axis=-1, keepdims=True) + EPS)
    return values * root, root


def unit_back(unit, root, grad):
    return root * (grad - unit * jnp.mean(grad * unit, axis=-1, keepdims=True))


def turn(values, cosine, sine):
    half = values.shape[-1] // 2
    swapped = jnp.concatenate([values[:, half:], values[:, :half]], axis=1)
    return values * cosine + swapped * sine


def token_table(segments, width):
    index = jnp.arange(segments.shape[1])
    same = segments[:, :, None] == segments[:, None, :]
    position = jnp.sum((same & (index[None, :] < index[:, None])).astype(jnp.int32), axis=2)
    frequency = jnp.exp(jnp.arange(HD // 2).astype(F32) * (-2.0 * math.log(THETA) / HD))
    phase = position.astype(F32).reshape(-1, 1) * frequency
    cosine, sine = jnp.cos(phase), jnp.sin(phase)
    packs = jnp.arange(segments.shape[0], dtype=jnp.int32) % (width // segments.shape[1])
    marks = (segments + 4 * packs[:, None]).astype(F32).reshape(-1, 1)
    marks = jnp.broadcast_to(marks, (marks.shape[0], width))
    return jnp.concatenate([cosine, cosine, -sine, sine, marks], axis=1)


def head(values, index):
    return values[:, index * HD : (index + 1) * HD]


def allowed_block(marks):
    later = lax.broadcasted_iota(jnp.int32, marks.shape, 1)
    return (marks == marks.T) & (later <= lax.broadcasted_iota(jnp.int32, marks.shape, 0))


def probabilities(query, key, allowed):
    scores = right_tmul(query, key) * HD ** (-0.5)
    exponent = jnp.where(allowed, jnp.exp(scores), 0.0)
    return exponent * (1.0 / jnp.sum(exponent, axis=-1, keepdims=True))


def attention_kernel(q_here, kv_here, *refs):
    here_ref, other_ref, table_ref, gain_ref, q_gain_ref, k_gain_ref, w_qkv_ref, w_out_ref = refs[:8]
    attn_in_ref, qkv_ref, mixed_ref, own_ref, away_ref = refs[8:]
    group = q_here // kv_here
    rows = here_ref.shape[0]
    gain = gain_ref[...]
    for index, tokens_ref in enumerate((here_ref, other_ref)):
        unit, _ = unit_rows(tokens_ref[...].astype(F32))
        attn_in_ref[index * rows : (index + 1) * rows, :] = (unit * gain).astype(BF)
    qkv = matmul(attn_in_ref[...], w_qkv_ref[...])
    qkv_ref[...] = qkv
    blocks = [slice(index * rows, (index + 1) * rows) for index in range(2)]
    allowed = [allowed_block(table_ref[part, 2 * HD :]) for part in blocks]
    cosine, sine = table_ref[:, :HD], table_ref[:, HD : 2 * HD]
    for kv in range(kv_here):
        key = turn(unit_rows(head(qkv, q_here + kv))[0] * k_gain_ref[...], cosine, sine).astype(BF)
        value = head(qkv, q_here + kv_here + kv).astype(BF)
        for h in range(kv * group, (kv + 1) * group):
            query = turn(unit_rows(head(qkv, h))[0] * q_gain_ref[...], cosine, sine).astype(BF)
            for index, part in enumerate(blocks):
                probs = probabilities(query[part], key[part], allowed[index])
                mixed_ref[part, h * HD : (h + 1) * HD] = matmul(probs.astype(BF), value[part]).astype(BF)
    mixed = mixed_ref[...]
    own_ref[...] = matmul(mixed[:rows], w_out_ref[...]).astype(BF)
    away_ref[...] = matmul(mixed[rows:], w_out_ref[...]).astype(BF)


def attention_back_kernel(q_here, kv_here, *refs):
    here_ref, other_ref, qkv_ref, table_ref, q_gain_ref, k_gain_ref, w_qkv_ref, w_out_ref = refs[:8]
    g_attn_ref, g_qkv_ref, own_ref, away_ref, gains_ref = refs[8:]
    group = q_here // kv_here
    rows = here_ref.shape[0]
    g_attn_ref[:rows, :] = here_ref[...]
    g_attn_ref[rows:, :] = other_ref[...]
    g_mixed = right_tmul(g_attn_ref[...], w_out_ref[...]).astype(BF)
    qkv = qkv_ref[...]
    blocks = [slice(index * rows, (index + 1) * rows) for index in range(2)]
    allowed = [allowed_block(table_ref[part, 2 * HD :]) for part in blocks]
    cosine, sine = table_ref[:, :HD], table_ref[:, HD : 2 * HD]
    q_gain, k_gain = q_gain_ref[...], k_gain_ref[...]
    scale = HD ** (-0.5)
    q_sum = jnp.zeros((1, HD), F32)
    k_sum = jnp.zeros((1, HD), F32)
    pieces = {}
    for kv in range(kv_here):
        k_unit, k_root = unit_rows(head(qkv, q_here + kv))
        key = turn(k_unit * k_gain, cosine, sine).astype(BF)
        value = head(qkv, q_here + kv_here + kv).astype(BF)
        g_k, g_v = [0.0, 0.0], [0.0, 0.0]
        for h in range(kv * group, (kv + 1) * group):
            q_unit, q_root = unit_rows(head(qkv, h))
            query = turn(q_unit * q_gain, cosine, sine).astype(BF)
            g_head = head(g_mixed, h)
            g_query = []
            for index, part in enumerate(blocks):
                probs = probabilities(query[part], key[part], allowed[index])
                g_probs = right_tmul(g_head[part], value[part])
                g_v[index] = g_v[index] + left_tmul(probs.astype(BF), g_head[part])
                g_scores = probs * (g_probs - jnp.sum(probs * g_probs, axis=-1, keepdims=True))
                g_scores = g_scores.astype(BF)
                g_k[index] = g_k[index] + left_tmul(g_scores, query[part])
                g_query.append(matmul(g_scores, key[part]))
            back = turn(jnp.concatenate(g_query, axis=0) * scale, cosine, -sine)
            q_sum = q_sum + jnp.sum(back * q_unit, axis=0, keepdims=True)
            pieces[h] = unit_back(q_unit, q_root, back * q_gain).astype(BF)
        back = turn(jnp.concatenate(g_k, axis=0) * scale, cosine, -sine)
        k_sum = k_sum + jnp.sum(back * k_unit, axis=0, keepdims=True)
        pieces[q_here + kv] = unit_back(k_unit, k_root, back * k_gain).astype(BF)
        pieces[q_here + kv_here + kv] = jnp.concatenate(g_v, axis=0).astype(BF)
    g_qkv = jnp.concatenate([pieces[index] for index in range(q_here + 2 * kv_here)], axis=1)
    g_qkv_ref[...] = g_qkv
    own_ref[...] = right_tmul(g_qkv[:rows], w_qkv_ref[...]).astype(BF)
    away_ref[...] = right_tmul(g_qkv[rows:], w_qkv_ref[...]).astype(BF)
    gains_ref[...] = jnp.concatenate([q_sum, k_sum], axis=0)


def single(array, block=None, index=0):
    block = array.shape if block is None else block
    return pl.BlockSpec(block, lambda step: (index,) + (0,) * (len(block) - 1))


def slot_call(kernel, name, arrays, specs, shapes):
    return pl.pallas_call(
        kernel,
        grid=(1,),
        in_specs=specs,
        out_specs=[single(shape) for shape in shapes],
        out_shape=shapes,
        compiler_params=pltpu.CompilerParams(vmem_limit_bytes=ATTENTION_BYTES),
        cost_estimate=LOW_COST,
        name=name,
    )(*arrays)


def attention(slot, here, other, table, gain, q_gain, k_gain, w_qkv, w_out, q_here, kv_here):
    rows, width = here.shape
    arrays = (here, other, table, gain, q_gain, k_gain, w_qkv, w_out)
    specs = [single(array) for array in arrays]
    specs[2] = single(table, (2 * rows, table.shape[1]), slot)
    shapes = [
        jax.ShapeDtypeStruct((2 * rows, width), BF),
        jax.ShapeDtypeStruct((2 * rows, w_qkv.shape[1]), F32),
        jax.ShapeDtypeStruct((2 * rows, q_here * HD), BF),
        jax.ShapeDtypeStruct((rows, width), BF),
        jax.ShapeDtypeStruct((rows, width), BF),
    ]
    kernel = functools.partial(attention_kernel, q_here, kv_here)
    return slot_call(kernel, "attention", arrays, specs, shapes)


def attention_back(slot, here, other, qkv, table, q_gain, k_gain, w_qkv, w_out, q_here, kv_here):
    rows, width = here.shape
    arrays = (here, other, qkv, table, q_gain, k_gain, w_qkv, w_out)
    specs = [single(array) for array in arrays]
    specs[3] = single(table, (2 * rows, table.shape[1]), slot)
    shapes = [
        jax.ShapeDtypeStruct((2 * rows, width), BF),
        jax.ShapeDtypeStruct((2 * rows, w_qkv.shape[1]), BF),
        jax.ShapeDtypeStruct((rows, width), BF),
        jax.ShapeDtypeStruct((rows, width), BF),
        jax.ShapeDtypeStruct((2, HD), F32),
    ]
    kernel = functools.partial(attention_back_kernel, q_here, kv_here)
    return slot_call(kernel, "attention_back", arrays, specs, shapes)


def place_kernel(moves, source_count, out_count, row_ref, column_ref, *refs):
    sources, outs = refs[:source_count], refs[source_count : source_count + out_count]
    refs = refs[source_count + out_count :]
    cast = outs[0].dtype != sources[0].dtype
    staged = refs[source_count:-2] if cast else ()
    loaded, loads, stores = refs[:source_count], refs[-2], refs[-1]
    reads = [
        pltpu.make_async_copy(source, buffer, loads.at[index])
        for index, (source, buffer) in enumerate(zip(sources, loaded))
    ]
    for read in reads:
        read.start()
    writes = []
    arrived = set()
    for index, (source, slot, rows, columns, out) in enumerate(moves):
        height, width = rows.stop - rows.start, columns.stop - columns.start
        row = pl.multiple_of(row_ref[index] * height, height)
        if source not in arrived:
            reads[source].wait()
            arrived.add(source)
        if cast:
            staged[index][...] = loaded[source][slot, rows, columns].astype(outs[out].dtype)
            block = staged[index]
        else:
            block = loaded[source].at[slot, rows, columns]
        if len(outs[out].shape) == 3:
            target = outs[out].at[column_ref[index], pl.ds(row, height), :]
        elif outs[out].shape[1] == width:
            target = outs[out].at[pl.ds(row, height), :]
        else:
            column = pl.multiple_of(column_ref[index] * width, width)
            target = outs[out].at[pl.ds(row, height), pl.ds(column, width)]
        writes.append(pltpu.make_async_copy(block, target, stores.at[index]))
        writes[-1].start()
    for write in writes:
        write.wait()


def place_blocks(sources, moves, row_blocks, column_blocks, shapes, dtype):
    scratch = [pltpu.VMEM(source.shape, source.dtype) for source in sources]
    if dtype != sources[0].dtype:
        scratch += [
            pltpu.VMEM((rows.stop - rows.start, columns.stop - columns.start), dtype)
            for _, _, rows, columns, _ in moves
        ]
    scratch += [pltpu.SemaphoreType.DMA((len(sources),)), pltpu.SemaphoreType.DMA((len(moves),))]
    anywhere = pl.BlockSpec(memory_space=pl.ANY)
    return pl.pallas_call(
        functools.partial(place_kernel, moves, len(sources), len(shapes)),
        in_specs=[pl.BlockSpec(memory_space=pltpu.SMEM)] * 2 + [anywhere] * len(sources),
        out_specs=[anywhere] * len(shapes),
        out_shape=[jax.ShapeDtypeStruct(shape, dtype) for shape in shapes],
        scratch_shapes=scratch,
        compiler_params=pltpu.CompilerParams(vmem_limit_bytes=PLACE_BYTES),
        cost_estimate=LOW_COST,
        name="place_blocks",
    )(row_blocks.astype(jnp.int32), column_blocks.astype(jnp.int32), *sources)


def after(values, *others):
    return lax.optimization_barrier((values, *others))[0]


def move(values, send):
    ranks, copies = lax.axis_size("fsdp"), lax.axis_size("rep")
    pairs = []
    for f in range(ranks):
        for r in range(copies):
            to = send(f, r)
            if to is not None:
                pairs.append((f * copies + r, to[0] * copies + to[1]))
    return lax.ppermute(values, ("fsdp", "rep"), pairs)


def ring(values, step):
    ranks = lax.axis_size("fsdp")
    return move(values, lambda f, r: ((f + 2 * step) % ranks, r))


def swap_core(values):
    return move(values, lambda f, r: (f, r ^ 1))


def swap_x(values):
    return move(values, lambda f, r: (f, r ^ 2))


def swap_twin(values):
    return move(values, lambda f, r: (f ^ 1, r ^ 1))


def place():
    f, r = lax.axis_index("fsdp"), lax.axis_index("rep")
    return f // 2, f % 2, r // 2, r % 2


def pick(values, index, axis=0):
    return lax.dynamic_index_in_dim(values, index, axis, keepdims=False)


def ordered(slots, z):
    depth = len(slots)
    out = jnp.zeros((depth, *slots[0].shape), slots[0].dtype)
    for k, slot in enumerate(slots):
        out = lax.dynamic_update_index_in_dim(out, slot, (z - k) % depth, 0)
    return out


def add(left, right):
    return (left.astype(F32) + right.astype(F32)).astype(BF)


def gather_group(values, name, beside=None):
    slots = []
    for s in range(lax.axis_size("fsdp") // 2):
        with jax.named_scope(f"gather_{name}_{s}"):
            if s > 0:
                values = ring(values if beside is None else beside(s, values), 1)
            slots.append((values, swap_core(values)))
    return slots


def scatter_group(partial, name, beside=None):
    moving = None
    for step, (own, away) in enumerate((*partial[1:], partial[0])):
        with jax.named_scope(f"scatter_{name}_{step}"):
            total = own.astype(F32) + swap_core(away).astype(F32)
            if moving is not None:
                total = total + ring(moving, 1).astype(F32)
            moving = total.astype(BF)
        if beside is not None:
            moving = beside(step, moving)
    return total


def total_sum(values):
    for bit in range(2):
        values = values + move(values, lambda f, r: (f, r ^ (1 << bit)))
    for bit in range((lax.axis_size("fsdp") - 1).bit_length()):
        values = values + move(values, lambda f, r: (f ^ (1 << bit), r))
    return values


class ColumnsIn:
    def __init__(self, parts, rows, name, hold=lambda slots: slots):
        with jax.named_scope(f"{name}_along_z"):
            slots = [ring(part, k) if k else part for k, part in enumerate(parts)]
            self.same = jnp.stack(hold(slots))
        with jax.named_scope(f"{name}_across"):
            self.across_x, self.across_y = swap_x(self.same), swap_twin(self.same)
        self.rows, self.name = rows, name

    def joined(self, split, *others):
        z, y, x, core = place()
        depth, columns = self.same.shape[0], self.same.shape[2]
        middle = depth // 2 if split else depth
        with jax.named_scope(f"{self.name}_across_both"):
            across_x, across_y = after((self.across_x, self.across_y), *others)
            rest = [swap_twin(across_x[:middle])]
            if split:
                rest.append(swap_x(across_y[middle:]))
        sources = [self.same, self.across_x, self.across_y, *rest]
        moves = [
            (source, slot, slice(0, self.rows), slice(0, columns), 0)
            for source, array in enumerate(sources)
            for slot in range(array.shape[0])
        ]
        where_z = (z - jnp.arange(depth)) % depth
        index = lambda yy, xx: (where_z * 2 + yy) * 2 + xx
        places = [index(y, x), index(y, 1 - x), index(1 - y, x), index(1 - y, 1 - x)]
        places = jnp.concatenate(places)
        shape = (4 * depth * self.rows, columns)
        return place_blocks(sources, moves, places, jnp.zeros_like(places), [shape], BF)[0]


def scoped(step):
    def wrap(method):
        def named(self, *others):
            with jax.named_scope(f"{self.name}_{step}"):
                return method(self, *others)

        return named

    return wrap


class ColumnsOut:
    def __init__(self, grad, y_first, name):
        self.name = name
        z, y, x, core = place()
        self.depth = lax.axis_size("fsdp") // 2
        self.y_first = y_first
        columns = grad.shape[1]
        self.blocks = grad.reshape(self.depth, 2, 2, -1, columns)
        axis, index = (1, 1 - y) if y_first else (2, 1 - x)
        self.payload = pick(self.blocks, index, axis)

    @scoped("first")
    def first(self, *others):
        z, y, x, core = place()
        axis, index = (1, y) if self.y_first else (2, x)
        swap = swap_twin if self.y_first else swap_x
        came, own = after(swap(self.payload), *others), pick(self.blocks, index, axis)
        here, there = (x, 1 - x) if self.y_first else (y, 1 - y)
        self.payload = add(pick(own, there, 1), pick(came, there, 1))
        self.kept = (pick(own, here, 1), pick(came, here, 1))

    @scoped("second")
    def second(self, *others):
        z, y, x, core = place()
        swap = swap_x if self.y_first else swap_twin
        came = after(swap(self.payload), *others).astype(F32)
        total = (self.kept[0].astype(F32) + self.kept[1].astype(F32) + came).astype(BF)
        self.payload = [pick(total, (z + k) % self.depth) for k in range(self.depth)]


def along_z(payloads, name):
    with jax.named_scope(f"sum_{name}_along_z"):
        parts = [jnp.concatenate(items, axis=1) for items in zip(*payloads)]
        return [ring(part, k) if k else part for k, part in enumerate(parts)]


def across_x(same, name):
    with jax.named_scope(f"sum_{name}_across"):
        return swap_x(same)


def columns_placed(same, across, widths, name):
    z, y, x, core = place()
    depth, rows, total = same.shape
    with jax.named_scope(f"sum_{name}_core"):
        parts = same, across, swap_core(same), swap_core(across)
    ones = jnp.ones((depth,), jnp.int32)
    row_blocks = jnp.concatenate([x * ones, (1 - x) * ones] * 2)
    where_z = (z - jnp.arange(depth)) % depth
    own, other = 2 * where_z + (y ^ core), 2 * where_z + (1 - (y ^ core))
    column_blocks = jnp.concatenate([own, own, other, other])
    aligned = all(width % 128 == 0 for width in widths)
    spans = []
    for width in widths if aligned else [total]:
        first = spans[-1].stop if spans else 0
        spans.append(slice(first, first + width))
    moves = [
        (source, slot, slice(0, rows), span, out)
        for source in range(4)
        for slot in range(depth)
        for out, span in enumerate(spans)
    ]
    if aligned:
        shapes = [(2 * rows, 2 * depth * width) for width in widths]
    else:
        shapes = [(2 * depth, 2 * rows, total)]
    repeat = lambda blocks: jnp.repeat(blocks, len(spans))
    outs = place_blocks(parts, moves, repeat(row_blocks), repeat(column_blocks), shapes, F32)
    if aligned:
        return outs
    rows_first = outs[0].transpose(1, 0, 2)
    pieces, first = [], 0
    for width in widths:
        pieces.append(rows_first[:, :, first : first + width].reshape(2 * rows, -1))
        first += width
    return pieces


def rows_across_y(weight, name):
    half = weight.shape[0] // 2
    with jax.named_scope(f"{name}_across_y"):
        part = lax.dynamic_slice_in_dim(weight, place()[2] * half, half, axis=0)
        return move(part, lambda f, r: (f ^ 1, r) if r % 2 else None)


def rows_here(weight, part, name):
    z, y, x, core = place()
    half = weight.shape[0] // 2
    with jax.named_scope(f"{name}_across_x"):
        other = move(part, lambda f, r: (f, r ^ 2) if r % 2 else None)
    low = jnp.where(core == 0, weight[:half], jnp.where(x == 0, part, other))
    high = jnp.where(core == 0, weight[half:], jnp.where(x == 0, other, part))
    return jnp.concatenate([low, high], axis=0)


class RowsOut:
    def __init__(self, grad, name):
        self.name = name
        self.grad = self.payload = grad.reshape(2, -1, grad.shape[1])

    @scoped("first")
    def first(self, *others):
        z, y, x, core = place()
        came = after(move(self.payload, lambda f, r: (f ^ 1, r ^ 1) if r % 2 else None), *others)
        self.payload = add(pick(self.grad, 1 - x), pick(came, 1 - x))
        self.kept = (pick(self.grad, x), pick(came, x))

    @scoped("second")
    def second(self, *others):
        came = move(self.payload, lambda f, r: None if r % 2 else (f, r ^ 2))
        came = after(came, *others).astype(F32)
        self.payload = (self.kept[0].astype(F32) + self.kept[1].astype(F32) + came).astype(BF)

    @scoped("third")
    def third(self, *others):
        came = after(move(self.payload, lambda f, r: None if r % 2 else (f, r ^ 2)), *others)
        self.payload = jnp.stack([self.payload, came])

    @scoped("last")
    def last(self):
        z, y, x, core = place()
        came = move(self.payload, lambda f, r: None if r % 2 else (f, r ^ 1))
        parts = jnp.where(core == 0, self.payload, came)
        rows, columns = parts.shape[1:]
        moves = [(0, slot, slice(0, rows), slice(0, columns), 0) for slot in range(2)]
        places = jnp.stack([x, 1 - x])
        return place_blocks([parts], moves, places, jnp.zeros_like(places), [(2 * rows, columns)], F32)[0]


def local(
    tokens_in,
    segment_ids,
    w_query,
    w_key,
    w_value,
    w_out,
    w_gate,
    w_up,
    w_down,
    gain_attn,
    gain_ffn,
    gain_query,
    gain_key,
    d_out,
):
    ranks = lax.axis_size("fsdp")
    rank = lax.axis_index("fsdp")
    depth = ranks // 2
    z, y, x, core = place()
    width = tokens_in.shape[1]
    pack = segment_ids.shape[1]
    heads = w_query.shape[1] // HD
    kv_heads = w_key.shape[1] // HD
    share = max(1, ranks // kv_heads)
    q_here = heads // ranks
    kv_here = max(1, kv_heads // ranks)
    group = q_here // kv_here
    q_cols, kv_cols = q_here * HD, kv_here * HD
    scale = HD ** (-0.5)

    q_gain = gain_query.astype(F32)[None]
    k_gain = gain_key.astype(F32)[None]

    rows_x = w_query.shape[0] // 2
    cut = lambda weight, start, size: lax.dynamic_slice(weight, (x * rows_x, start), (rows_x, size))
    wide = q_cols + 2 * kv_cols
    seg_size = segment_ids.size
    extra = jnp.concatenate([segment_ids.reshape(-1).astype(BF), gain_attn, gain_ffn])
    extra = jnp.pad(extra, (0, 16 * wide - extra.size)).reshape(16, wide)

    def cut_qkv(block):
        kv = block // share * kv_cols
        parts = [cut(w_query, block * q_cols, q_cols), cut(w_key, kv, kv_cols), cut(w_value, kv, kv_cols)]
        return jnp.concatenate([jnp.concatenate(parts, axis=1), extra], axis=0)

    def cutter(weight):
        size = weight.shape[1] // ranks
        return lambda block: cut(weight, block * size, size)

    qkv_parts = [cut_qkv(2 * ((z + k) % depth) + (y ^ core)) for k in range(depth)]
    qkv_in = ColumnsIn(qkv_parts, rows_x, "w_qkv")
    w_qkv = qkv_in.joined(False)
    w_out_here = rows_here(w_out, rows_across_y(w_out, "w_out"), "w_out")
    down_part = rows_across_y(after(w_down, w_qkv), "w_down")
    w_down_here = rows_here(w_down, down_part, "w_down")
    w_gate_late, w_up_late = after((w_gate, w_up), qkv_in.same)
    columns_here = w_gate.shape[1] // ranks

    def cut_glu(block):
        first = block * columns_here
        return jnp.concatenate(
            [cut(w_gate_late, first, columns_here), cut(w_up_late, first, columns_here)], axis=1
        )

    glu_parts = [cut_glu(2 * ((z + k) % depth) + (y ^ core)) for k in range(depth)]
    glu_in = ColumnsIn(glu_parts, rows_x, "w_glu", lambda slots: after((*slots,), w_qkv, w_out_here))
    own_slots, twin_slots = qkv_in.same, qkv_in.across_y
    own_extra = own_slots[:, rows_x:].reshape(depth, -1)
    twin_extra = twin_slots[:, rows_x:].reshape(depth, -1)
    seg_slots = own_extra[:, :seg_size].reshape(depth, 1, -1, pack)
    segments = jnp.concatenate([seg_slots, swap_core(seg_slots)], axis=1).reshape(-1, pack).astype(jnp.int32)
    span = slice(seg_size, seg_size + 2 * gain_attn.size)
    pieces = jnp.stack([own_extra[:, span], twin_extra[:, span]], axis=1)
    pieces = ordered([pieces[k] for k in range(depth)], z).astype(F32)
    pieces = jnp.where(y == 0, pieces, pieces[:, ::-1])
    gains = pieces.reshape(depth, 2, 2, -1).transpose(2, 0, 1, 3).reshape(2, -1)
    attn_gain, ffn_gain = gains[0], gains[1]

    token_ties = {1: (glu_in.same, attn_gain, down_part), 2: (w_down_here,)}
    beside_tokens = lambda s, sent: after(sent, *token_ties.get(s, ()))
    token_slots = gather_group(tokens_in, "tokens", beside_tokens)
    block_rows = tokens_in.shape[0]
    table = token_table(segments, block_rows)
    kept, partial = [None] * depth, [None] * depth
    order = (*range(1, depth), 0)
    for s in order:
        here, other = token_slots[s]
        if s == depth - 1:
            here = after(here, glu_in.across_x, glu_in.across_y)
        *kept[s], own, away = attention(
            s, here, other, table, attn_gain[None], q_gain, k_gain, w_qkv, w_out_here, q_here, kv_here
        )
        partial[s] = (own, away)
    tokens = tokens_in.astype(F32)
    unit_tokens, root_tokens = unit_rows(tokens)

    w_glu = glu_in.joined(True)
    attn_branch = after(scatter_group(partial, "attn_branch"), w_glu)

    middle = tokens + attn_branch
    unit_middle, root_middle = unit_rows(middle)
    ffn_slots = gather_group((unit_middle * ffn_gain).astype(BF), "ffn_in")
    beside_d_out = lambda s, sent: after(sent, ffn_slots[-1][0]) if s == 1 else sent
    grad_slots = gather_group(d_out, "d_out", beside_d_out)
    glu_kept, back_partial, down_partial = [None] * depth, [None] * depth, []
    for s in order:
        ffn_in = jnp.concatenate(ffn_slots[s], axis=0)
        g_ffn = jnp.concatenate(grad_slots[s], axis=0)
        gate_up = matmul(ffn_in, w_glu)
        gate, up = gate_up[:, :columns_here], gate_up[:, columns_here:]
        sig = jax.nn.sigmoid(gate)
        silu = gate * sig
        hidden = (silu * up).astype(BF)
        g_hidden = right_tmul(g_ffn, w_down_here).astype(BF).astype(F32)
        g_gate = (g_hidden * up * sig * (1 + gate * (1 - sig))).astype(BF)
        g_up = (g_hidden * silu).astype(BF)
        part = right_tmul(jnp.concatenate([g_gate, g_up], axis=1), w_glu).astype(BF)
        back_partial[s] = (part[:block_rows], part[block_rows:])
        glu_kept[s] = (ffn_in, g_ffn, hidden, g_gate, g_up)
    ffn_in, g_ffn, hidden, g_gate, g_up = (jnp.concatenate(items, axis=0) for items in zip(*glu_kept))
    sums = {}

    def beside_feed(step, sent):
        if step == depth - 3:
            grad = left_tmul(*after((ffn_in, g_gate), sent)).astype(BF)
            sums["gate"] = ColumnsOut(grad, True, "sum_gate")
            grad = left_tmul(*after((ffn_in, g_up), sums["gate"].payload)).astype(BF)
            sums["up"] = ColumnsOut(grad, False, "sum_up")
        if step == depth - 2:
            sent = after(sent, sums["up"].payload)
        return sent

    g_ffn_in = scatter_group(back_partial, "g_ffn_in", beside_feed)
    gate_sum, up_sum = sums["gate"], sums["up"]
    g_ffn_in = after(g_ffn_in, gate_sum.payload, up_sum.payload)
    ffn_gain_grad = jnp.sum(g_ffn_in * unit_middle, axis=0)
    g_middle = d_out.astype(F32) + unit_back(unit_middle, root_middle, g_ffn_in * ffn_gain)

    attn_slots = gather_group(g_middle.astype(BF), "g_attn")
    back_kept, partial = [None] * depth, [None] * depth
    head_gains = 0.0
    for s in order:
        here, other = attn_slots[s]
        if s == 2:
            gate_sum.first(partial[1][1])
            up_sum.first(partial[1][1])
            here = after(here, gate_sum.payload, up_sum.payload)
        if s == 3:
            gate_sum.second(partial[2][1])
            up_sum.second(partial[2][1])
            grad_down = left_tmul(*after((hidden, g_ffn), up_sum.payload)).astype(BF)
            down_sum = RowsOut(grad_down, "sum_down")
            here = after(here, gate_sum.payload, up_sum.payload, down_sum.payload)
        g_attn, g_qkv, own, away, gain_part = attention_back(
            s, here, other, kept[s][1], table, q_gain, k_gain, w_qkv, w_out_here, q_here, kv_here
        )
        head_gains = head_gains + gain_part
        back_kept[s] = (g_attn, g_qkv)
        partial[s] = (own, away)
    attn_in, _, mixed = (jnp.concatenate(items, axis=0) for items in zip(*kept))
    g_attn, g_qkv = (jnp.concatenate(items, axis=0) for items in zip(*back_kept))
    grad_qkv = left_tmul(attn_in, g_qkv).astype(BF)
    qkv_sum = ColumnsOut(grad_qkv, True, "sum_qkv")
    grad_out = left_tmul(*after((mixed, g_attn), qkv_sum.payload)).astype(BF)
    out_sum = RowsOut(grad_out, "sum_out")
    glu_parts = [jnp.concatenate(pair, axis=1) for pair in zip(gate_sum.payload, up_sum.payload)]
    glu_slots = {0: glu_parts[0]}
    steps = sorted(range(1, depth), key=lambda k: -min(k, depth - k))
    last = None
    for k in steps:
        with jax.named_scope(f"sum_glu_along_z_{k}"):
            part = glu_parts[k] if last is None else after(glu_parts[k], last)
            last = glu_slots[k] = ring(part, k)
        if k == steps[0]:
            last = after(last, qkv_sum.payload, out_sum.payload)
    glu_same = jnp.stack([glu_slots[k] for k in range(depth)])
    glu_across = across_x(glu_same, "glu")

    def beside_back(step, sent):
        if step == 0:
            sent = after(sent, glu_slots[steps[0]])
        if step == 1:
            sent = after(sent, glu_same)
            for item in (down_sum, qkv_sum, out_sum):
                item.first(sent)
        if step == 2:
            sent = after(sent, down_sum.payload, qkv_sum.payload, out_sum.payload)
        return sent

    g_attn_in = scatter_group(partial, "g_attn_in", beside_back)
    attn_gain_grad = jnp.sum(g_attn_in * unit_tokens, axis=0)
    d_tokens = g_middle + unit_back(unit_tokens, root_tokens, g_attn_in * attn_gain)

    for s in range(depth):
        part = matmul(after(glu_kept[s][2], glu_same), w_down_here).astype(BF)
        down_partial.append((part[:block_rows], part[block_rows:]))
    ffn_ties = {0: (glu_across, d_tokens)}
    glu_placed = []

    def beside_branch(step, sent):
        if step == 0:
            glu_placed.extend(columns_placed(glu_same, glu_across, [columns_here, columns_here], "glu"))
        if step == 1:
            qkv_sum.second(sent)
            out_sum.second(sent)
            ffn_ties[1] = (qkv_sum.payload, out_sum.payload)
        if step == 2:
            down_sum.second(sent)
            ffn_ties[2] = (down_sum.payload, *glu_placed)
        return after(sent, *ffn_ties.get(step, ()))

    ffn_branch = scatter_group(down_partial, "ffn_branch", beside_branch)
    block = middle + ffn_branch
    grad_gate, grad_up = glu_placed
    qkv_slots = along_z([qkv_sum.payload], "qkv")
    qkv_same = jnp.stack(qkv_slots)
    qkv_across = across_x(qkv_same, "qkv")
    grad_query, grad_kv = columns_placed(qkv_same, qkv_across, [q_cols, 2 * kv_cols], "qkv")
    down_sum.third(ffn_branch)
    out_sum.third(ffn_branch)
    grad_down, grad_out = down_sum.last(), out_sum.last()
    grad_kv = grad_kv.reshape(grad_kv.shape[0], -1, share, 2 * kv_cols).sum(axis=2)
    grad_key = grad_kv[:, :, :kv_cols].reshape(grad_kv.shape[0], -1)
    grad_value = grad_kv[:, :, kv_cols:].reshape(grad_kv.shape[0], -1)
    squares = jnp.stack(
        [jnp.sum(item * item) for item in (middle, attn_branch, ffn_branch, block, d_tokens)]
    )
    small = jnp.concatenate([attn_gain_grad, ffn_gain_grad, head_gains[0], head_gains[1], squares])
    with jax.named_scope("total_sum"):
        small = total_sum(small)
    gain_rows = gain_attn.shape[0]
    attn_gain_sum = lax.dynamic_slice(small, (rank * gain_rows,), (gain_rows,))
    ffn_gain_sum = lax.dynamic_slice(small, (width + rank * gain_rows,), (gain_rows,))
    entries = tokens_in.shape[0] * ranks * lax.axis_size("rep") * width
    stats = jnp.sqrt(small[2 * width + 2 * HD :] / entries)
    return (
        block.astype(BF),
        d_tokens.astype(BF),
        grad_query,
        grad_key,
        grad_value,
        grad_out,
        grad_gate,
        grad_up,
        grad_down,
        attn_gain_sum,
        ffn_gain_sum,
        small[2 * width : 2 * width + HD],
        small[2 * width + HD : 2 * width + 2 * HD],
        stats,
    )


def solution(mesh):
    rows = P(("fsdp", "rep"), None)
    weight = P("fsdp", None)
    return jax.shard_map(
        local,
        mesh=mesh,
        in_specs=(rows, rows, *[weight] * 7, P("fsdp"), P("fsdp"), P(), P(), rows),
        out_specs=(rows, rows, *[weight] * 7, P("fsdp"), P("fsdp"), P(), P(), P()),
        check_vma=False,
    )
```

```python
import functools
import math

import jax
import jax.numpy as jnp
from jax import lax
from jax.experimental import pallas as pl
from jax.experimental.pallas import tpu as pltpu
from jax.sharding import PartitionSpec as P

HD = 64
EPS = 1e-05
THETA = 1000000.0
NEG = -1e30
BF = jnp.bfloat16
F32 = jnp.float32
ATTENTION_BYTES = 24 * 1024 * 1024
PLACE_BYTES = 44 * 1024 * 1024
LOW_COST = pl.CostEstimate(flops=1, bytes_accessed=1, transcendentals=0)


def matmul(left, right):
    return jnp.dot(left, right, preferred_element_type=F32)


def left_tmul(left, right):
    return lax.dot_general(left, right, (((0,), (0,)), ((), ())), preferred_element_type=F32)


def right_tmul(left, right):
    return lax.dot_general(left, right, (((1,), (1,)), ((), ())), preferred_element_type=F32)


def unit_rows(values):
    root = lax.rsqrt(jnp.mean(values * values, axis=-1, keepdims=True) + EPS)
    return values * root, root


def unit_back(unit, root, grad):
    return root * (grad - unit * jnp.mean(grad * unit, axis=-1, keepdims=True))


def turn(values, cosine, sine):
    half = values.shape[-1] // 2
    swapped = jnp.concatenate([values[:, half:], values[:, :half]], axis=1)
    return values * cosine + swapped * sine


def token_table(segments, width):
    index = jnp.arange(segments.shape[1])
    same = segments[:, :, None] == segments[:, None, :]
    position = jnp.sum((same & (index[None, :] < index[:, None])).astype(jnp.int32), axis=2)
    frequency = jnp.exp(jnp.arange(HD // 2).astype(F32) * (-2.0 * math.log(THETA) / HD))
    phase = position.astype(F32).reshape(-1, 1) * frequency
    cosine, sine = jnp.cos(phase), jnp.sin(phase)
    packs = jnp.arange(segments.shape[0], dtype=jnp.int32) % (width // segments.shape[1])
    marks = (segments + 4 * packs[:, None]).astype(F32).reshape(-1, 1)
    marks = jnp.broadcast_to(marks, (marks.shape[0], width))
    return jnp.concatenate([cosine, cosine, -sine, sine, marks], axis=1)


def head(values, index):
    return values[:, index * HD : (index + 1) * HD]


def allowed_block(marks):
    later = lax.broadcasted_iota(jnp.int32, marks.shape, 1)
    return (marks == marks.T) & (later <= lax.broadcasted_iota(jnp.int32, marks.shape, 0))


def probabilities(query, key, allowed):
    scores = right_tmul(query, key) * HD ** (-0.5)
    exponent = jnp.where(allowed, jnp.exp(scores), 0.0)
    return exponent * (1.0 / jnp.sum(exponent, axis=-1, keepdims=True))


def attention_kernel(q_here, kv_here, *refs):
    here_ref, other_ref, table_ref, gain_ref, q_gain_ref, k_gain_ref, w_qkv_ref, w_out_ref = refs[:8]
    attn_in_ref, qkv_ref, mixed_ref, own_ref, away_ref = refs[8:]
    group = q_here // kv_here
    rows = here_ref.shape[0]
    gain = gain_ref[...]
    for index, tokens_ref in enumerate((here_ref, other_ref)):
        unit, _ = unit_rows(tokens_ref[...].astype(F32))
        attn_in_ref[index * rows : (index + 1) * rows, :] = (unit * gain).astype(BF)
    qkv = matmul(attn_in_ref[...], w_qkv_ref[...])
    qkv_ref[...] = qkv
    blocks = [slice(index * rows, (index + 1) * rows) for index in range(2)]
    allowed = [allowed_block(table_ref[part, 2 * HD :]) for part in blocks]
    cosine, sine = table_ref[:, :HD], table_ref[:, HD : 2 * HD]
    for kv in range(kv_here):
        key = turn(unit_rows(head(qkv, q_here + kv))[0] * k_gain_ref[...], cosine, sine).astype(BF)
        value = head(qkv, q_here + kv_here + kv).astype(BF)
        for h in range(kv * group, (kv + 1) * group):
            query = turn(unit_rows(head(qkv, h))[0] * q_gain_ref[...], cosine, sine).astype(BF)
            for index, part in enumerate(blocks):
                probs = probabilities(query[part], key[part], allowed[index])
                mixed_ref[part, h * HD : (h + 1) * HD] = matmul(probs.astype(BF), value[part]).astype(BF)
    mixed = mixed_ref[...]
    own_ref[...] = matmul(mixed[:rows], w_out_ref[...]).astype(BF)
    away_ref[...] = matmul(mixed[rows:], w_out_ref[...]).astype(BF)


def attention_back_kernel(q_here, kv_here, *refs):
    here_ref, other_ref, qkv_ref, table_ref, q_gain_ref, k_gain_ref, w_qkv_ref, w_out_ref = refs[:8]
    g_attn_ref, g_qkv_ref, own_ref, away_ref, gains_ref = refs[8:]
    group = q_here // kv_here
    rows = here_ref.shape[0]
    g_attn_ref[:rows, :] = here_ref[...]
    g_attn_ref[rows:, :] = other_ref[...]
    g_mixed = right_tmul(g_attn_ref[...], w_out_ref[...]).astype(BF)
    qkv = qkv_ref[...]
    blocks = [slice(index * rows, (index + 1) * rows) for index in range(2)]
    allowed = [allowed_block(table_ref[part, 2 * HD :]) for part in blocks]
    cosine, sine = table_ref[:, :HD], table_ref[:, HD : 2 * HD]
    q_gain, k_gain = q_gain_ref[...], k_gain_ref[...]
    scale = HD ** (-0.5)
    q_sum = jnp.zeros((1, HD), F32)
    k_sum = jnp.zeros((1, HD), F32)
    pieces = {}
    for kv in range(kv_here):
        k_unit, k_root = unit_rows(head(qkv, q_here + kv))
        key = turn(k_unit * k_gain, cosine, sine).astype(BF)
        value = head(qkv, q_here + kv_here + kv).astype(BF)
        g_k, g_v = [0.0, 0.0], [0.0, 0.0]
        for h in range(kv * group, (kv + 1) * group):
            q_unit, q_root = unit_rows(head(qkv, h))
            query = turn(q_unit * q_gain, cosine, sine).astype(BF)
            g_head = head(g_mixed, h)
            g_query = []
            for index, part in enumerate(blocks):
                probs = probabilities(query[part], key[part], allowed[index])
                g_probs = right_tmul(g_head[part], value[part])
                g_v[index] = g_v[index] + left_tmul(probs.astype(BF), g_head[part])
                g_scores = probs * (g_probs - jnp.sum(probs * g_probs, axis=-1, keepdims=True))
                g_scores = g_scores.astype(BF)
                g_k[index] = g_k[index] + left_tmul(g_scores, query[part])
                g_query.append(matmul(g_scores, key[part]))
            back = turn(jnp.concatenate(g_query, axis=0) * scale, cosine, -sine)
            q_sum = q_sum + jnp.sum(back * q_unit, axis=0, keepdims=True)
            pieces[h] = unit_back(q_unit, q_root, back * q_gain).astype(BF)
        back = turn(jnp.concatenate(g_k, axis=0) * scale, cosine, -sine)
        k_sum = k_sum + jnp.sum(back * k_unit, axis=0, keepdims=True)
        pieces[q_here + kv] = unit_back(k_unit, k_root, back * k_gain).astype(BF)
        pieces[q_here + kv_here + kv] = jnp.concatenate(g_v, axis=0).astype(BF)
    g_qkv = jnp.concatenate([pieces[index] for index in range(q_here + 2 * kv_here)], axis=1)
    g_qkv_ref[...] = g_qkv
    own_ref[...] = right_tmul(g_qkv[:rows], w_qkv_ref[...]).astype(BF)
    away_ref[...] = right_tmul(g_qkv[rows:], w_qkv_ref[...]).astype(BF)
    gains_ref[...] = jnp.concatenate([q_sum, k_sum], axis=0)


def single(array, block=None, index=0):
    block = array.shape if block is None else block
    return pl.BlockSpec(block, lambda step: (index,) + (0,) * (len(block) - 1))


def slot_call(kernel, name, arrays, specs, shapes):
    return pl.pallas_call(
        kernel,
        grid=(1,),
        in_specs=specs,
        out_specs=[single(shape) for shape in shapes],
        out_shape=shapes,
        compiler_params=pltpu.CompilerParams(vmem_limit_bytes=ATTENTION_BYTES),
        cost_estimate=LOW_COST,
        name=name,
    )(*arrays)


def attention(slot, here, other, table, gain, q_gain, k_gain, w_qkv, w_out, q_here, kv_here):
    rows, width = here.shape
    arrays = (here, other, table, gain, q_gain, k_gain, w_qkv, w_out)
    specs = [single(array) for array in arrays]
    specs[2] = single(table, (2 * rows, table.shape[1]), slot)
    shapes = [
        jax.ShapeDtypeStruct((2 * rows, width), BF),
        jax.ShapeDtypeStruct((2 * rows, w_qkv.shape[1]), F32),
        jax.ShapeDtypeStruct((2 * rows, q_here * HD), BF),
        jax.ShapeDtypeStruct((rows, width), BF),
        jax.ShapeDtypeStruct((rows, width), BF),
    ]
    kernel = functools.partial(attention_kernel, q_here, kv_here)
    return slot_call(kernel, "attention", arrays, specs, shapes)


def attention_back(slot, here, other, qkv, table, q_gain, k_gain, w_qkv, w_out, q_here, kv_here):
    rows, width = here.shape
    arrays = (here, other, qkv, table, q_gain, k_gain, w_qkv, w_out)
    specs = [single(array) for array in arrays]
    specs[3] = single(table, (2 * rows, table.shape[1]), slot)
    shapes = [
        jax.ShapeDtypeStruct((2 * rows, width), BF),
        jax.ShapeDtypeStruct((2 * rows, w_qkv.shape[1]), BF),
        jax.ShapeDtypeStruct((rows, width), BF),
        jax.ShapeDtypeStruct((rows, width), BF),
        jax.ShapeDtypeStruct((2, HD), F32),
    ]
    kernel = functools.partial(attention_back_kernel, q_here, kv_here)
    return slot_call(kernel, "attention_back", arrays, specs, shapes)


def place_kernel(moves, source_count, out_count, row_ref, column_ref, *refs):
    sources, outs = refs[:source_count], refs[source_count : source_count + out_count]
    refs = refs[source_count + out_count :]
    cast = outs[0].dtype != sources[0].dtype
    staged = refs[source_count:-2] if cast else ()
    loaded, loads, stores = refs[:source_count], refs[-2], refs[-1]
    reads = [
        pltpu.make_async_copy(source, buffer, loads.at[index])
        for index, (source, buffer) in enumerate(zip(sources, loaded))
    ]
    for read in reads:
        read.start()
    writes = []
    arrived = set()
    for index, (source, slot, rows, columns, out) in enumerate(moves):
        height, width = rows.stop - rows.start, columns.stop - columns.start
        row = pl.multiple_of(row_ref[index] * height, height)
        if source not in arrived:
            reads[source].wait()
            arrived.add(source)
        if cast:
            staged[index][...] = loaded[source][slot, rows, columns].astype(outs[out].dtype)
            block = staged[index]
        else:
            block = loaded[source].at[slot, rows, columns]
        if len(outs[out].shape) == 3:
            target = outs[out].at[column_ref[index], pl.ds(row, height), :]
        elif outs[out].shape[1] == width:
            target = outs[out].at[pl.ds(row, height), :]
        else:
            column = pl.multiple_of(column_ref[index] * width, width)
            target = outs[out].at[pl.ds(row, height), pl.ds(column, width)]
        writes.append(pltpu.make_async_copy(block, target, stores.at[index]))
        writes[-1].start()
    for write in writes:
        write.wait()


def place_blocks(sources, moves, row_blocks, column_blocks, shapes, dtype):
    scratch = [pltpu.VMEM(source.shape, source.dtype) for source in sources]
    if dtype != sources[0].dtype:
        scratch += [
            pltpu.VMEM((rows.stop - rows.start, columns.stop - columns.start), dtype)
            for _, _, rows, columns, _ in moves
        ]
    scratch += [pltpu.SemaphoreType.DMA((len(sources),)), pltpu.SemaphoreType.DMA((len(moves),))]
    anywhere = pl.BlockSpec(memory_space=pl.ANY)
    return pl.pallas_call(
        functools.partial(place_kernel, moves, len(sources), len(shapes)),
        in_specs=[pl.BlockSpec(memory_space=pltpu.SMEM)] * 2 + [anywhere] * len(sources),
        out_specs=[anywhere] * len(shapes),
        out_shape=[jax.ShapeDtypeStruct(shape, dtype) for shape in shapes],
        scratch_shapes=scratch,
        compiler_params=pltpu.CompilerParams(vmem_limit_bytes=PLACE_BYTES),
        cost_estimate=LOW_COST,
        name="place_blocks",
    )(row_blocks.astype(jnp.int32), column_blocks.astype(jnp.int32), *sources)


def after(values, *others):
    return lax.optimization_barrier((values, *others))[0]


def move(values, send):
    ranks, copies = lax.axis_size("fsdp"), lax.axis_size("rep")
    pairs = []
    for f in range(ranks):
        for r in range(copies):
            to = send(f, r)
            if to is not None:
                pairs.append((f * copies + r, to[0] * copies + to[1]))
    return lax.ppermute(values, ("fsdp", "rep"), pairs)


def ring(values, step):
    ranks = lax.axis_size("fsdp")
    return move(values, lambda f, r: ((f + 2 * step) % ranks, r))


def swap_core(values):
    return move(values, lambda f, r: (f, r ^ 1))


def swap_x(values):
    return move(values, lambda f, r: (f, r ^ 2))


def swap_twin(values):
    return move(values, lambda f, r: (f ^ 1, r ^ 1))


def place():
    f, r = lax.axis_index("fsdp"), lax.axis_index("rep")
    return f // 2, f % 2, r // 2, r % 2


def pick(values, index, axis=0):
    return lax.dynamic_index_in_dim(values, index, axis, keepdims=False)


def ordered(slots, z):
    depth = len(slots)
    out = jnp.zeros((depth, *slots[0].shape), slots[0].dtype)
    for k, slot in enumerate(slots):
        out = lax.dynamic_update_index_in_dim(out, slot, (z - k) % depth, 0)
    return out


def add(left, right):
    return (left.astype(F32) + right.astype(F32)).astype(BF)


def gather_group(values, name, beside=None):
    slots = []
    for s in range(lax.axis_size("fsdp") // 2):
        with jax.named_scope(f"gather_{name}_{s}"):
            if s > 0:
                values = ring(values if beside is None else beside(s, values), 1)
            slots.append((values, swap_core(values)))
    return slots


def scatter_group(partial, name, beside=None):
    moving = None
    for step, (own, away) in enumerate((*partial[1:], partial[0])):
        with jax.named_scope(f"scatter_{name}_{step}"):
            total = own.astype(F32) + swap_core(away).astype(F32)
            if moving is not None:
                total = total + ring(moving, 1).astype(F32)
            moving = total.astype(BF)
        if beside is not None:
            moving = beside(step, moving)
    return total


def total_sum(values):
    for bit in range(2):
        values = values + move(values, lambda f, r: (f, r ^ (1 << bit)))
    for bit in range((lax.axis_size("fsdp") - 1).bit_length()):
        values = values + move(values, lambda f, r: (f ^ (1 << bit), r))
    return values


class ColumnsIn:
    def __init__(self, parts, rows, name, hold=lambda slots: slots):
        with jax.named_scope(f"{name}_along_z"):
            slots = [ring(part, k) if k else part for k, part in enumerate(parts)]
            self.same = jnp.stack(hold(slots))
        with jax.named_scope(f"{name}_across"):
            self.across_x, self.across_y = swap_x(self.same), swap_twin(self.same)
        self.rows, self.name = rows, name

    def joined(self, split, *others):
        z, y, x, core = place()
        depth, columns = self.same.shape[0], self.same.shape[2]
        middle = depth // 2 if split else depth
        with jax.named_scope(f"{self.name}_across_both"):
            across_x, across_y = after((self.across_x, self.across_y), *others)
            rest = [swap_twin(across_x[:middle])]
            if split:
                rest.append(swap_x(across_y[middle:]))
        sources = [self.same, self.across_x, self.across_y, *rest]
        moves = [
            (source, slot, slice(0, self.rows), slice(0, columns), 0)
            for source, array in enumerate(sources)
            for slot in range(array.shape[0])
        ]
        where_z = (z - jnp.arange(depth)) % depth
        index = lambda yy, xx: (where_z * 2 + yy) * 2 + xx
        places = [index(y, x), index(y, 1 - x), index(1 - y, x), index(1 - y, 1 - x)]
        places = jnp.concatenate(places)
        shape = (4 * depth * self.rows, columns)
        return place_blocks(sources, moves, places, jnp.zeros_like(places), [shape], BF)[0]


def scoped(step):
    def wrap(method):
        def named(self, *others):
            with jax.named_scope(f"{self.name}_{step}"):
                return method(self, *others)

        return named

    return wrap


class ColumnsOut:
    def __init__(self, grad, y_first, name):
        self.name = name
        z, y, x, core = place()
        self.depth = lax.axis_size("fsdp") // 2
        self.y_first = y_first
        columns = grad.shape[1]
        self.blocks = grad.reshape(self.depth, 2, 2, -1, columns)
        axis, index = (1, 1 - y) if y_first else (2, 1 - x)
        self.payload = pick(self.blocks, index, axis)

    @scoped("first")
    def first(self, *others):
        z, y, x, core = place()
        axis, index = (1, y) if self.y_first else (2, x)
        swap = swap_twin if self.y_first else swap_x
        came, own = after(swap(self.payload), *others), pick(self.blocks, index, axis)
        here, there = (x, 1 - x) if self.y_first else (y, 1 - y)
        self.payload = add(pick(own, there, 1), pick(came, there, 1))
        self.kept = (pick(own, here, 1), pick(came, here, 1))

    @scoped("second")
    def second(self, *others):
        z, y, x, core = place()
        swap = swap_x if self.y_first else swap_twin
        came = after(swap(self.payload), *others).astype(F32)
        total = (self.kept[0].astype(F32) + self.kept[1].astype(F32) + came).astype(BF)
        self.payload = [pick(total, (z + k) % self.depth) for k in range(self.depth)]


def along_z(payloads, name):
    with jax.named_scope(f"sum_{name}_along_z"):
        parts = [jnp.concatenate(items, axis=1) for items in zip(*payloads)]
        return [ring(part, k) if k else part for k, part in enumerate(parts)]


def across_x(same, name):
    with jax.named_scope(f"sum_{name}_across"):
        return swap_x(same)


def columns_placed(same, across, widths, name):
    z, y, x, core = place()
    depth, rows, total = same.shape
    with jax.named_scope(f"sum_{name}_core"):
        parts = same, across, swap_core(same), swap_core(across)
    ones = jnp.ones((depth,), jnp.int32)
    row_blocks = jnp.concatenate([x * ones, (1 - x) * ones] * 2)
    where_z = (z - jnp.arange(depth)) % depth
    own, other = 2 * where_z + (y ^ core), 2 * where_z + (1 - (y ^ core))
    column_blocks = jnp.concatenate([own, own, other, other])
    aligned = all(width % 128 == 0 for width in widths)
    spans = []
    for width in widths if aligned else [total]:
        first = spans[-1].stop if spans else 0
        spans.append(slice(first, first + width))
    moves = [
        (source, slot, slice(0, rows), span, out)
        for source in range(4)
        for slot in range(depth)
        for out, span in enumerate(spans)
    ]
    if aligned:
        shapes = [(2 * rows, 2 * depth * width) for width in widths]
    else:
        shapes = [(2 * depth, 2 * rows, total)]
    repeat = lambda blocks: jnp.repeat(blocks, len(spans))
    outs = place_blocks(parts, moves, repeat(row_blocks), repeat(column_blocks), shapes, F32)
    if aligned:
        return outs
    rows_first = outs[0].transpose(1, 0, 2)
    pieces, first = [], 0
    for width in widths:
        pieces.append(rows_first[:, :, first : first + width].reshape(2 * rows, -1))
        first += width
    return pieces


def rows_across_y(weight, name):
    half = weight.shape[0] // 2
    with jax.named_scope(f"{name}_across_y"):
        part = lax.dynamic_slice_in_dim(weight, place()[2] * half, half, axis=0)
        return move(part, lambda f, r: (f ^ 1, r) if r % 2 else None)


def rows_here(weight, part, name):
    z, y, x, core = place()
    half = weight.shape[0] // 2
    with jax.named_scope(f"{name}_across_x"):
        other = move(part, lambda f, r: (f, r ^ 2) if r % 2 else None)
    low = jnp.where(core == 0, weight[:half], jnp.where(x == 0, part, other))
    high = jnp.where(core == 0, weight[half:], jnp.where(x == 0, other, part))
    return jnp.concatenate([low, high], axis=0)


class RowsOut:
    def __init__(self, grad, name):
        self.name = name
        self.grad = self.payload = grad.reshape(2, -1, grad.shape[1])

    @scoped("first")
    def first(self, *others):
        z, y, x, core = place()
        came = after(move(self.payload, lambda f, r: (f ^ 1, r ^ 1) if r % 2 else None), *others)
        self.payload = add(pick(self.grad, 1 - x), pick(came, 1 - x))
        self.kept = (pick(self.grad, x), pick(came, x))

    @scoped("second")
    def second(self, *others):
        came = move(self.payload, lambda f, r: None if r % 2 else (f, r ^ 2))
        came = after(came, *others).astype(F32)
        self.payload = (self.kept[0].astype(F32) + self.kept[1].astype(F32) + came).astype(BF)

    @scoped("third")
    def third(self, *others):
        came = after(move(self.payload, lambda f, r: None if r % 2 else (f, r ^ 2)), *others)
        self.payload = jnp.stack([self.payload, came])

    @scoped("last")
    def last(self):
        z, y, x, core = place()
        came = move(self.payload, lambda f, r: None if r % 2 else (f, r ^ 1))
        parts = jnp.where(core == 0, self.payload, came)
        rows, columns = parts.shape[1:]
        moves = [(0, slot, slice(0, rows), slice(0, columns), 0) for slot in range(2)]
        places = jnp.stack([x, 1 - x])
        return place_blocks([parts], moves, places, jnp.zeros_like(places), [(2 * rows, columns)], F32)[0]


def local(
    tokens_in,
    segment_ids,
    w_query,
    w_key,
    w_value,
    w_out,
    w_gate,
    w_up,
    w_down,
    gain_attn,
    gain_ffn,
    gain_query,
    gain_key,
    d_out,
):
    ranks = lax.axis_size("fsdp")
    rank = lax.axis_index("fsdp")
    depth = ranks // 2
    z, y, x, core = place()
    width = tokens_in.shape[1]
    pack = segment_ids.shape[1]
    heads = w_query.shape[1] // HD
    kv_heads = w_key.shape[1] // HD
    share = max(1, ranks // kv_heads)
    q_here = heads // ranks
    kv_here = max(1, kv_heads // ranks)
    group = q_here // kv_here
    q_cols, kv_cols = q_here * HD, kv_here * HD
    scale = HD ** (-0.5)

    q_gain = gain_query.astype(F32)[None]
    k_gain = gain_key.astype(F32)[None]

    rows_x = w_query.shape[0] // 2
    cut = lambda weight, start, size: lax.dynamic_slice(weight, (x * rows_x, start), (rows_x, size))
    wide = q_cols + 2 * kv_cols
    seg_size = segment_ids.size
    extra = jnp.concatenate([segment_ids.reshape(-1).astype(BF), gain_attn, gain_ffn])
    extra = jnp.pad(extra, (0, 16 * wide - extra.size)).reshape(16, wide)

    def cut_qkv(block):
        kv = block // share * kv_cols
        parts = [cut(w_query, block * q_cols, q_cols), cut(w_key, kv, kv_cols), cut(w_value, kv, kv_cols)]
        return jnp.concatenate([jnp.concatenate(parts, axis=1), extra], axis=0)

    def cutter(weight):
        size = weight.shape[1] // ranks
        return lambda block: cut(weight, block * size, size)

    qkv_parts = [cut_qkv(2 * ((z + k) % depth) + (y ^ core)) for k in range(depth)]
    qkv_in = ColumnsIn(qkv_parts, rows_x, "w_qkv")
    w_qkv = qkv_in.joined(False)
    w_out_here = rows_here(w_out, rows_across_y(w_out, "w_out"), "w_out")
    down_part = rows_across_y(after(w_down, w_qkv), "w_down")
    w_down_here = rows_here(w_down, down_part, "w_down")
    w_gate_late, w_up_late = after((w_gate, w_up), qkv_in.same)
    columns_here = w_gate.shape[1] // ranks

    def cut_glu(block):
        first = block * columns_here
        return jnp.concatenate(
            [cut(w_gate_late, first, columns_here), cut(w_up_late, first, columns_here)], axis=1
        )

    glu_parts = [cut_glu(2 * ((z + k) % depth) + (y ^ core)) for k in range(depth)]
    glu_in = ColumnsIn(glu_parts, rows_x, "w_glu", lambda slots: after((*slots,), w_qkv, w_out_here))
    own_slots, twin_slots = qkv_in.same, qkv_in.across_y
    own_extra = own_slots[:, rows_x:].reshape(depth, -1)
    twin_extra = twin_slots[:, rows_x:].reshape(depth, -1)
    seg_slots = own_extra[:, :seg_size].reshape(depth, 1, -1, pack)
    segments = jnp.concatenate([seg_slots, swap_core(seg_slots)], axis=1).reshape(-1, pack).astype(jnp.int32)
    span = slice(seg_size, seg_size + 2 * gain_attn.size)
    pieces = jnp.stack([own_extra[:, span], twin_extra[:, span]], axis=1)
    pieces = ordered([pieces[k] for k in range(depth)], z).astype(F32)
    pieces = jnp.where(y == 0, pieces, pieces[:, ::-1])
    gains = pieces.reshape(depth, 2, 2, -1).transpose(2, 0, 1, 3).reshape(2, -1)
    attn_gain, ffn_gain = gains[0], gains[1]

    token_ties = {1: (glu_in.same, attn_gain, down_part), 2: (w_down_here,)}
    beside_tokens = lambda s, sent: after(sent, *token_ties.get(s, ()))
    token_slots = gather_group(tokens_in, "tokens", beside_tokens)
    block_rows = tokens_in.shape[0]
    table = token_table(segments, block_rows)
    kept, partial = [None] * depth, [None] * depth
    order = (*range(1, depth), 0)
    for s in order:
        here, other = token_slots[s]
        if s == depth - 1:
            here = after(here, glu_in.across_x, glu_in.across_y)
        *kept[s], own, away = attention(
            s, here, other, table, attn_gain[None], q_gain, k_gain, w_qkv, w_out_here, q_here, kv_here
        )
        partial[s] = (own, away)
    tokens = tokens_in.astype(F32)
    unit_tokens, root_tokens = unit_rows(tokens)

    w_glu = glu_in.joined(True)
    attn_branch = after(scatter_group(partial, "attn_branch"), w_glu)

    middle = tokens + attn_branch
    unit_middle, root_middle = unit_rows(middle)
    ffn_slots = gather_group((unit_middle * ffn_gain).astype(BF), "ffn_in")
    beside_d_out = lambda s, sent: after(sent, ffn_slots[-1][0]) if s == 1 else sent
    grad_slots = gather_group(d_out, "d_out", beside_d_out)
    glu_kept, back_partial, down_partial = [None] * depth, [None] * depth, []
    for s in order:
        ffn_in = jnp.concatenate(ffn_slots[s], axis=0)
        g_ffn = jnp.concatenate(grad_slots[s], axis=0)
        gate_up = matmul(ffn_in, w_glu)
        gate, up = gate_up[:, :columns_here], gate_up[:, columns_here:]
        sig = jax.nn.sigmoid(gate)
        silu = gate * sig
        hidden = (silu * up).astype(BF)
        g_hidden = right_tmul(g_ffn, w_down_here).astype(BF).astype(F32)
        g_gate = (g_hidden * up * sig * (1 + gate * (1 - sig))).astype(BF)
        g_up = (g_hidden * silu).astype(BF)
        part = right_tmul(jnp.concatenate([g_gate, g_up], axis=1), w_glu).astype(BF)
        back_partial[s] = (part[:block_rows], part[block_rows:])
        glu_kept[s] = (ffn_in, g_ffn, hidden, g_gate, g_up)
    ffn_in, g_ffn, hidden, g_gate, g_up = (jnp.concatenate(items, axis=0) for items in zip(*glu_kept))
    sums = {}

    def beside_feed(step, sent):
        if step == depth - 3:
            grad = left_tmul(*after((ffn_in, g_gate), sent)).astype(BF)
            sums["gate"] = ColumnsOut(grad, True, "sum_gate")
            grad = left_tmul(*after((ffn_in, g_up), sums["gate"].payload)).astype(BF)
            sums["up"] = ColumnsOut(grad, False, "sum_up")
        if step == depth - 2:
            sent = after(sent, sums["up"].payload)
        return sent

    g_ffn_in = scatter_group(back_partial, "g_ffn_in", beside_feed)
    gate_sum, up_sum = sums["gate"], sums["up"]
    g_ffn_in = after(g_ffn_in, gate_sum.payload, up_sum.payload)
    ffn_gain_grad = jnp.sum(g_ffn_in * unit_middle, axis=0)
    g_middle = d_out.astype(F32) + unit_back(unit_middle, root_middle, g_ffn_in * ffn_gain)

    attn_slots = gather_group(g_middle.astype(BF), "g_attn")
    back_kept, partial = [None] * depth, [None] * depth
    head_gains = 0.0
    for s in order:
        here, other = attn_slots[s]
        if s == 2:
            gate_sum.first(partial[1][1])
            up_sum.first(partial[1][1])
            here = after(here, gate_sum.payload, up_sum.payload)
        if s == 3:
            gate_sum.second(partial[2][1])
            up_sum.second(partial[2][1])
            grad_down = left_tmul(*after((hidden, g_ffn), up_sum.payload)).astype(BF)
            down_sum = RowsOut(grad_down, "sum_down")
            here = after(here, gate_sum.payload, up_sum.payload, down_sum.payload)
        g_attn, g_qkv, own, away, gain_part = attention_back(
            s, here, other, kept[s][1], table, q_gain, k_gain, w_qkv, w_out_here, q_here, kv_here
        )
        head_gains = head_gains + gain_part
        back_kept[s] = (g_attn, g_qkv)
        partial[s] = (own, away)
    attn_in, _, mixed = (jnp.concatenate(items, axis=0) for items in zip(*kept))
    g_attn, g_qkv = (jnp.concatenate(items, axis=0) for items in zip(*back_kept))
    grad_qkv = left_tmul(attn_in, g_qkv).astype(BF)
    qkv_sum = ColumnsOut(grad_qkv, True, "sum_qkv")
    grad_out = left_tmul(*after((mixed, g_attn), qkv_sum.payload)).astype(BF)
    out_sum = RowsOut(grad_out, "sum_out")
    glu_parts = [jnp.concatenate(pair, axis=1) for pair in zip(gate_sum.payload, up_sum.payload)]
    glu_slots = {0: glu_parts[0]}
    steps = sorted(range(1, depth), key=lambda k: -min(k, depth - k))
    last = None
    for k in steps:
        with jax.named_scope(f"sum_glu_along_z_{k}"):
            part = glu_parts[k] if last is None else after(glu_parts[k], last)
            last = glu_slots[k] = ring(part, k)
        if k == steps[0]:
            last = after(last, qkv_sum.payload, out_sum.payload)
    glu_same = jnp.stack([glu_slots[k] for k in range(depth)])
    glu_across = across_x(glu_same, "glu")

    def beside_back(step, sent):
        if step == 0:
            sent = after(sent, glu_slots[steps[0]])
        if step == 1:
            sent = after(sent, glu_same)
            for item in (down_sum, qkv_sum, out_sum):
                item.first(sent)
        if step == 2:
            sent = after(sent, down_sum.payload, qkv_sum.payload, out_sum.payload, glu_across)
        return sent

    g_attn_in = scatter_group(partial, "g_attn_in", beside_back)
    attn_gain_grad = jnp.sum(g_attn_in * unit_tokens, axis=0)
    d_tokens = g_middle + unit_back(unit_tokens, root_tokens, g_attn_in * attn_gain)

    for s in range(depth):
        part = matmul(after(glu_kept[s][2], glu_same), w_down_here).astype(BF)
        down_partial.append((part[:block_rows], part[block_rows:]))
    glu_placed = columns_placed(glu_same, glu_across, [columns_here, columns_here], "glu")

    arrived = []

    def beside_branch(step, sent):
        arrived.append(sent)
        if step == 0:
            return after(sent, d_tokens)
        if step == 1:
            down_sum.second(d_tokens)
            return after(sent, down_sum.payload)
        if step == 2:
            qkv_sum.second(arrived[1])
            out_sum.second(arrived[1])
            return after(sent, qkv_sum.payload, out_sum.payload)
        return sent

    ffn_branch = scatter_group(down_partial, "ffn_branch", beside_branch)
    block = middle + after(ffn_branch, *glu_placed)
    grad_gate, grad_up = glu_placed
    qkv_slots = along_z([qkv_sum.payload], "qkv")
    qkv_same = jnp.stack(after((*qkv_slots,), arrived[2]))
    qkv_across = across_x(qkv_same, "qkv")
    grad_query, grad_kv = columns_placed(qkv_same, qkv_across, [q_cols, 2 * kv_cols], "qkv")
    down_sum.third()
    out_sum.third()
    grad_down, grad_out = down_sum.last(), out_sum.last()
    grad_kv = grad_kv.reshape(grad_kv.shape[0], -1, share, 2 * kv_cols).sum(axis=2)
    grad_key = grad_kv[:, :, :kv_cols].reshape(grad_kv.shape[0], -1)
    grad_value = grad_kv[:, :, kv_cols:].reshape(grad_kv.shape[0], -1)
    squares = jnp.stack(
        [jnp.sum(item * item) for item in (middle, attn_branch, ffn_branch, block, d_tokens)]
    )
    small = jnp.concatenate([attn_gain_grad, ffn_gain_grad, head_gains[0], head_gains[1], squares])
    with jax.named_scope("total_sum"):
        small = total_sum(small)
    gain_rows = gain_attn.shape[0]
    attn_gain_sum = lax.dynamic_slice(small, (rank * gain_rows,), (gain_rows,))
    ffn_gain_sum = lax.dynamic_slice(small, (width + rank * gain_rows,), (gain_rows,))
    entries = tokens_in.shape[0] * ranks * lax.axis_size("rep") * width
    stats = jnp.sqrt(small[2 * width + 2 * HD :] / entries)
    return (
        block.astype(BF),
        d_tokens.astype(BF),
        grad_query,
        grad_key,
        grad_value,
        grad_out,
        grad_gate,
        grad_up,
        grad_down,
        attn_gain_sum,
        ffn_gain_sum,
        small[2 * width : 2 * width + HD],
        small[2 * width + HD : 2 * width + 2 * HD],
        stats,
    )


def solution(mesh):
    rows = P(("fsdp", "rep"), None)
    weight = P("fsdp", None)
    return jax.shard_map(
        local,
        mesh=mesh,
        in_specs=(rows, rows, *[weight] * 7, P("fsdp"), P("fsdp"), P(), P(), rows),
        out_specs=(rows, rows, *[weight] * 7, P("fsdp"), P("fsdp"), P(), P(), P()),
        check_vma=False,
    )
```

```python
import functools
import math

import jax
import jax.numpy as jnp
from jax import lax
from jax.experimental import pallas as pl
from jax.experimental.pallas import tpu as pltpu
from jax.sharding import PartitionSpec as P

HD = 64
EPS = 1e-05
THETA = 1000000.0
NEG = -1e30
BF = jnp.bfloat16
F32 = jnp.float32
ATTENTION_BYTES = 24 * 1024 * 1024
PLACE_BYTES = 44 * 1024 * 1024
LOW_COST = pl.CostEstimate(flops=1, bytes_accessed=1, transcendentals=0)


def matmul(left, right):
    return jnp.dot(left, right, preferred_element_type=F32)


def left_tmul(left, right):
    return lax.dot_general(left, right, (((0,), (0,)), ((), ())), preferred_element_type=F32)


def right_tmul(left, right):
    return lax.dot_general(left, right, (((1,), (1,)), ((), ())), preferred_element_type=F32)


def unit_rows(values):
    root = lax.rsqrt(jnp.mean(values * values, axis=-1, keepdims=True) + EPS)
    return values * root, root


def unit_back(unit, root, grad):
    return root * (grad - unit * jnp.mean(grad * unit, axis=-1, keepdims=True))


def turn(values, cosine, sine):
    half = values.shape[-1] // 2
    swapped = jnp.concatenate([values[:, half:], values[:, :half]], axis=1)
    return values * cosine + swapped * sine


def token_table(segments, width):
    index = jnp.arange(segments.shape[1])
    same = segments[:, :, None] == segments[:, None, :]
    position = jnp.sum((same & (index[None, :] < index[:, None])).astype(jnp.int32), axis=2)
    frequency = jnp.exp(jnp.arange(HD // 2).astype(F32) * (-2.0 * math.log(THETA) / HD))
    phase = position.astype(F32).reshape(-1, 1) * frequency
    cosine, sine = jnp.cos(phase), jnp.sin(phase)
    packs = jnp.arange(segments.shape[0], dtype=jnp.int32) % (width // segments.shape[1])
    marks = (segments + 4 * packs[:, None]).astype(F32).reshape(-1, 1)
    marks = jnp.broadcast_to(marks, (marks.shape[0], width))
    return jnp.concatenate([cosine, cosine, -sine, sine, marks], axis=1)


def head(values, index):
    return values[:, index * HD : (index + 1) * HD]


def allowed_block(marks):
    later = lax.broadcasted_iota(jnp.int32, marks.shape, 1)
    return (marks == marks.T) & (later <= lax.broadcasted_iota(jnp.int32, marks.shape, 0))


def probabilities(query, key, allowed):
    scores = right_tmul(query, key) * HD ** (-0.5)
    exponent = jnp.where(allowed, jnp.exp(scores), 0.0)
    return exponent * (1.0 / jnp.sum(exponent, axis=-1, keepdims=True))


def attention_kernel(q_here, kv_here, *refs):
    here_ref, other_ref, table_ref, gain_ref, q_gain_ref, k_gain_ref, w_qkv_ref, w_out_ref = refs[:8]
    attn_in_ref, qkv_ref, mixed_ref, own_ref, away_ref = refs[8:]
    group = q_here // kv_here
    rows = here_ref.shape[0]
    gain = gain_ref[...]
    for index, tokens_ref in enumerate((here_ref, other_ref)):
        unit, _ = unit_rows(tokens_ref[...].astype(F32))
        attn_in_ref[index * rows : (index + 1) * rows, :] = (unit * gain).astype(BF)
    qkv = matmul(attn_in_ref[...], w_qkv_ref[...])
    qkv_ref[...] = qkv
    blocks = [slice(index * rows, (index + 1) * rows) for index in range(2)]
    allowed = [allowed_block(table_ref[part, 2 * HD :]) for part in blocks]
    cosine, sine = table_ref[:, :HD], table_ref[:, HD : 2 * HD]
    for kv in range(kv_here):
        key = turn(unit_rows(head(qkv, q_here + kv))[0] * k_gain_ref[...], cosine, sine).astype(BF)
        value = head(qkv, q_here + kv_here + kv).astype(BF)
        for h in range(kv * group, (kv + 1) * group):
            query = turn(unit_rows(head(qkv, h))[0] * q_gain_ref[...], cosine, sine).astype(BF)
            for index, part in enumerate(blocks):
                probs = probabilities(query[part], key[part], allowed[index])
                mixed_ref[part, h * HD : (h + 1) * HD] = matmul(probs.astype(BF), value[part]).astype(BF)
    mixed = mixed_ref[...]
    own_ref[...] = matmul(mixed[:rows], w_out_ref[...]).astype(BF)
    away_ref[...] = matmul(mixed[rows:], w_out_ref[...]).astype(BF)


def attention_back_kernel(q_here, kv_here, *refs):
    here_ref, other_ref, qkv_ref, table_ref, q_gain_ref, k_gain_ref, w_qkv_ref, w_out_ref = refs[:8]
    g_attn_ref, g_qkv_ref, own_ref, away_ref, gains_ref = refs[8:]
    group = q_here // kv_here
    rows = here_ref.shape[0]
    g_attn_ref[:rows, :] = here_ref[...]
    g_attn_ref[rows:, :] = other_ref[...]
    g_mixed = right_tmul(g_attn_ref[...], w_out_ref[...]).astype(BF)
    qkv = qkv_ref[...]
    blocks = [slice(index * rows, (index + 1) * rows) for index in range(2)]
    allowed = [allowed_block(table_ref[part, 2 * HD :]) for part in blocks]
    cosine, sine = table_ref[:, :HD], table_ref[:, HD : 2 * HD]
    q_gain, k_gain = q_gain_ref[...], k_gain_ref[...]
    scale = HD ** (-0.5)
    q_sum = jnp.zeros((1, HD), F32)
    k_sum = jnp.zeros((1, HD), F32)
    pieces = {}
    for kv in range(kv_here):
        k_unit, k_root = unit_rows(head(qkv, q_here + kv))
        key = turn(k_unit * k_gain, cosine, sine).astype(BF)
        value = head(qkv, q_here + kv_here + kv).astype(BF)
        g_k, g_v = [0.0, 0.0], [0.0, 0.0]
        for h in range(kv * group, (kv + 1) * group):
            q_unit, q_root = unit_rows(head(qkv, h))
            query = turn(q_unit * q_gain, cosine, sine).astype(BF)
            g_head = head(g_mixed, h)
            g_query = []
            for index, part in enumerate(blocks):
                probs = probabilities(query[part], key[part], allowed[index])
                g_probs = right_tmul(g_head[part], value[part])
                g_v[index] = g_v[index] + left_tmul(probs.astype(BF), g_head[part])
                g_scores = probs * (g_probs - jnp.sum(probs * g_probs, axis=-1, keepdims=True))
                g_scores = g_scores.astype(BF)
                g_k[index] = g_k[index] + left_tmul(g_scores, query[part])
                g_query.append(matmul(g_scores, key[part]))
            back = turn(jnp.concatenate(g_query, axis=0) * scale, cosine, -sine)
            q_sum = q_sum + jnp.sum(back * q_unit, axis=0, keepdims=True)
            pieces[h] = unit_back(q_unit, q_root, back * q_gain).astype(BF)
        back = turn(jnp.concatenate(g_k, axis=0) * scale, cosine, -sine)
        k_sum = k_sum + jnp.sum(back * k_unit, axis=0, keepdims=True)
        pieces[q_here + kv] = unit_back(k_unit, k_root, back * k_gain).astype(BF)
        pieces[q_here + kv_here + kv] = jnp.concatenate(g_v, axis=0).astype(BF)
    g_qkv = jnp.concatenate([pieces[index] for index in range(q_here + 2 * kv_here)], axis=1)
    g_qkv_ref[...] = g_qkv
    own_ref[...] = right_tmul(g_qkv[:rows], w_qkv_ref[...]).astype(BF)
    away_ref[...] = right_tmul(g_qkv[rows:], w_qkv_ref[...]).astype(BF)
    gains_ref[...] = jnp.concatenate([q_sum, k_sum], axis=0)


def single(array, block=None, index=0):
    block = array.shape if block is None else block
    return pl.BlockSpec(block, lambda step: (index,) + (0,) * (len(block) - 1))


def slot_call(kernel, name, arrays, specs, shapes):
    return pl.pallas_call(
        kernel,
        grid=(1,),
        in_specs=specs,
        out_specs=[single(shape) for shape in shapes],
        out_shape=shapes,
        compiler_params=pltpu.CompilerParams(vmem_limit_bytes=ATTENTION_BYTES),
        cost_estimate=LOW_COST,
        name=name,
    )(*arrays)


def attention(slot, here, other, table, gain, q_gain, k_gain, w_qkv, w_out, q_here, kv_here):
    rows, width = here.shape
    arrays = (here, other, table, gain, q_gain, k_gain, w_qkv, w_out)
    specs = [single(array) for array in arrays]
    specs[2] = single(table, (2 * rows, table.shape[1]), slot)
    shapes = [
        jax.ShapeDtypeStruct((2 * rows, width), BF),
        jax.ShapeDtypeStruct((2 * rows, w_qkv.shape[1]), F32),
        jax.ShapeDtypeStruct((2 * rows, q_here * HD), BF),
        jax.ShapeDtypeStruct((rows, width), BF),
        jax.ShapeDtypeStruct((rows, width), BF),
    ]
    kernel = functools.partial(attention_kernel, q_here, kv_here)
    return slot_call(kernel, "attention", arrays, specs, shapes)


def attention_back(slot, here, other, qkv, table, q_gain, k_gain, w_qkv, w_out, q_here, kv_here):
    rows, width = here.shape
    arrays = (here, other, qkv, table, q_gain, k_gain, w_qkv, w_out)
    specs = [single(array) for array in arrays]
    specs[3] = single(table, (2 * rows, table.shape[1]), slot)
    shapes = [
        jax.ShapeDtypeStruct((2 * rows, width), BF),
        jax.ShapeDtypeStruct((2 * rows, w_qkv.shape[1]), BF),
        jax.ShapeDtypeStruct((rows, width), BF),
        jax.ShapeDtypeStruct((rows, width), BF),
        jax.ShapeDtypeStruct((2, HD), F32),
    ]
    kernel = functools.partial(attention_back_kernel, q_here, kv_here)
    return slot_call(kernel, "attention_back", arrays, specs, shapes)


def place_kernel(moves, source_count, out_count, row_ref, column_ref, *refs):
    sources, outs = refs[:source_count], refs[source_count : source_count + out_count]
    refs = refs[source_count + out_count :]
    cast = outs[0].dtype != sources[0].dtype
    staged = refs[source_count:-2] if cast else ()
    loaded, loads, stores = refs[:source_count], refs[-2], refs[-1]
    reads = [
        pltpu.make_async_copy(source, buffer, loads.at[index])
        for index, (source, buffer) in enumerate(zip(sources, loaded))
    ]
    for read in reads:
        read.start()
    writes = []
    arrived = set()
    for index, (source, slot, rows, columns, out) in enumerate(moves):
        height, width = rows.stop - rows.start, columns.stop - columns.start
        row = pl.multiple_of(row_ref[index] * height, height)
        if source not in arrived:
            reads[source].wait()
            arrived.add(source)
        if cast:
            staged[index][...] = loaded[source][slot, rows, columns].astype(outs[out].dtype)
            block = staged[index]
        else:
            block = loaded[source].at[slot, rows, columns]
        if len(outs[out].shape) == 3:
            target = outs[out].at[column_ref[index], pl.ds(row, height), :]
        elif outs[out].shape[1] == width:
            target = outs[out].at[pl.ds(row, height), :]
        else:
            column = pl.multiple_of(column_ref[index] * width, width)
            target = outs[out].at[pl.ds(row, height), pl.ds(column, width)]
        writes.append(pltpu.make_async_copy(block, target, stores.at[index]))
        writes[-1].start()
    for write in writes:
        write.wait()


def place_blocks(sources, moves, row_blocks, column_blocks, shapes, dtype):
    scratch = [pltpu.VMEM(source.shape, source.dtype) for source in sources]
    if dtype != sources[0].dtype:
        scratch += [
            pltpu.VMEM((rows.stop - rows.start, columns.stop - columns.start), dtype)
            for _, _, rows, columns, _ in moves
        ]
    scratch += [pltpu.SemaphoreType.DMA((len(sources),)), pltpu.SemaphoreType.DMA((len(moves),))]
    anywhere = pl.BlockSpec(memory_space=pl.ANY)
    return pl.pallas_call(
        functools.partial(place_kernel, moves, len(sources), len(shapes)),
        in_specs=[pl.BlockSpec(memory_space=pltpu.SMEM)] * 2 + [anywhere] * len(sources),
        out_specs=[anywhere] * len(shapes),
        out_shape=[jax.ShapeDtypeStruct(shape, dtype) for shape in shapes],
        scratch_shapes=scratch,
        compiler_params=pltpu.CompilerParams(vmem_limit_bytes=PLACE_BYTES),
        cost_estimate=LOW_COST,
        name="place_blocks",
    )(row_blocks.astype(jnp.int32), column_blocks.astype(jnp.int32), *sources)


def after(values, *others):
    return lax.optimization_barrier((values, *others))[0]


def move(values, send):
    ranks, copies = lax.axis_size("fsdp"), lax.axis_size("rep")
    pairs = []
    for f in range(ranks):
        for r in range(copies):
            to = send(f, r)
            if to is not None:
                pairs.append((f * copies + r, to[0] * copies + to[1]))
    return lax.ppermute(values, ("fsdp", "rep"), pairs)


def ring(values, step):
    ranks = lax.axis_size("fsdp")
    return move(values, lambda f, r: ((f + 2 * step) % ranks, r))


def swap_core(values):
    return move(values, lambda f, r: (f, r ^ 1))


def swap_x(values):
    return move(values, lambda f, r: (f, r ^ 2))


def swap_twin(values):
    return move(values, lambda f, r: (f ^ 1, r ^ 1))


def place():
    f, r = lax.axis_index("fsdp"), lax.axis_index("rep")
    return f // 2, f % 2, r // 2, r % 2


def pick(values, index, axis=0):
    return lax.dynamic_index_in_dim(values, index, axis, keepdims=False)


def ordered(slots, z):
    depth = len(slots)
    out = jnp.zeros((depth, *slots[0].shape), slots[0].dtype)
    for k, slot in enumerate(slots):
        out = lax.dynamic_update_index_in_dim(out, slot, (z - k) % depth, 0)
    return out


def add(left, right):
    return (left.astype(F32) + right.astype(F32)).astype(BF)


def gather_group(values, name, beside=None):
    slots = []
    for s in range(lax.axis_size("fsdp") // 2):
        with jax.named_scope(f"gather_{name}_{s}"):
            if s > 0:
                values = ring(values if beside is None else beside(s, values), 1)
            slots.append((values, swap_core(values)))
    return slots


def scatter_group(partial, name, beside=None):
    moving = None
    for step, (own, away) in enumerate((*partial[1:], partial[0])):
        with jax.named_scope(f"scatter_{name}_{step}"):
            total = own.astype(F32) + swap_core(away).astype(F32)
            if moving is not None:
                total = total + ring(moving, 1).astype(F32)
            moving = total.astype(BF)
        if beside is not None:
            moving = beside(step, moving)
    return total


def total_sum(values, beside):
    steps = [lambda f, r, bit=bit: (f, r ^ (1 << bit)) for bit in range(2)]
    ranks = lax.axis_size("fsdp")
    steps += [lambda f, r, bit=bit: (f ^ (1 << bit), r) for bit in range((ranks - 1).bit_length())]
    for index, step in enumerate(steps):
        values = values + after(move(values, step), *beside.get(index, ()))
    return values


class ColumnsIn:
    def __init__(self, parts, rows, name, hold=lambda slots: slots):
        with jax.named_scope(f"{name}_along_z"):
            slots = [ring(part, k) if k else part for k, part in enumerate(parts)]
            self.same = jnp.stack(hold(slots))
        with jax.named_scope(f"{name}_across"):
            self.across_x, self.across_y = swap_x(self.same), swap_twin(self.same)
        self.rows, self.name = rows, name

    def joined(self, split, *others):
        z, y, x, core = place()
        depth, columns = self.same.shape[0], self.same.shape[2]
        middle = depth // 2 if split else depth
        with jax.named_scope(f"{self.name}_across_both"):
            across_x, across_y = after((self.across_x, self.across_y), *others)
            rest = [swap_twin(across_x[:middle])]
            if split:
                rest.append(swap_x(across_y[middle:]))
        sources = [self.same, self.across_x, self.across_y, *rest]
        moves = [
            (source, slot, slice(0, self.rows), slice(0, columns), 0)
            for source, array in enumerate(sources)
            for slot in range(array.shape[0])
        ]
        where_z = (z - jnp.arange(depth)) % depth
        index = lambda yy, xx: (where_z * 2 + yy) * 2 + xx
        places = [index(y, x), index(y, 1 - x), index(1 - y, x), index(1 - y, 1 - x)]
        places = jnp.concatenate(places)
        shape = (4 * depth * self.rows, columns)
        return place_blocks(sources, moves, places, jnp.zeros_like(places), [shape], BF)[0]


def scoped(step):
    def wrap(method):
        def named(self, *others):
            with jax.named_scope(f"{self.name}_{step}"):
                return method(self, *others)

        return named

    return wrap


class ColumnsOut:
    def __init__(self, grad, y_first, name):
        self.name = name
        z, y, x, core = place()
        self.depth = lax.axis_size("fsdp") // 2
        self.y_first = y_first
        columns = grad.shape[1]
        self.blocks = grad.reshape(self.depth, 2, 2, -1, columns)
        axis, index = (1, 1 - y) if y_first else (2, 1 - x)
        self.payload = pick(self.blocks, index, axis)

    @scoped("first")
    def first(self, *others):
        z, y, x, core = place()
        axis, index = (1, y) if self.y_first else (2, x)
        swap = swap_twin if self.y_first else swap_x
        came, own = after(swap(self.payload), *others), pick(self.blocks, index, axis)
        here, there = (x, 1 - x) if self.y_first else (y, 1 - y)
        self.payload = add(pick(own, there, 1), pick(came, there, 1))
        self.kept = (pick(own, here, 1), pick(came, here, 1))

    @scoped("second")
    def second(self, *others):
        z, y, x, core = place()
        swap = swap_x if self.y_first else swap_twin
        came = after(swap(self.payload), *others).astype(F32)
        total = (self.kept[0].astype(F32) + self.kept[1].astype(F32) + came).astype(BF)
        self.payload = [pick(total, (z + k) % self.depth) for k in range(self.depth)]


def along_z(payloads, name):
    with jax.named_scope(f"sum_{name}_along_z"):
        parts = [jnp.concatenate(items, axis=1) for items in zip(*payloads)]
        return [ring(part, k) if k else part for k, part in enumerate(parts)]


def across_x(same, name):
    with jax.named_scope(f"sum_{name}_across"):
        return swap_x(same)


def columns_placed(same, across, widths, name):
    z, y, x, core = place()
    depth, rows, total = same.shape
    with jax.named_scope(f"sum_{name}_core"):
        parts = same, across, swap_core(same), swap_core(across)
    ones = jnp.ones((depth,), jnp.int32)
    row_blocks = jnp.concatenate([x * ones, (1 - x) * ones] * 2)
    where_z = (z - jnp.arange(depth)) % depth
    own, other = 2 * where_z + (y ^ core), 2 * where_z + (1 - (y ^ core))
    column_blocks = jnp.concatenate([own, own, other, other])
    aligned = all(width % 128 == 0 for width in widths)
    spans = []
    for width in widths if aligned else [total]:
        first = spans[-1].stop if spans else 0
        spans.append(slice(first, first + width))
    moves = [
        (source, slot, slice(0, rows), span, out)
        for source in range(4)
        for slot in range(depth)
        for out, span in enumerate(spans)
    ]
    if aligned:
        shapes = [(2 * rows, 2 * depth * width) for width in widths]
    else:
        shapes = [(2 * depth, 2 * rows, total)]
    repeat = lambda blocks: jnp.repeat(blocks, len(spans))
    outs = place_blocks(parts, moves, repeat(row_blocks), repeat(column_blocks), shapes, F32)
    if aligned:
        return outs
    rows_first = outs[0].transpose(1, 0, 2)
    pieces, first = [], 0
    for width in widths:
        pieces.append(rows_first[:, :, first : first + width].reshape(2 * rows, -1))
        first += width
    return pieces


def rows_across_y(weight, name):
    half = weight.shape[0] // 2
    with jax.named_scope(f"{name}_across_y"):
        part = lax.dynamic_slice_in_dim(weight, place()[2] * half, half, axis=0)
        return move(part, lambda f, r: (f ^ 1, r) if r % 2 else None)


def rows_here(weight, part, name):
    z, y, x, core = place()
    half = weight.shape[0] // 2
    with jax.named_scope(f"{name}_across_x"):
        other = move(part, lambda f, r: (f, r ^ 2) if r % 2 else None)
    low = jnp.where(core == 0, weight[:half], jnp.where(x == 0, part, other))
    high = jnp.where(core == 0, weight[half:], jnp.where(x == 0, other, part))
    return jnp.concatenate([low, high], axis=0)


class RowsOut:
    def __init__(self, grad, name):
        self.name = name
        self.grad = self.payload = grad.reshape(2, -1, grad.shape[1])

    @scoped("first")
    def first(self, *others):
        z, y, x, core = place()
        came = after(move(self.payload, lambda f, r: (f ^ 1, r ^ 1) if r % 2 else None), *others)
        self.payload = add(pick(self.grad, 1 - x), pick(came, 1 - x))
        self.kept = (pick(self.grad, x), pick(came, x))

    @scoped("second")
    def second(self, *others):
        came = move(self.payload, lambda f, r: None if r % 2 else (f, r ^ 2))
        came = after(came, *others).astype(F32)
        self.payload = (self.kept[0].astype(F32) + self.kept[1].astype(F32) + came).astype(BF)

    @scoped("third")
    def third(self, *others):
        came = after(move(self.payload, lambda f, r: None if r % 2 else (f, r ^ 2)), *others)
        self.payload = jnp.stack([self.payload, came])

    @scoped("last")
    def last(self):
        z, y, x, core = place()
        came = move(self.payload, lambda f, r: None if r % 2 else (f, r ^ 1))
        parts = jnp.where(core == 0, self.payload, came)
        rows, columns = parts.shape[1:]
        moves = [(0, slot, slice(0, rows), slice(0, columns), 0) for slot in range(2)]
        places = jnp.stack([x, 1 - x])
        return place_blocks([parts], moves, places, jnp.zeros_like(places), [(2 * rows, columns)], F32)[0]


def local(
    tokens_in,
    segment_ids,
    w_query,
    w_key,
    w_value,
    w_out,
    w_gate,
    w_up,
    w_down,
    gain_attn,
    gain_ffn,
    gain_query,
    gain_key,
    d_out,
):
    ranks = lax.axis_size("fsdp")
    rank = lax.axis_index("fsdp")
    depth = ranks // 2
    z, y, x, core = place()
    width = tokens_in.shape[1]
    pack = segment_ids.shape[1]
    heads = w_query.shape[1] // HD
    kv_heads = w_key.shape[1] // HD
    share = max(1, ranks // kv_heads)
    q_here = heads // ranks
    kv_here = max(1, kv_heads // ranks)
    group = q_here // kv_here
    q_cols, kv_cols = q_here * HD, kv_here * HD
    scale = HD ** (-0.5)

    q_gain = gain_query.astype(F32)[None]
    k_gain = gain_key.astype(F32)[None]

    rows_x = w_query.shape[0] // 2
    cut = lambda weight, start, size: lax.dynamic_slice(weight, (x * rows_x, start), (rows_x, size))
    wide = q_cols + 2 * kv_cols
    seg_size = segment_ids.size
    extra = jnp.concatenate([segment_ids.reshape(-1).astype(BF), gain_attn, gain_ffn])
    extra = jnp.pad(extra, (0, 16 * wide - extra.size)).reshape(16, wide)

    def cut_qkv(block):
        kv = block // share * kv_cols
        parts = [cut(w_query, block * q_cols, q_cols), cut(w_key, kv, kv_cols), cut(w_value, kv, kv_cols)]
        return jnp.concatenate([jnp.concatenate(parts, axis=1), extra], axis=0)

    def cutter(weight):
        size = weight.shape[1] // ranks
        return lambda block: cut(weight, block * size, size)

    qkv_parts = [cut_qkv(2 * ((z + k) % depth) + (y ^ core)) for k in range(depth)]
    qkv_in = ColumnsIn(qkv_parts, rows_x, "w_qkv")
    w_qkv = qkv_in.joined(False)
    w_out_here = rows_here(w_out, rows_across_y(w_out, "w_out"), "w_out")
    down_part = rows_across_y(after(w_down, w_qkv), "w_down")
    w_down_here = rows_here(w_down, down_part, "w_down")
    w_gate_late, w_up_late = after((w_gate, w_up), qkv_in.same)
    columns_here = w_gate.shape[1] // ranks

    def cut_glu(block):
        first = block * columns_here
        return jnp.concatenate(
            [cut(w_gate_late, first, columns_here), cut(w_up_late, first, columns_here)], axis=1
        )

    glu_parts = [cut_glu(2 * ((z + k) % depth) + (y ^ core)) for k in range(depth)]
    glu_in = ColumnsIn(glu_parts, rows_x, "w_glu", lambda slots: after((*slots,), w_qkv, w_out_here))
    own_slots, twin_slots = qkv_in.same, qkv_in.across_y
    own_extra = own_slots[:, rows_x:].reshape(depth, -1)
    twin_extra = twin_slots[:, rows_x:].reshape(depth, -1)
    seg_slots = own_extra[:, :seg_size].reshape(depth, 1, -1, pack)
    segments = jnp.concatenate([seg_slots, swap_core(seg_slots)], axis=1).reshape(-1, pack).astype(jnp.int32)
    span = slice(seg_size, seg_size + 2 * gain_attn.size)
    pieces = jnp.stack([own_extra[:, span], twin_extra[:, span]], axis=1)
    pieces = ordered([pieces[k] for k in range(depth)], z).astype(F32)
    pieces = jnp.where(y == 0, pieces, pieces[:, ::-1])
    gains = pieces.reshape(depth, 2, 2, -1).transpose(2, 0, 1, 3).reshape(2, -1)
    attn_gain, ffn_gain = gains[0], gains[1]

    token_ties = {1: (glu_in.same, attn_gain, down_part), 2: (w_down_here,)}
    beside_tokens = lambda s, sent: after(sent, *token_ties.get(s, ()))
    token_slots = gather_group(tokens_in, "tokens", beside_tokens)
    block_rows = tokens_in.shape[0]
    table = token_table(segments, block_rows)
    kept, partial = [None] * depth, [None] * depth
    order = (*range(1, depth), 0)
    for s in order:
        here, other = token_slots[s]
        if s == depth - 1:
            here = after(here, glu_in.across_x, glu_in.across_y)
        *kept[s], own, away = attention(
            s, here, other, table, attn_gain[None], q_gain, k_gain, w_qkv, w_out_here, q_here, kv_here
        )
        partial[s] = (own, away)
    tokens = tokens_in.astype(F32)
    unit_tokens, root_tokens = unit_rows(tokens)

    w_glu = glu_in.joined(True)
    attn_branch = after(scatter_group(partial, "attn_branch"), w_glu)

    middle = tokens + attn_branch
    unit_middle, root_middle = unit_rows(middle)
    ffn_slots = gather_group((unit_middle * ffn_gain).astype(BF), "ffn_in")
    beside_d_out = lambda s, sent: after(sent, ffn_slots[-1][0]) if s == 1 else sent
    grad_slots = gather_group(d_out, "d_out", beside_d_out)
    glu_kept, back_partial, down_partial = [None] * depth, [None] * depth, []
    for s in order:
        ffn_in = jnp.concatenate(ffn_slots[s], axis=0)
        g_ffn = jnp.concatenate(grad_slots[s], axis=0)
        gate_up = matmul(ffn_in, w_glu)
        gate, up = gate_up[:, :columns_here], gate_up[:, columns_here:]
        sig = jax.nn.sigmoid(gate)
        silu = gate * sig
        hidden = (silu * up).astype(BF)
        g_hidden = right_tmul(g_ffn, w_down_here).astype(BF).astype(F32)
        g_gate = (g_hidden * up * sig * (1 + gate * (1 - sig))).astype(BF)
        g_up = (g_hidden * silu).astype(BF)
        part = right_tmul(jnp.concatenate([g_gate, g_up], axis=1), w_glu).astype(BF)
        back_partial[s] = (part[:block_rows], part[block_rows:])
        glu_kept[s] = (ffn_in, g_ffn, hidden, g_gate, g_up)
    ffn_in, g_ffn, hidden, g_gate, g_up = (jnp.concatenate(items, axis=0) for items in zip(*glu_kept))
    sums = {}

    def beside_feed(step, sent):
        if step == depth - 3:
            grad = left_tmul(*after((ffn_in, g_gate), sent)).astype(BF)
            sums["gate"] = ColumnsOut(grad, True, "sum_gate")
            grad = left_tmul(*after((ffn_in, g_up), sums["gate"].payload)).astype(BF)
            sums["up"] = ColumnsOut(grad, False, "sum_up")
        if step == depth - 2:
            sent = after(sent, sums["up"].payload)
        return sent

    g_ffn_in = scatter_group(back_partial, "g_ffn_in", beside_feed)
    gate_sum, up_sum = sums["gate"], sums["up"]
    g_ffn_in = after(g_ffn_in, gate_sum.payload, up_sum.payload)
    ffn_gain_grad = jnp.sum(g_ffn_in * unit_middle, axis=0)
    g_middle = d_out.astype(F32) + unit_back(unit_middle, root_middle, g_ffn_in * ffn_gain)

    attn_slots = gather_group(g_middle.astype(BF), "g_attn")
    back_kept, partial = [None] * depth, [None] * depth
    head_gains = 0.0
    for s in order:
        here, other = attn_slots[s]
        if s == 2:
            gate_sum.first(partial[1][1])
            up_sum.first(partial[1][1])
            here = after(here, gate_sum.payload, up_sum.payload)
        if s == 3:
            gate_sum.second(partial[2][1])
            up_sum.second(partial[2][1])
            grad_down = left_tmul(*after((hidden, g_ffn), up_sum.payload)).astype(BF)
            down_sum = RowsOut(grad_down, "sum_down")
            here = after(here, gate_sum.payload, up_sum.payload, down_sum.payload)
        g_attn, g_qkv, own, away, gain_part = attention_back(
            s, here, other, kept[s][1], table, q_gain, k_gain, w_qkv, w_out_here, q_here, kv_here
        )
        head_gains = head_gains + gain_part
        back_kept[s] = (g_attn, g_qkv)
        partial[s] = (own, away)
    attn_in, _, mixed = (jnp.concatenate(items, axis=0) for items in zip(*kept))
    g_attn, g_qkv = (jnp.concatenate(items, axis=0) for items in zip(*back_kept))
    grad_qkv = left_tmul(attn_in, g_qkv).astype(BF)
    qkv_sum = ColumnsOut(grad_qkv, True, "sum_qkv")
    grad_out = left_tmul(*after((mixed, g_attn), qkv_sum.payload)).astype(BF)
    out_sum = RowsOut(grad_out, "sum_out")
    glu_parts = [jnp.concatenate(pair, axis=1) for pair in zip(gate_sum.payload, up_sum.payload)]
    glu_slots = {0: glu_parts[0]}
    steps = sorted(range(1, depth), key=lambda k: -min(k, depth - k))
    last = None
    for k in steps:
        with jax.named_scope(f"sum_glu_along_z_{k}"):
            part = glu_parts[k] if last is None else after(glu_parts[k], last)
            last = glu_slots[k] = ring(part, k)
        if k == steps[0]:
            last = after(last, qkv_sum.payload, out_sum.payload)
    glu_same = jnp.stack([glu_slots[k] for k in range(depth)])
    glu_across = across_x(glu_same, "glu")

    def beside_back(step, sent):
        if step == 0:
            sent = after(sent, glu_slots[steps[0]])
        if step == 1:
            sent = after(sent, glu_same)
            for item in (down_sum, qkv_sum, out_sum):
                item.first(sent)
        if step == 2:
            sent = after(sent, down_sum.payload, qkv_sum.payload, out_sum.payload, glu_across)
        return sent

    g_attn_in = scatter_group(partial, "g_attn_in", beside_back)
    attn_gain_grad = jnp.sum(g_attn_in * unit_tokens, axis=0)
    d_tokens = g_middle + unit_back(unit_tokens, root_tokens, g_attn_in * attn_gain)

    for s in range(depth):
        part = matmul(after(glu_kept[s][2], glu_same), w_down_here).astype(BF)
        down_partial.append((part[:block_rows], part[block_rows:]))
    glu_placed = columns_placed(glu_same, glu_across, [columns_here, columns_here], "glu")

    arrived = []

    def beside_branch(step, sent):
        arrived.append(sent)
        if step == 0:
            return after(sent, d_tokens)
        if step == 1:
            down_sum.second(d_tokens)
            return after(sent, down_sum.payload)
        if step == 2:
            qkv_sum.second(arrived[1])
            out_sum.second(arrived[1])
            return after(sent, qkv_sum.payload, out_sum.payload)
        return sent

    ffn_branch = scatter_group(down_partial, "ffn_branch", beside_branch)
    grad_gate, grad_up = glu_placed
    qkv_slots = along_z([qkv_sum.payload], "qkv")
    qkv_same = jnp.stack(after((*qkv_slots,), arrived[-1]))
    block = middle + after(ffn_branch, *glu_placed, qkv_same)
    qkv_across = across_x(qkv_same, "qkv")
    grad_query, grad_kv = columns_placed(qkv_same, qkv_across, [q_cols, 2 * kv_cols], "qkv")
    down_sum.third(arrived[2])
    out_sum.third(arrived[-1])
    grad_down, grad_out = down_sum.last(), out_sum.last()
    grad_kv = grad_kv.reshape(grad_kv.shape[0], -1, share, 2 * kv_cols).sum(axis=2)
    grad_key = grad_kv[:, :, :kv_cols].reshape(grad_kv.shape[0], -1)
    grad_value = grad_kv[:, :, kv_cols:].reshape(grad_kv.shape[0], -1)
    squares = jnp.stack(
        [jnp.sum(item * item) for item in (middle, attn_branch, ffn_branch, block, d_tokens)]
    )
    small = jnp.concatenate([attn_gain_grad, ffn_gain_grad, head_gains[0], head_gains[1], squares])
    with jax.named_scope("total_sum"):
        small = total_sum(small, {0: (grad_down,), 1: (grad_out,), 3: (grad_query,)})
    gain_rows = gain_attn.shape[0]
    attn_gain_sum = lax.dynamic_slice(small, (rank * gain_rows,), (gain_rows,))
    ffn_gain_sum = lax.dynamic_slice(small, (width + rank * gain_rows,), (gain_rows,))
    entries = tokens_in.shape[0] * ranks * lax.axis_size("rep") * width
    stats = jnp.sqrt(small[2 * width + 2 * HD :] / entries)
    return (
        block.astype(BF),
        d_tokens.astype(BF),
        grad_query,
        grad_key,
        grad_value,
        grad_out,
        grad_gate,
        grad_up,
        grad_down,
        attn_gain_sum,
        ffn_gain_sum,
        small[2 * width : 2 * width + HD],
        small[2 * width + HD : 2 * width + 2 * HD],
        stats,
    )


def solution(mesh):
    rows = P(("fsdp", "rep"), None)
    weight = P("fsdp", None)
    return jax.shard_map(
        local,
        mesh=mesh,
        in_specs=(rows, rows, *[weight] * 7, P("fsdp"), P("fsdp"), P(), P(), rows),
        out_specs=(rows, rows, *[weight] * 7, P("fsdp"), P("fsdp"), P(), P(), P()),
        check_vma=False,
    )
```

```python
import functools
import math

import jax
import jax.numpy as jnp
from jax import lax
from jax.experimental import pallas as pl
from jax.experimental.pallas import tpu as pltpu
from jax.sharding import PartitionSpec as P

HD = 64
EPS = 1e-05
THETA = 1000000.0
NEG = -1e30
BF = jnp.bfloat16
F32 = jnp.float32
ATTENTION_BYTES = 24 * 1024 * 1024
PLACE_BYTES = 44 * 1024 * 1024
LOW_COST = pl.CostEstimate(flops=1, bytes_accessed=1, transcendentals=0)


def matmul(left, right):
    return jnp.dot(left, right, preferred_element_type=F32)


def left_tmul(left, right):
    return lax.dot_general(left, right, (((0,), (0,)), ((), ())), preferred_element_type=F32)


def right_tmul(left, right):
    return lax.dot_general(left, right, (((1,), (1,)), ((), ())), preferred_element_type=F32)


def unit_rows(values):
    root = lax.rsqrt(jnp.mean(values * values, axis=-1, keepdims=True) + EPS)
    return values * root, root


def unit_back(unit, root, grad):
    return root * (grad - unit * jnp.mean(grad * unit, axis=-1, keepdims=True))


def turn(values, cosine, sine):
    half = values.shape[-1] // 2
    swapped = jnp.concatenate([values[:, half:], values[:, :half]], axis=1)
    return values * cosine + swapped * sine


def token_table(segments, width):
    index = jnp.arange(segments.shape[1])
    same = segments[:, :, None] == segments[:, None, :]
    position = jnp.sum((same & (index[None, :] < index[:, None])).astype(jnp.int32), axis=2)
    frequency = jnp.exp(jnp.arange(HD // 2).astype(F32) * (-2.0 * math.log(THETA) / HD))
    phase = position.astype(F32).reshape(-1, 1) * frequency
    cosine, sine = jnp.cos(phase), jnp.sin(phase)
    packs = jnp.arange(segments.shape[0], dtype=jnp.int32) % (width // segments.shape[1])
    marks = (segments + 4 * packs[:, None]).astype(F32).reshape(-1, 1)
    marks = jnp.broadcast_to(marks, (marks.shape[0], width))
    return jnp.concatenate([cosine, cosine, -sine, sine, marks], axis=1)


def head(values, index):
    return values[:, index * HD : (index + 1) * HD]


def allowed_block(marks):
    later = lax.broadcasted_iota(jnp.int32, marks.shape, 1)
    return (marks == marks.T) & (later <= lax.broadcasted_iota(jnp.int32, marks.shape, 0))


def probabilities(query, key, allowed):
    scores = right_tmul(query, key) * HD ** (-0.5)
    exponent = jnp.where(allowed, jnp.exp(scores), 0.0)
    return exponent * (1.0 / jnp.sum(exponent, axis=-1, keepdims=True))


def attention_kernel(q_here, kv_here, *refs):
    here_ref, other_ref, table_ref, gain_ref, q_gain_ref, k_gain_ref, w_qkv_ref, w_out_ref = refs[:8]
    attn_in_ref, qkv_ref, mixed_ref, own_ref, away_ref = refs[8:]
    group = q_here // kv_here
    rows = here_ref.shape[0]
    gain = gain_ref[...]
    for index, tokens_ref in enumerate((here_ref, other_ref)):
        unit, _ = unit_rows(tokens_ref[...].astype(F32))
        attn_in_ref[index * rows : (index + 1) * rows, :] = (unit * gain).astype(BF)
    qkv = matmul(attn_in_ref[...], w_qkv_ref[...])
    qkv_ref[...] = qkv
    blocks = [slice(index * rows, (index + 1) * rows) for index in range(2)]
    allowed = [allowed_block(table_ref[part, 2 * HD :]) for part in blocks]
    cosine, sine = table_ref[:, :HD], table_ref[:, HD : 2 * HD]
    for kv in range(kv_here):
        key = turn(unit_rows(head(qkv, q_here + kv))[0] * k_gain_ref[...], cosine, sine).astype(BF)
        value = head(qkv, q_here + kv_here + kv).astype(BF)
        for h in range(kv * group, (kv + 1) * group):
            query = turn(unit_rows(head(qkv, h))[0] * q_gain_ref[...], cosine, sine).astype(BF)
            for index, part in enumerate(blocks):
                probs = probabilities(query[part], key[part], allowed[index])
                mixed_ref[part, h * HD : (h + 1) * HD] = matmul(probs.astype(BF), value[part]).astype(BF)
    mixed = mixed_ref[...]
    own_ref[...] = matmul(mixed[:rows], w_out_ref[...]).astype(BF)
    away_ref[...] = matmul(mixed[rows:], w_out_ref[...]).astype(BF)


def attention_back_kernel(q_here, kv_here, *refs):
    here_ref, other_ref, qkv_ref, table_ref, q_gain_ref, k_gain_ref, w_qkv_ref, w_out_ref = refs[:8]
    g_attn_ref, g_qkv_ref, own_ref, away_ref, gains_ref = refs[8:]
    group = q_here // kv_here
    rows = here_ref.shape[0]
    g_attn_ref[:rows, :] = here_ref[...]
    g_attn_ref[rows:, :] = other_ref[...]
    g_mixed = right_tmul(g_attn_ref[...], w_out_ref[...]).astype(BF)
    qkv = qkv_ref[...]
    blocks = [slice(index * rows, (index + 1) * rows) for index in range(2)]
    allowed = [allowed_block(table_ref[part, 2 * HD :]) for part in blocks]
    cosine, sine = table_ref[:, :HD], table_ref[:, HD : 2 * HD]
    q_gain, k_gain = q_gain_ref[...], k_gain_ref[...]
    scale = HD ** (-0.5)
    q_sum = jnp.zeros((1, HD), F32)
    k_sum = jnp.zeros((1, HD), F32)
    pieces = {}
    for kv in range(kv_here):
        k_unit, k_root = unit_rows(head(qkv, q_here + kv))
        key = turn(k_unit * k_gain, cosine, sine).astype(BF)
        value = head(qkv, q_here + kv_here + kv).astype(BF)
        g_k, g_v = [0.0, 0.0], [0.0, 0.0]
        for h in range(kv * group, (kv + 1) * group):
            q_unit, q_root = unit_rows(head(qkv, h))
            query = turn(q_unit * q_gain, cosine, sine).astype(BF)
            g_head = head(g_mixed, h)
            g_query = []
            for index, part in enumerate(blocks):
                probs = probabilities(query[part], key[part], allowed[index])
                g_probs = right_tmul(g_head[part], value[part])
                g_v[index] = g_v[index] + left_tmul(probs.astype(BF), g_head[part])
                g_scores = probs * (g_probs - jnp.sum(probs * g_probs, axis=-1, keepdims=True))
                g_scores = g_scores.astype(BF)
                g_k[index] = g_k[index] + left_tmul(g_scores, query[part])
                g_query.append(matmul(g_scores, key[part]))
            back = turn(jnp.concatenate(g_query, axis=0) * scale, cosine, -sine)
            q_sum = q_sum + jnp.sum(back * q_unit, axis=0, keepdims=True)
            pieces[h] = unit_back(q_unit, q_root, back * q_gain).astype(BF)
        back = turn(jnp.concatenate(g_k, axis=0) * scale, cosine, -sine)
        k_sum = k_sum + jnp.sum(back * k_unit, axis=0, keepdims=True)
        pieces[q_here + kv] = unit_back(k_unit, k_root, back * k_gain).astype(BF)
        pieces[q_here + kv_here + kv] = jnp.concatenate(g_v, axis=0).astype(BF)
    g_qkv = jnp.concatenate([pieces[index] for index in range(q_here + 2 * kv_here)], axis=1)
    g_qkv_ref[...] = g_qkv
    own_ref[...] = right_tmul(g_qkv[:rows], w_qkv_ref[...]).astype(BF)
    away_ref[...] = right_tmul(g_qkv[rows:], w_qkv_ref[...]).astype(BF)
    gains_ref[...] = jnp.concatenate([q_sum, k_sum], axis=0)


def single(array, block=None, index=0):
    block = array.shape if block is None else block
    return pl.BlockSpec(block, lambda step: (index,) + (0,) * (len(block) - 1))


def slot_call(kernel, name, arrays, specs, shapes):
    return pl.pallas_call(
        kernel,
        grid=(1,),
        in_specs=specs,
        out_specs=[single(shape) for shape in shapes],
        out_shape=shapes,
        compiler_params=pltpu.CompilerParams(vmem_limit_bytes=ATTENTION_BYTES),
        cost_estimate=LOW_COST,
        name=name,
    )(*arrays)


def attention(slot, here, other, table, gain, q_gain, k_gain, w_qkv, w_out, q_here, kv_here):
    rows, width = here.shape
    arrays = (here, other, table, gain, q_gain, k_gain, w_qkv, w_out)
    specs = [single(array) for array in arrays]
    specs[2] = single(table, (2 * rows, table.shape[1]), slot)
    shapes = [
        jax.ShapeDtypeStruct((2 * rows, width), BF),
        jax.ShapeDtypeStruct((2 * rows, w_qkv.shape[1]), F32),
        jax.ShapeDtypeStruct((2 * rows, q_here * HD), BF),
        jax.ShapeDtypeStruct((rows, width), BF),
        jax.ShapeDtypeStruct((rows, width), BF),
    ]
    kernel = functools.partial(attention_kernel, q_here, kv_here)
    return slot_call(kernel, "attention", arrays, specs, shapes)


def attention_back(slot, here, other, qkv, table, q_gain, k_gain, w_qkv, w_out, q_here, kv_here):
    rows, width = here.shape
    arrays = (here, other, qkv, table, q_gain, k_gain, w_qkv, w_out)
    specs = [single(array) for array in arrays]
    specs[3] = single(table, (2 * rows, table.shape[1]), slot)
    shapes = [
        jax.ShapeDtypeStruct((2 * rows, width), BF),
        jax.ShapeDtypeStruct((2 * rows, w_qkv.shape[1]), BF),
        jax.ShapeDtypeStruct((rows, width), BF),
        jax.ShapeDtypeStruct((rows, width), BF),
        jax.ShapeDtypeStruct((2, HD), F32),
    ]
    kernel = functools.partial(attention_back_kernel, q_here, kv_here)
    return slot_call(kernel, "attention_back", arrays, specs, shapes)


def place_kernel(moves, source_count, out_count, row_ref, column_ref, *refs):
    sources, outs = refs[:source_count], refs[source_count : source_count + out_count]
    refs = refs[source_count + out_count :]
    cast = outs[0].dtype != sources[0].dtype
    staged = refs[source_count:-2] if cast else ()
    loaded, loads, stores = refs[:source_count], refs[-2], refs[-1]
    reads = [
        pltpu.make_async_copy(source, buffer, loads.at[index])
        for index, (source, buffer) in enumerate(zip(sources, loaded))
    ]
    for read in reads:
        read.start()
    writes = []
    arrived = set()
    for index, (source, slot, rows, columns, out) in enumerate(moves):
        height, width = rows.stop - rows.start, columns.stop - columns.start
        row = pl.multiple_of(row_ref[index] * height, height)
        if source not in arrived:
            reads[source].wait()
            arrived.add(source)
        if cast:
            staged[index][...] = loaded[source][slot, rows, columns].astype(outs[out].dtype)
            block = staged[index]
        else:
            block = loaded[source].at[slot, rows, columns]
        if len(outs[out].shape) == 3:
            target = outs[out].at[column_ref[index], pl.ds(row, height), :]
        elif outs[out].shape[1] == width:
            target = outs[out].at[pl.ds(row, height), :]
        else:
            column = pl.multiple_of(column_ref[index] * width, width)
            target = outs[out].at[pl.ds(row, height), pl.ds(column, width)]
        writes.append(pltpu.make_async_copy(block, target, stores.at[index]))
        writes[-1].start()
    for write in writes:
        write.wait()


def place_blocks(sources, moves, row_blocks, column_blocks, shapes, dtype):
    scratch = [pltpu.VMEM(source.shape, source.dtype) for source in sources]
    if dtype != sources[0].dtype:
        scratch += [
            pltpu.VMEM((rows.stop - rows.start, columns.stop - columns.start), dtype)
            for _, _, rows, columns, _ in moves
        ]
    scratch += [pltpu.SemaphoreType.DMA((len(sources),)), pltpu.SemaphoreType.DMA((len(moves),))]
    anywhere = pl.BlockSpec(memory_space=pl.ANY)
    return pl.pallas_call(
        functools.partial(place_kernel, moves, len(sources), len(shapes)),
        in_specs=[pl.BlockSpec(memory_space=pltpu.SMEM)] * 2 + [anywhere] * len(sources),
        out_specs=[anywhere] * len(shapes),
        out_shape=[jax.ShapeDtypeStruct(shape, dtype) for shape in shapes],
        scratch_shapes=scratch,
        compiler_params=pltpu.CompilerParams(vmem_limit_bytes=PLACE_BYTES),
        cost_estimate=LOW_COST,
        name="place_blocks",
    )(row_blocks.astype(jnp.int32), column_blocks.astype(jnp.int32), *sources)


def after(values, *others):
    return lax.optimization_barrier((values, *others))[0]


def move(values, send):
    ranks, copies = lax.axis_size("fsdp"), lax.axis_size("rep")
    pairs = []
    for f in range(ranks):
        for r in range(copies):
            to = send(f, r)
            if to is not None:
                pairs.append((f * copies + r, to[0] * copies + to[1]))
    return lax.ppermute(values, ("fsdp", "rep"), pairs)


def ring(values, step):
    ranks = lax.axis_size("fsdp")
    return move(values, lambda f, r: ((f + 2 * step) % ranks, r))


def swap_core(values):
    return move(values, lambda f, r: (f, r ^ 1))


def swap_x(values):
    return move(values, lambda f, r: (f, r ^ 2))


def swap_twin(values):
    return move(values, lambda f, r: (f ^ 1, r ^ 1))


def place():
    f, r = lax.axis_index("fsdp"), lax.axis_index("rep")
    return f // 2, f % 2, r // 2, r % 2


def pick(values, index, axis=0):
    return lax.dynamic_index_in_dim(values, index, axis, keepdims=False)


def ordered(slots, z):
    depth = len(slots)
    out = jnp.zeros((depth, *slots[0].shape), slots[0].dtype)
    for k, slot in enumerate(slots):
        out = lax.dynamic_update_index_in_dim(out, slot, (z - k) % depth, 0)
    return out


def add(left, right):
    return (left.astype(F32) + right.astype(F32)).astype(BF)


def gather_group(values, name, beside=None):
    slots = []
    for s in range(lax.axis_size("fsdp") // 2):
        with jax.named_scope(f"gather_{name}_{s}"):
            if s > 0:
                values = ring(values if beside is None else beside(s, values), 1)
            slots.append((values, swap_core(values)))
    return slots


def scatter_group(partial, name, beside=None):
    moving = None
    for step, (own, away) in enumerate((*partial[1:], partial[0])):
        with jax.named_scope(f"scatter_{name}_{step}"):
            total = own.astype(F32) + swap_core(away).astype(F32)
            if moving is not None:
                total = total + ring(moving, 1).astype(F32)
            moving = total.astype(BF)
        if beside is not None:
            moving = beside(step, moving)
    return total


def total_sum(values, beside):
    steps = [lambda f, r, bit=bit: (f, r ^ (1 << bit)) for bit in range(2)]
    ranks = lax.axis_size("fsdp")
    steps += [lambda f, r, bit=bit: (f ^ (1 << bit), r) for bit in range((ranks - 1).bit_length())]
    for index, step in enumerate(steps):
        values = values + after(move(values, step), *beside.get(index, ()))
    return values


class ColumnsIn:
    def __init__(self, parts, rows, name, hold=lambda slots: slots):
        with jax.named_scope(f"{name}_along_z"):
            slots = [ring(part, k) if k else part for k, part in enumerate(parts)]
            self.same = jnp.stack(hold(slots))
        with jax.named_scope(f"{name}_across"):
            self.across_x, self.across_y = swap_x(self.same), swap_twin(self.same)
        self.rows, self.name = rows, name

    def joined(self, split, *others):
        z, y, x, core = place()
        depth, columns = self.same.shape[0], self.same.shape[2]
        middle = depth // 2 if split else depth
        with jax.named_scope(f"{self.name}_across_both"):
            across_x, across_y = after((self.across_x, self.across_y), *others)
            rest = [swap_twin(across_x[:middle])]
            if split:
                rest.append(swap_x(across_y[middle:]))
        sources = [self.same, self.across_x, self.across_y, *rest]
        moves = [
            (source, slot, slice(0, self.rows), slice(0, columns), 0)
            for source, array in enumerate(sources)
            for slot in range(array.shape[0])
        ]
        where_z = (z - jnp.arange(depth)) % depth
        index = lambda yy, xx: (where_z * 2 + yy) * 2 + xx
        places = [index(y, x), index(y, 1 - x), index(1 - y, x), index(1 - y, 1 - x)]
        places = jnp.concatenate(places)
        shape = (4 * depth * self.rows, columns)
        return place_blocks(sources, moves, places, jnp.zeros_like(places), [shape], BF)[0]


def scoped(step):
    def wrap(method):
        def named(self, *others):
            with jax.named_scope(f"{self.name}_{step}"):
                return method(self, *others)

        return named

    return wrap


class ColumnsOut:
    def __init__(self, grad, y_first, name):
        self.name = name
        z, y, x, core = place()
        self.depth = lax.axis_size("fsdp") // 2
        self.y_first = y_first
        columns = grad.shape[1]
        self.blocks = grad.reshape(self.depth, 2, 2, -1, columns)
        axis, index = (1, 1 - y) if y_first else (2, 1 - x)
        self.payload = pick(self.blocks, index, axis)

    @scoped("first")
    def first(self, *others):
        z, y, x, core = place()
        axis, index = (1, y) if self.y_first else (2, x)
        swap = swap_twin if self.y_first else swap_x
        came, own = after(swap(self.payload), *others), pick(self.blocks, index, axis)
        here, there = (x, 1 - x) if self.y_first else (y, 1 - y)
        self.payload = add(pick(own, there, 1), pick(came, there, 1))
        self.kept = (pick(own, here, 1), pick(came, here, 1))

    @scoped("second")
    def second(self, *others):
        z, y, x, core = place()
        swap = swap_x if self.y_first else swap_twin
        came = after(swap(self.payload), *others).astype(F32)
        total = (self.kept[0].astype(F32) + self.kept[1].astype(F32) + came).astype(BF)
        self.payload = [pick(total, (z + k) % self.depth) for k in range(self.depth)]


def along_z(payloads, name):
    with jax.named_scope(f"sum_{name}_along_z"):
        parts = [jnp.concatenate(items, axis=1) for items in zip(*payloads)]
        return [ring(part, k) if k else part for k, part in enumerate(parts)]


def across_x(same, name):
    with jax.named_scope(f"sum_{name}_across"):
        return swap_x(same)


def columns_placed(same, across, widths, name):
    z, y, x, core = place()
    depth, rows, total = same.shape
    with jax.named_scope(f"sum_{name}_core"):
        parts = same, across, swap_core(same), swap_core(across)
    ones = jnp.ones((depth,), jnp.int32)
    row_blocks = jnp.concatenate([x * ones, (1 - x) * ones] * 2)
    where_z = (z - jnp.arange(depth)) % depth
    own, other = 2 * where_z + (y ^ core), 2 * where_z + (1 - (y ^ core))
    column_blocks = jnp.concatenate([own, own, other, other])
    aligned = all(width % 128 == 0 for width in widths)
    spans = []
    for width in widths if aligned else [total]:
        first = spans[-1].stop if spans else 0
        spans.append(slice(first, first + width))
    moves = [
        (source, slot, slice(0, rows), span, out)
        for source in range(4)
        for slot in range(depth)
        for out, span in enumerate(spans)
    ]
    if aligned:
        shapes = [(2 * rows, 2 * depth * width) for width in widths]
    else:
        shapes = [(2 * depth, 2 * rows, total)]
    repeat = lambda blocks: jnp.repeat(blocks, len(spans))
    outs = place_blocks(parts, moves, repeat(row_blocks), repeat(column_blocks), shapes, F32)
    if aligned:
        return outs
    rows_first = outs[0].transpose(1, 0, 2)
    pieces, first = [], 0
    for width in widths:
        pieces.append(rows_first[:, :, first : first + width].reshape(2 * rows, -1))
        first += width
    return pieces


def rows_across_y(weight, name):
    half = weight.shape[0] // 2
    with jax.named_scope(f"{name}_across_y"):
        part = lax.dynamic_slice_in_dim(weight, place()[2] * half, half, axis=0)
        return move(part, lambda f, r: (f ^ 1, r) if r % 2 else None)


def rows_here(weight, part, name):
    z, y, x, core = place()
    half = weight.shape[0] // 2
    with jax.named_scope(f"{name}_across_x"):
        other = move(part, lambda f, r: (f, r ^ 2) if r % 2 else None)
    low = jnp.where(core == 0, weight[:half], jnp.where(x == 0, part, other))
    high = jnp.where(core == 0, weight[half:], jnp.where(x == 0, other, part))
    return jnp.concatenate([low, high], axis=0)


class RowsOut:
    def __init__(self, grad, name):
        self.name = name
        self.grad = self.payload = grad.reshape(2, -1, grad.shape[1])

    @scoped("first")
    def first(self, *others):
        z, y, x, core = place()
        came = after(move(self.payload, lambda f, r: (f ^ 1, r ^ 1) if r % 2 else None), *others)
        self.payload = add(pick(self.grad, 1 - x), pick(came, 1 - x))
        self.kept = (pick(self.grad, x), pick(came, x))

    @scoped("second")
    def second(self, *others):
        came = move(self.payload, lambda f, r: None if r % 2 else (f, r ^ 2))
        came = after(came, *others).astype(F32)
        self.payload = (self.kept[0].astype(F32) + self.kept[1].astype(F32) + came).astype(BF)

    @scoped("third")
    def third(self, *others):
        came = after(move(self.payload, lambda f, r: None if r % 2 else (f, r ^ 2)), *others)
        self.payload = jnp.stack([self.payload, came])

    @scoped("last")
    def last(self):
        z, y, x, core = place()
        came = move(self.payload, lambda f, r: None if r % 2 else (f, r ^ 1))
        parts = jnp.where(core == 0, self.payload, came)
        rows, columns = parts.shape[1:]
        moves = [(0, slot, slice(0, rows), slice(0, columns), 0) for slot in range(2)]
        places = jnp.stack([x, 1 - x])
        return place_blocks([parts], moves, places, jnp.zeros_like(places), [(2 * rows, columns)], F32)[0]


def local(
    tokens_in,
    segment_ids,
    w_query,
    w_key,
    w_value,
    w_out,
    w_gate,
    w_up,
    w_down,
    gain_attn,
    gain_ffn,
    gain_query,
    gain_key,
    d_out,
):
    ranks = lax.axis_size("fsdp")
    rank = lax.axis_index("fsdp")
    depth = ranks // 2
    z, y, x, core = place()
    width = tokens_in.shape[1]
    pack = segment_ids.shape[1]
    heads = w_query.shape[1] // HD
    kv_heads = w_key.shape[1] // HD
    share = max(1, ranks // kv_heads)
    q_here = heads // ranks
    kv_here = max(1, kv_heads // ranks)
    group = q_here // kv_here
    q_cols, kv_cols = q_here * HD, kv_here * HD
    scale = HD ** (-0.5)

    q_gain = gain_query.astype(F32)[None]
    k_gain = gain_key.astype(F32)[None]

    rows_x = w_query.shape[0] // 2
    cut = lambda weight, start, size: lax.dynamic_slice(weight, (x * rows_x, start), (rows_x, size))
    wide = q_cols + 2 * kv_cols
    seg_size = segment_ids.size
    extra = jnp.concatenate([segment_ids.reshape(-1).astype(BF), gain_attn, gain_ffn])
    extra = jnp.pad(extra, (0, 16 * wide - extra.size)).reshape(16, wide)

    def cut_qkv(block):
        kv = block // share * kv_cols
        parts = [cut(w_query, block * q_cols, q_cols), cut(w_key, kv, kv_cols), cut(w_value, kv, kv_cols)]
        return jnp.concatenate([jnp.concatenate(parts, axis=1), extra], axis=0)

    def cutter(weight):
        size = weight.shape[1] // ranks
        return lambda block: cut(weight, block * size, size)

    qkv_parts = [cut_qkv(2 * ((z + k) % depth) + (y ^ core)) for k in range(depth)]
    qkv_in = ColumnsIn(qkv_parts, rows_x, "w_qkv")
    w_qkv = qkv_in.joined(False)
    w_out_here = rows_here(w_out, rows_across_y(w_out, "w_out"), "w_out")
    down_part = rows_across_y(after(w_down, w_qkv), "w_down")
    w_down_here = rows_here(w_down, down_part, "w_down")
    w_gate_late, w_up_late = after((w_gate, w_up), qkv_in.same)
    columns_here = w_gate.shape[1] // ranks

    def cut_glu(block):
        first = block * columns_here
        return jnp.concatenate(
            [cut(w_gate_late, first, columns_here), cut(w_up_late, first, columns_here)], axis=1
        )

    glu_parts = [cut_glu(2 * ((z + k) % depth) + (y ^ core)) for k in range(depth)]
    glu_in = ColumnsIn(glu_parts, rows_x, "w_glu", lambda slots: after((*slots,), w_qkv, w_out_here))
    own_slots, twin_slots = qkv_in.same, qkv_in.across_y
    own_extra = own_slots[:, rows_x:].reshape(depth, -1)
    twin_extra = twin_slots[:, rows_x:].reshape(depth, -1)
    seg_slots = own_extra[:, :seg_size].reshape(depth, 1, -1, pack)
    segments = jnp.concatenate([seg_slots, swap_core(seg_slots)], axis=1).reshape(-1, pack).astype(jnp.int32)
    span = slice(seg_size, seg_size + 2 * gain_attn.size)
    pieces = jnp.stack([own_extra[:, span], twin_extra[:, span]], axis=1)
    pieces = ordered([pieces[k] for k in range(depth)], z).astype(F32)
    pieces = jnp.where(y == 0, pieces, pieces[:, ::-1])
    gains = pieces.reshape(depth, 2, 2, -1).transpose(2, 0, 1, 3).reshape(2, -1)
    attn_gain, ffn_gain = gains[0], gains[1]

    token_ties = {1: (glu_in.same, attn_gain, down_part), 2: (w_down_here,)}
    beside_tokens = lambda s, sent: after(sent, *token_ties.get(s, ()))
    token_slots = gather_group(tokens_in, "tokens", beside_tokens)
    block_rows = tokens_in.shape[0]
    table = token_table(segments, block_rows)
    kept, partial = [None] * depth, [None] * depth
    order = (*range(1, depth), 0)
    for s in order:
        here, other = token_slots[s]
        if s == depth - 1:
            here = after(here, glu_in.across_x, glu_in.across_y)
        *kept[s], own, away = attention(
            s, here, other, table, attn_gain[None], q_gain, k_gain, w_qkv, w_out_here, q_here, kv_here
        )
        partial[s] = (own, away)
    tokens = tokens_in.astype(F32)
    unit_tokens, root_tokens = unit_rows(tokens)

    w_glu = glu_in.joined(True)
    attn_branch = after(scatter_group(partial, "attn_branch"), w_glu)

    middle = tokens + attn_branch
    unit_middle, root_middle = unit_rows(middle)
    ffn_slots = gather_group((unit_middle * ffn_gain).astype(BF), "ffn_in")
    beside_d_out = lambda s, sent: after(sent, ffn_slots[-1][0]) if s == 1 else sent
    grad_slots = gather_group(d_out, "d_out", beside_d_out)
    glu_kept, back_partial, down_partial = [None] * depth, [None] * depth, []
    for s in order:
        ffn_in = jnp.concatenate(ffn_slots[s], axis=0)
        g_ffn = jnp.concatenate(grad_slots[s], axis=0)
        gate_up = matmul(ffn_in, w_glu)
        gate, up = gate_up[:, :columns_here], gate_up[:, columns_here:]
        sig = jax.nn.sigmoid(gate)
        silu = gate * sig
        hidden = (silu * up).astype(BF)
        g_hidden = right_tmul(g_ffn, w_down_here).astype(BF).astype(F32)
        g_gate = (g_hidden * up * sig * (1 + gate * (1 - sig))).astype(BF)
        g_up = (g_hidden * silu).astype(BF)
        part = right_tmul(jnp.concatenate([g_gate, g_up], axis=1), w_glu).astype(BF)
        back_partial[s] = (part[:block_rows], part[block_rows:])
        glu_kept[s] = (ffn_in, g_ffn, hidden, g_gate, g_up)
    ffn_in, g_ffn, hidden, g_gate, g_up = (jnp.concatenate(items, axis=0) for items in zip(*glu_kept))
    sums = {}

    def beside_feed(step, sent):
        if step == depth - 3:
            grad = left_tmul(*after((ffn_in, g_gate), sent)).astype(BF)
            sums["gate"] = ColumnsOut(grad, True, "sum_gate")
            grad = left_tmul(*after((ffn_in, g_up), sums["gate"].payload)).astype(BF)
            sums["up"] = ColumnsOut(grad, False, "sum_up")
        if step == depth - 2:
            sent = after(sent, sums["up"].payload)
        return sent

    g_ffn_in = scatter_group(back_partial, "g_ffn_in", beside_feed)
    gate_sum, up_sum = sums["gate"], sums["up"]
    g_ffn_in = after(g_ffn_in, gate_sum.payload, up_sum.payload)
    ffn_gain_grad = jnp.sum(g_ffn_in * unit_middle, axis=0)
    g_middle = d_out.astype(F32) + unit_back(unit_middle, root_middle, g_ffn_in * ffn_gain)

    attn_slots = gather_group(g_middle.astype(BF), "g_attn")
    back_kept, partial = [None] * depth, [None] * depth
    head_gains = 0.0
    for s in order:
        here, other = attn_slots[s]
        if s == 2:
            gate_sum.first(partial[1][1])
            up_sum.first(partial[1][1])
            here = after(here, gate_sum.payload, up_sum.payload)
        if s == 3:
            gate_sum.second(partial[2][1])
            up_sum.second(partial[2][1])
            grad_down = left_tmul(*after((hidden, g_ffn), up_sum.payload)).astype(BF)
            down_sum = RowsOut(grad_down, "sum_down")
            here = after(here, gate_sum.payload, up_sum.payload, down_sum.payload)
        g_attn, g_qkv, own, away, gain_part = attention_back(
            s, here, other, kept[s][1], table, q_gain, k_gain, w_qkv, w_out_here, q_here, kv_here
        )
        head_gains = head_gains + gain_part
        back_kept[s] = (g_attn, g_qkv)
        partial[s] = (own, away)
    attn_in, _, mixed = (jnp.concatenate(items, axis=0) for items in zip(*kept))
    g_attn, g_qkv = (jnp.concatenate(items, axis=0) for items in zip(*back_kept))
    grad_qkv = left_tmul(attn_in, g_qkv).astype(BF)
    qkv_sum = ColumnsOut(grad_qkv, True, "sum_qkv")
    grad_out = left_tmul(*after((mixed, g_attn), qkv_sum.payload)).astype(BF)
    out_sum = RowsOut(grad_out, "sum_out")
    glu_parts = [jnp.concatenate(pair, axis=1) for pair in zip(gate_sum.payload, up_sum.payload)]
    glu_slots = {0: glu_parts[0]}
    steps = sorted(range(1, depth), key=lambda k: -min(k, depth - k))
    last = None
    for k in steps:
        with jax.named_scope(f"sum_glu_along_z_{k}"):
            part = glu_parts[k] if last is None else after(glu_parts[k], last)
            last = glu_slots[k] = ring(part, k)
        if k == steps[0]:
            last = after(last, qkv_sum.payload, out_sum.payload)
    glu_same = jnp.stack([glu_slots[k] for k in range(depth)])
    glu_across = across_x(glu_same, "glu")

    def beside_back(step, sent):
        if step == 0:
            sent = after(sent, glu_slots[steps[0]])
        if step == 1:
            sent = after(sent, glu_same)
            for item in (down_sum, qkv_sum, out_sum):
                item.first(sent)
        if step == 2:
            sent = after(sent, down_sum.payload, qkv_sum.payload, out_sum.payload, glu_across)
        return sent

    g_attn_in = scatter_group(partial, "g_attn_in", beside_back)
    attn_gain_grad = jnp.sum(g_attn_in * unit_tokens, axis=0)
    d_tokens = g_middle + unit_back(unit_tokens, root_tokens, g_attn_in * attn_gain)

    for s in range(depth):
        part = matmul(after(glu_kept[s][2], glu_same), w_down_here).astype(BF)
        down_partial.append((part[:block_rows], part[block_rows:]))
    glu_placed = columns_placed(glu_same, glu_across, [columns_here, columns_here], "glu")

    arrived = []

    def beside_branch(step, sent):
        arrived.append(sent)
        if step == 0:
            return after(sent, d_tokens)
        if step == 1:
            down_sum.second(d_tokens)
            return after(sent, down_sum.payload)
        if step == 2:
            qkv_sum.second(arrived[1])
            out_sum.second(arrived[1])
            return after(sent, qkv_sum.payload, out_sum.payload)
        return sent

    ffn_branch = scatter_group(down_partial, "ffn_branch", beside_branch)
    grad_gate, grad_up = glu_placed
    qkv_slots = along_z([qkv_sum.payload], "qkv")
    qkv_same = jnp.stack(after((*qkv_slots,), arrived[-1]))
    block = middle + after(ffn_branch, *glu_placed, qkv_same)
    qkv_across = across_x(qkv_same, "qkv")
    grad_query, grad_kv = columns_placed(qkv_same, qkv_across, [q_cols, 2 * kv_cols], "qkv")
    down_sum.third(arrived[2])
    out_sum.third(arrived[2])
    grad_down, grad_out = down_sum.last(), out_sum.last()
    grad_kv = grad_kv.reshape(grad_kv.shape[0], -1, share, 2 * kv_cols).sum(axis=2)
    grad_key = grad_kv[:, :, :kv_cols].reshape(grad_kv.shape[0], -1)
    grad_value = grad_kv[:, :, kv_cols:].reshape(grad_kv.shape[0], -1)
    squares = jnp.stack(
        [jnp.sum(item * item) for item in (middle, attn_branch, ffn_branch, block, d_tokens)]
    )
    small = jnp.concatenate([attn_gain_grad, ffn_gain_grad, head_gains[0], head_gains[1], squares])
    with jax.named_scope("total_sum"):
        small = total_sum(small, {0: (grad_down,), 1: (grad_out,), 3: (grad_query,)})
    gain_rows = gain_attn.shape[0]
    attn_gain_sum = lax.dynamic_slice(small, (rank * gain_rows,), (gain_rows,))
    ffn_gain_sum = lax.dynamic_slice(small, (width + rank * gain_rows,), (gain_rows,))
    entries = tokens_in.shape[0] * ranks * lax.axis_size("rep") * width
    stats = jnp.sqrt(small[2 * width + 2 * HD :] / entries)
    return (
        block.astype(BF),
        d_tokens.astype(BF),
        grad_query,
        grad_key,
        grad_value,
        grad_out,
        grad_gate,
        grad_up,
        grad_down,
        attn_gain_sum,
        ffn_gain_sum,
        small[2 * width : 2 * width + HD],
        small[2 * width + HD : 2 * width + 2 * HD],
        stats,
    )


def solution(mesh):
    rows = P(("fsdp", "rep"), None)
    weight = P("fsdp", None)
    return jax.shard_map(
        local,
        mesh=mesh,
        in_specs=(rows, rows, *[weight] * 7, P("fsdp"), P("fsdp"), P(), P(), rows),
        out_specs=(rows, rows, *[weight] * 7, P("fsdp"), P("fsdp"), P(), P(), P()),
        check_vma=False,
    )
```
